32 devices in a mesh: cells: 16 (over z, y, x), sub: 2 (over core).
Axes of the slice: x: 2, y: 2, z: 4, core: 2. Of those that a mesh axis runs over, the one named last changes fastest.
Arguments:
- snapshots: float32 [16384, 256], P(('cells', 'sub')), may hold values from -10 to 10, as said below
- volumes: float32 [16384], P(('cells', 'sub')), may hold values from 0.1 to 10
- live_rows: int32 [32], P(('cells', 'sub')), may hold values from 256 to 512, as said below
- probes: float32 [64, 16384], P(None, ('cells', 'sub')), may hold values from -6 to 6
Outputs:
- basis: float32 [16384, 256], P(('cells', 'sub'))
- factor: float32 [256, 256], replicated
- coefficients: float32 [64, 256], replicated
The draws below stay inside these ranges and needn't reach their ends.
Inputs may be any that keep to these rules, and one draw needn't show every extreme that they name: `live_rows`: each entry is the live row count of one device's block of 512 row slots; live rows come first in the block. Some device has all 512 live, some has 256. `snapshots`: the columns are linearly independent.
All inputs are finite; a program needn't handle non-finite values.
Results may differ from the reference program's by a relative error of at most 0.00013.
Values sent between devices are 32-bit elements; how exact they have to be, the bound alone decides.
No kernel may reach another device: no remote copies, remote signals or barrier semaphores. Data moves between devices by JAX's collectives and lax.ppermute only.
A program may use at most 64 MiB of HBM per device.

```python
import math
import jax
import jax.numpy as jnp
from jax import lax

ROW_DEV = 512
SNAPS = 256
PROBES = 64
ROWS = 16384


def draw_snapshots(key, part):
    key_base, key_mix = jax.random.split(jax.random.fold_in(key, 11), 2)
    identity = jnp.eye(SNAPS, dtype=jnp.float32)
    base = jax.random.normal(key_base, (ROWS, SNAPS), jnp.float32)
    mixing = identity + 0.6 * jax.random.normal(key_mix, (SNAPS, SNAPS), jnp.float32) / jnp.sqrt(jnp.float32(SNAPS))
    mixed = jnp.dot(base, mixing, precision=lax.Precision.HIGHEST, preferred_element_type=jnp.float32)
    return jnp.clip(mixed, -10.0, 10.0)


def draw_live_rows(key, part):
    key_counts, key_pick = jax.random.split(jax.random.fold_in(key, 23), 2)
    blocks = ROWS // ROW_DEV
    counts = jax.random.randint(key_counts, (blocks,), ROW_DEV // 2, ROW_DEV + 1, jnp.int32)
    chosen = jax.random.randint(key_pick, (), 0, blocks, jnp.int32)
    other = (chosen + 1) % blocks
    positions = lax.iota(jnp.int32, blocks)
    counts = jnp.where(positions == chosen, ROW_DEV, counts)
    counts = jnp.where(positions == other, ROW_DEV // 2, counts)
    return counts.astype(jnp.int32)


def block_levels(own_key, dims, cuts, least, high):
    loudness = 1.0
    for position, parts in cuts:
        steps = jax.random.uniform(jax.random.fold_in(jax.random.fold_in(own_key, 6), position), (parts,), jnp.float32, least / len(cuts), high / len(cuts))
        loudness = loudness * jnp.repeat(jnp.exp(steps), dims[position] // parts).reshape((-1,) + (1,) * (len(dims) - 1 - position))
    return loudness


def gaussian(rng, extent, spread, most, cuts=(), kind=jnp.bfloat16):
    entries = jax.random.normal(rng, extent, jnp.float32) * spread
    if len(cuts) > 0:
        entries = block_levels(rng, extent, cuts, -0.22, 0.18) * entries
    return jnp.clip(entries, min=-most, max=most).astype(kind)


def setup_inputs(seed: int = 0) -> dict:
    arg_keys = jax.random.split(jax.random.key(seed), 5)
    snapshots = draw_snapshots(jax.random.fold_in(arg_keys[4], 71), 0)
    volumes = jnp.clip(jnp.exp(math.log(10.0) - 4.6051702 * jax.random.uniform(arg_keys[1], (ROWS,), jnp.float32) ** block_levels(arg_keys[1], (ROWS,), ((0, 32),), -0.2, 0.2)), 0.1, 10.0)
    live_rows = draw_live_rows(jax.random.fold_in(arg_keys[4], 71), 0)
    probes = gaussian(arg_keys[3], (PROBES, ROWS), 1.0, 6.0, ((1, 32),), jnp.float32)
    return dict(snapshots=snapshots, volumes=volumes, live_rows=live_rows, probes=probes)


HIGHEST = lax.Precision.HIGHEST

def reference(snapshots, volumes, live_rows, probes):
    total_rows = snapshots.shape[0]
    row_ids = lax.iota(jnp.int32, total_rows)
    block_ids = (row_ids // ROW_DEV).astype(jnp.int32)
    slot_ids = (row_ids % ROW_DEV).astype(jnp.int32)
    live_mask = slot_ids < live_rows[block_ids]
    row_scale = jnp.where(live_mask, jnp.sqrt(volumes), jnp.float32(0.0))
    weighted = snapshots * row_scale[:, None]
    gram_matrix = lax.dot_general(weighted.astype(jnp.float32), weighted.astype(jnp.float32), (((0,), (0,)), ((), ())), precision=HIGHEST, preferred_element_type=jnp.float32) / jnp.float32(total_rows)
    lower_factor = jnp.linalg.cholesky(gram_matrix)
    factor = lower_factor.T
    identity = jnp.eye(SNAPS, dtype=jnp.float32)
    inverse = lax.linalg.triangular_solve(factor, identity, left_side=True, lower=False)
    basis = jnp.dot(weighted.astype(jnp.float32), inverse.astype(jnp.float32), precision=HIGHEST, preferred_element_type=jnp.float32)
    probe_weighted = probes * row_scale[None, :]
    coefficients = jnp.dot(probe_weighted.astype(jnp.float32), basis.astype(jnp.float32), precision=HIGHEST, preferred_element_type=jnp.float32) / jnp.sqrt(jnp.float32(total_rows))
    return (basis, factor, coefficients)
```

```python
import functools
import jax
import jax.numpy as jnp
from jax import lax
from jax.experimental import pallas as pl
from jax.experimental.pallas import tpu as pltpu
from jax.sharding import PartitionSpec as P

HIGHEST = lax.Precision.HIGHEST
LANES = 128
BLOCK = 8
F32 = jnp.float32


def recip(value):
    guess = pl.reciprocal(value, approx=True)
    guess = guess * (2.0 - value * guess)
    return guess * (2.0 - value * guess)


def lanes_of(tile, column):
    return jnp.broadcast_to(tile[:, column : column + 1], (BLOCK, LANES))


def row_of(tile, index):
    return jnp.broadcast_to(tile[index : index + 1, :], (BLOCK, LANES))


def eliminate(work, factor_ref, linv_ref, order, panel):
    tiles = order // LANES
    sub_ids = lax.broadcasted_iota(jnp.int32, (BLOCK, LANES), 0)
    lane_ids = lax.broadcasted_iota(jnp.int32, (BLOCK, LANES), 1)
    zero = jnp.zeros((BLOCK, LANES), F32)
    one = jnp.ones((BLOCK, LANES), F32)

    def load(row, tile):
        return work[row : row + BLOCK, tile * LANES : (tile + 1) * LANES]

    for start in range(0, order, BLOCK):
        first = (start // panel) * panel
        last = first + panel
        home, offset = start // LANES, start % LANES
        in_block = (lane_ids >= offset) & (lane_ids < offset + BLOCK)
        own = [load(start, t) for t in range(tiles)]
        diag_tile = own[home]
        columns = [lanes_of(diag_tile, offset + c) for c in range(BLOCK)]
        entry = {(r, c): row_of(columns[c], r) for c in range(BLOCK) for r in range(c + 1)}
        rows = [[row_of(own[t], r) for t in range(tiles)] for r in range(BLOCK)]
        kept = [rows[r][home] for r in range(BLOCK)]
        for r in range(BLOCK):
            rows[r][home] = jnp.where(in_block, jnp.where(lane_ids == offset + r, one, zero), rows[r][home])
        ahead = start + BLOCK
        follows = ahead < last
        if follows:
            below = [load(ahead, t) for t in range(tiles)]
            below_columns = [lanes_of(below[home], offset + c) for c in range(BLOCK)]
            below[home] = jnp.where(in_block, zero, below[home])
        inverse_pivot, scaled = [], {}
        for i in range(BLOCK):
            inv = recip(entry[i, i])
            inverse_pivot.append(inv)
            for r in range(i + 1, BLOCK):
                scaled[r, i] = entry[i, r] * inv
            for r in range(i + 1, BLOCK):
                for c in range(r, BLOCK):
                    entry[r, c] = entry[r, c] - scaled[r, i] * entry[i, c]
            if follows:
                weight = below_columns[i] * inv
                for c in range(i + 1, BLOCK):
                    below_columns[c] = below_columns[c] - below_columns[i] * scaled[c, i]
                for t in range(tiles):
                    below[t] = below[t] - weight * rows[i][t]
            for r in range(i + 1, BLOCK):
                for t in range(tiles):
                    rows[r][t] = rows[r][t] - scaled[r, i] * rows[i][t]
                kept[r] = kept[r] - scaled[r, i] * kept[i]
        if follows:
            for t in range(tiles):
                work[ahead : ahead + BLOCK, t * LANES : (t + 1) * LANES] = below[t]
        roots = [jnp.sqrt(entry[i, i]) * inverse_pivot[i] for i in range(BLOCK)]

        def gather(parts):
            total = parts[0]
            for r in range(1, BLOCK):
                total = jnp.where(sub_ids == r, parts[r], total)
            return total

        root = gather(roots)
        for t in range(tiles):
            merged = gather([rows[r][t] for r in range(BLOCK)]) * root
            column_ids = lane_ids + t * LANES
            lower = jnp.where(column_ids <= start + sub_ids, merged, zero)
            if t == home:
                merged_kept = gather(kept) * root
                upper = jnp.where(in_block, merged_kept, merged)
            else:
                upper = merged
            upper = jnp.where(column_ids >= start + sub_ids, upper, zero)
            factor_ref[start : start + BLOCK, t * LANES : (t + 1) * LANES] = upper
            linv_ref[start : start + BLOCK, t * LANES : (t + 1) * LANES] = lower
        if ahead + BLOCK < last:
            solved = [None] * BLOCK
            for r in reversed(range(BLOCK)):
                solved[r] = [rows[r][t] * inverse_pivot[r] for t in range(tiles)]
                for c in range(r + 1, BLOCK):
                    for t in range(tiles):
                        solved[r][t] = solved[r][t] - scaled[c, r] * solved[c][t]
            for row in range(ahead + BLOCK, last, BLOCK):
                target = [load(row, t) for t in range(tiles)]
                source = target[home]
                target[home] = jnp.where(in_block, zero, source)
                for c in range(BLOCK):
                    weight = lanes_of(source, offset + c)
                    for t in range(tiles):
                        target[t] = target[t] - weight * solved[c][t]
                for t in range(tiles):
                    work[row : row + BLOCK, t * LANES : (t + 1) * LANES] = target[t]
        if ahead == last and last < order:
            left = factor_ref[first:last, last:]
            mixed = jnp.concatenate([linv_ref[first:last, :last], factor_ref[first:last, last:]], axis=1)
            product = lax.dot_general(
                left, mixed, (((0,), (0,)), ((), ())), precision=HIGHEST, preferred_element_type=F32
            )
            ids = lax.broadcasted_iota(jnp.int32, (order - last, order), 1)
            previous = jnp.where((ids >= first) & (ids < last), 0.0, work[last:, :])
            work[last:, :] = previous - product


def finish_kernel(panel, gram_ref, cross_ref, weighted_ref, basis_ref, factor_ref, coef_ref, work, linv):
    order = gram_ref.shape[0]
    work[...] = gram_ref[...]
    eliminate(work, factor_ref, linv, order, panel)
    dims = (((1,), (1,)), ((), ()))
    basis_ref[...] = lax.dot_general(
        weighted_ref[...], linv[...], dims, precision=HIGHEST, preferred_element_type=F32
    )
    coef_ref[...] = lax.dot_general(
        cross_ref[...], linv[...], dims, precision=HIGHEST, preferred_element_type=F32
    )


def finish(gram, cross, weighted, panel=128):
    order = gram.shape[0]
    rows, probes = weighted.shape[0], cross.shape[0]
    whole = pl.BlockSpec(memory_space=pltpu.VMEM)
    return pl.pallas_call(
        functools.partial(finish_kernel, panel),
        out_shape=(
            jax.ShapeDtypeStruct((rows, order), F32),
            jax.ShapeDtypeStruct((order, order), F32),
            jax.ShapeDtypeStruct((probes, order), F32),
        ),
        in_specs=[whole] * 3,
        out_specs=(whole,) * 3,
        scratch_shapes=[pltpu.VMEM((order, order), F32), pltpu.VMEM((order, order), F32)],
        compiler_params=pltpu.CompilerParams(vmem_limit_bytes=32 * 1024 * 1024),
    )(gram, cross, weighted)


def exchange(value, axis, bit):
    size = lax.axis_size(axis)
    return lax.ppermute(value, axis, [(i, i ^ bit) for i in range(size)])


def reduce_all(value):
    half = value.shape[0] // 2
    core = lax.axis_index("sub") % 2
    low, high = value[:half], value[half:]
    mine = jnp.where(core == 0, low, high)
    mine = mine + exchange(jnp.where(core == 0, high, low), "sub", 1)
    for axis, begin in (("cells", 1), ("sub", 2)):
        bit = begin
        while bit < lax.axis_size(axis):
            mine = mine + exchange(mine, axis, bit)
            bit *= 2
    other = exchange(mine, "sub", 1)
    low = jnp.where(core == 0, mine, other)
    high = jnp.where(core == 0, other, mine)
    return jnp.concatenate([low, high], axis=0)


def per_device(snapshots, volumes, live_rows, probes):
    row_count, order = snapshots.shape
    total_rows = row_count * lax.axis_size("cells") * lax.axis_size("sub")
    root_total = jnp.sqrt(jnp.float32(total_rows))
    live_mask = lax.iota(jnp.int32, row_count) < live_rows[0]
    row_scale = jnp.where(live_mask, jnp.sqrt(volumes), jnp.float32(0.0))
    weighted = snapshots * row_scale[:, None]
    probe_weighted = probes * row_scale[None, :]
    gram_local = lax.dot_general(
        weighted, weighted, (((0,), (0,)), ((), ())), precision=HIGHEST, preferred_element_type=F32
    ) / jnp.float32(total_rows)
    cross_local = jnp.dot(probe_weighted, weighted, precision=HIGHEST, preferred_element_type=F32) / root_total
    total = reduce_all(jnp.concatenate([gram_local, cross_local], axis=0))
    return finish(total[:order], total[order:], weighted)


def solution(mesh):
    placed = (
        P(("cells", "sub"), None),
        P(("cells", "sub")),
        P(("cells", "sub")),
        P(None, ("cells", "sub")),
    )
    return jax.shard_map(
        per_device,
        mesh=mesh,
        in_specs=placed,
        out_specs=(P(("cells", "sub"), None), P(), P()),
        check_vma=False,
    )
```

```python
import functools
import jax
import jax.numpy as jnp
from jax import lax
from jax.experimental import pallas as pl
from jax.experimental.pallas import tpu as pltpu
from jax.sharding import PartitionSpec as P

HIGHEST = lax.Precision.HIGHEST
LANES = 128
BLOCK = 8
F32 = jnp.float32


def recip(value):
    guess = pl.reciprocal(value, approx=True)
    guess = guess * (2.0 - value * guess)
    return guess * (2.0 - value * guess)


def lanes_of(tile, column):
    return jnp.broadcast_to(tile[:, column : column + 1], (BLOCK, LANES))


def row_of(tile, index):
    return jnp.broadcast_to(tile[index : index + 1, :], (BLOCK, LANES))


def eliminate(work, factor_ref, linv_ref, order, panel):
    tiles = order // LANES
    sub_ids = lax.broadcasted_iota(jnp.int32, (BLOCK, LANES), 0)
    lane_ids = lax.broadcasted_iota(jnp.int32, (BLOCK, LANES), 1)
    zero = jnp.zeros((BLOCK, LANES), F32)
    one = jnp.ones((BLOCK, LANES), F32)

    def load(row, tile):
        return work[row : row + BLOCK, tile * LANES : (tile + 1) * LANES]

    for start in range(0, order, BLOCK):
        first = (start // panel) * panel
        last = first + panel
        home, offset = start // LANES, start % LANES
        in_block = (lane_ids >= offset) & (lane_ids < offset + BLOCK)
        own = [load(start, t) for t in range(tiles)]
        diag_tile = own[home]
        columns = [lanes_of(diag_tile, offset + c) for c in range(BLOCK)]
        entry = {(r, c): row_of(columns[c], r) for c in range(BLOCK) for r in range(c + 1)}
        rows = [[row_of(own[t], r) for t in range(tiles)] for r in range(BLOCK)]
        kept = [rows[r][home] for r in range(BLOCK)]
        for r in range(BLOCK):
            rows[r][home] = jnp.where(in_block, jnp.where(lane_ids == offset + r, one, zero), rows[r][home])
        ahead = start + BLOCK
        follows = ahead < last
        if follows:
            below = [load(ahead, t) for t in range(tiles)]
            below_columns = [lanes_of(below[home], offset + c) for c in range(BLOCK)]
            below[home] = jnp.where(in_block, zero, below[home])
        inverse_pivot, scaled = [], {}
        for i in range(BLOCK):
            inv = recip(entry[i, i])
            inverse_pivot.append(inv)
            for r in range(i + 1, BLOCK):
                scaled[r, i] = entry[i, r] * inv
            for r in range(i + 1, BLOCK):
                for c in range(r, BLOCK):
                    entry[r, c] = entry[r, c] - scaled[r, i] * entry[i, c]
            if follows:
                weight = below_columns[i] * inv
                for c in range(i + 1, BLOCK):
                    below_columns[c] = below_columns[c] - below_columns[i] * scaled[c, i]
                for t in range(tiles):
                    below[t] = below[t] - weight * rows[i][t]
            for r in range(i + 1, BLOCK):
                for t in range(tiles):
                    rows[r][t] = rows[r][t] - scaled[r, i] * rows[i][t]
                kept[r] = kept[r] - scaled[r, i] * kept[i]
        if follows:
            for t in range(tiles):
                work[ahead : ahead + BLOCK, t * LANES : (t + 1) * LANES] = below[t]
        roots = [jnp.sqrt(entry[i, i]) * inverse_pivot[i] for i in range(BLOCK)]

        def gather(parts):
            total = parts[0]
            for r in range(1, BLOCK):
                total = jnp.where(sub_ids == r, parts[r], total)
            return total

        root = gather(roots)
        for t in range(tiles):
            merged = gather([rows[r][t] for r in range(BLOCK)]) * root
            column_ids = lane_ids + t * LANES
            lower = jnp.where(column_ids <= start + sub_ids, merged, zero)
            if t == home:
                merged_kept = gather(kept) * root
                upper = jnp.where(in_block, merged_kept, merged)
            else:
                upper = merged
            upper = jnp.where(column_ids >= start + sub_ids, upper, zero)
            factor_ref[start : start + BLOCK, t * LANES : (t + 1) * LANES] = upper
            linv_ref[start : start + BLOCK, t * LANES : (t + 1) * LANES] = lower
        if ahead + BLOCK < last:
            solved = [None] * BLOCK
            for r in reversed(range(BLOCK)):
                solved[r] = [rows[r][t] * inverse_pivot[r] for t in range(tiles)]
                for c in range(r + 1, BLOCK):
                    for t in range(tiles):
                        solved[r][t] = solved[r][t] - scaled[c, r] * solved[c][t]
            for row in range(ahead + BLOCK, last, BLOCK):
                target = [load(row, t) for t in range(tiles)]
                source = target[home]
                target[home] = jnp.where(in_block, zero, source)
                for c in range(BLOCK):
                    weight = lanes_of(source, offset + c)
                    for t in range(tiles):
                        target[t] = target[t] - weight * solved[c][t]
                for t in range(tiles):
                    work[row : row + BLOCK, t * LANES : (t + 1) * LANES] = target[t]
        if ahead == last and last < order:
            left = factor_ref[first:last, last:]
            mixed = jnp.concatenate([linv_ref[first:last, :last], factor_ref[first:last, last:]], axis=1)
            product = lax.dot_general(
                left, mixed, (((0,), (0,)), ((), ())), precision=HIGHEST, preferred_element_type=F32
            )
            ids = lax.broadcasted_iota(jnp.int32, (order - last, order), 1)
            previous = jnp.where((ids >= first) & (ids < last), 0.0, work[last:, :])
            work[last:, :] = previous - product


def packed_rows(order, probes):
    return -(-(order // 2 + probes + 1) // (2 * BLOCK)) * 2 * BLOCK


def live_volumes(volumes_ref, live_ref, begin):
    ids = lax.broadcasted_iota(jnp.int32, (1, LANES), 1) + begin
    part = volumes_ref[pl.ds(begin, LANES)].reshape(1, LANES)
    return jnp.where(ids < live_ref[0], part, 0.0)


def sums_kernel(total_rows, snapshots_ref, volumes_ref, live_ref, probes_ref, core_ref, keep_ref, send_ref, packed):
    row_count, order = snapshots_ref.shape
    probes = probes_ref.shape[0]
    half = order // 2
    volume = jnp.concatenate([live_volumes(volumes_ref, live_ref, b) for b in range(0, row_count, LANES)], axis=1)
    snapshots = snapshots_ref[...]
    scaled = snapshots.T * (volume * (1.0 / total_rows))
    gram = jnp.dot(scaled, snapshots, precision=HIGHEST, preferred_element_type=F32)
    probe_scaled = probes_ref[...] * (volume * (1.0 / total_rows**0.5))
    cross = jnp.dot(probe_scaled, snapshots, precision=HIGHEST, preferred_element_type=F32)
    row_ids = lax.broadcasted_iota(jnp.int32, (half, half), 0)
    column_ids = lax.broadcasted_iota(jnp.int32, (half, half), 1)
    packed[:half, :half] = jnp.where(row_ids <= column_ids, gram[:half, :half], gram[half:, half:])
    packed[:half, half:] = gram[:half, half:]
    packed[half : half + probes, :] = cross
    rest = packed.shape[0] - half - probes
    packed[half + probes :, :] = jnp.zeros((rest, order), F32)
    diagonal = jnp.sum(jnp.where(row_ids == column_ids, gram[half:, half:], 0.0), axis=0, keepdims=True)
    packed[half + probes : half + probes + 1, :half] = diagonal
    middle = packed.shape[0] // 2
    low = core_ref[0] == 0

    @pl.when(low)
    def _():
        keep_ref[...] = packed[:middle, :]
        send_ref[...] = packed[middle:, :]

    @pl.when(jnp.logical_not(low))
    def _():
        keep_ref[...] = packed[middle:, :]
        send_ref[...] = packed[:middle, :]


def local_sums(total_rows, snapshots, volumes, live_rows, probes, core):
    order = snapshots.shape[1]
    size = packed_rows(order, probes.shape[0])
    whole = pl.BlockSpec(memory_space=pltpu.VMEM)
    scalar = pl.BlockSpec(memory_space=pltpu.SMEM)
    return pl.pallas_call(
        functools.partial(sums_kernel, total_rows),
        out_shape=(jax.ShapeDtypeStruct((size // 2, order), F32),) * 2,
        in_specs=[whole, whole, scalar, whole, scalar],
        out_specs=(whole, whole),
        scratch_shapes=[pltpu.VMEM((size, order), F32)],
        compiler_params=pltpu.CompilerParams(vmem_limit_bytes=24 * 1024 * 1024),
    )(snapshots, volumes, live_rows, probes, core)


def finish_kernel(panel, mine_ref, other_ref, snapshots_ref, volumes_ref, live_ref, core_ref, basis_ref, factor_ref, coef_ref, work, linv, packed):
    row_count, order = snapshots_ref.shape
    probes = coef_ref.shape[0]
    half = order // 2
    middle = mine_ref.shape[0]
    low = core_ref[0] == 0

    @pl.when(low)
    def _():
        packed[:middle, :] = mine_ref[...]
        packed[middle:, :] = other_ref[...]

    @pl.when(jnp.logical_not(low))
    def _():
        packed[middle:, :] = mine_ref[...]
        packed[:middle, :] = other_ref[...]

    row_ids = lax.broadcasted_iota(jnp.int32, (half, half), 0)
    column_ids = lax.broadcasted_iota(jnp.int32, (half, half), 1)
    square = packed[:half, :half]
    turned = square.T
    work[:half, :half] = jnp.where(row_ids <= column_ids, square, turned)
    work[:half, half:] = packed[:half, half:]
    second = jnp.where(row_ids > column_ids, square, turned)
    diagonal = packed[half + probes : half + probes + 1, :half]
    work[half:, half:] = jnp.where(row_ids == column_ids, diagonal, second)
    work[half:, :half] = jnp.zeros((half, half), F32)
    eliminate(work, factor_ref, linv, order, panel)
    dims = (((1,), (1,)), ((), ()))
    inverse = linv[...]
    coef_ref[...] = lax.dot_general(
        packed[half : half + probes, :], inverse, dims, precision=HIGHEST, preferred_element_type=F32
    )
    for begin in range(0, row_count, LANES):
        scale = jnp.sqrt(live_volumes(volumes_ref, live_ref, begin))
        scale = jnp.broadcast_to(scale, (LANES, LANES)).T
        weighted = snapshots_ref[begin : begin + LANES, :] * jnp.concatenate([scale] * (order // LANES), axis=1)
        basis_ref[begin : begin + LANES, :] = lax.dot_general(
            weighted, inverse, dims, precision=HIGHEST, preferred_element_type=F32
        )


def finish(mine, other, snapshots, volumes, live_rows, core, probes):
    row_count, order = snapshots.shape
    whole = pl.BlockSpec(memory_space=pltpu.VMEM)
    scalar = pl.BlockSpec(memory_space=pltpu.SMEM)
    return pl.pallas_call(
        functools.partial(finish_kernel, order // 2),
        out_shape=(
            jax.ShapeDtypeStruct((row_count, order), F32),
            jax.ShapeDtypeStruct((order, order), F32),
            jax.ShapeDtypeStruct((probes, order), F32),
        ),
        in_specs=[whole] * 4 + [scalar] * 2,
        out_specs=(whole,) * 3,
        scratch_shapes=[
            pltpu.VMEM((order, order), F32),
            pltpu.VMEM((order, order), F32),
            pltpu.VMEM((2 * mine.shape[0], order), F32),
        ],
        compiler_params=pltpu.CompilerParams(vmem_limit_bytes=32 * 1024 * 1024),
    )(mine, other, snapshots, volumes, live_rows, core)


def exchange(value, bits):
    count = lax.axis_size("cells") * lax.axis_size("sub")
    return lax.ppermute(value, ("cells", "sub"), [(i, i ^ bits[i % 2]) for i in range(count)])


def reduce_halves(keep, send):
    count = lax.axis_size("cells") * lax.axis_size("sub")
    bits = [1 << k for k in range(1, count.bit_length() - 1)]
    split = len(bits) // 2
    mine = keep + exchange(send, (1, 1))
    for first, second in zip(bits[:split], bits[split : 2 * split]):
        mine = mine + exchange(mine, (first, second))
        mine = mine + exchange(mine, (second, first))
    for bit in bits[2 * split :]:
        mine = mine + exchange(mine, (bit, bit))
    return mine, exchange(mine, (1, 1))


def per_device(snapshots, volumes, live_rows, probes):
    count = lax.axis_size("cells") * lax.axis_size("sub")
    core = (lax.axis_index("sub") % 2).astype(jnp.int32).reshape(1)
    keep, send = local_sums(snapshots.shape[0] * count, snapshots, volumes, live_rows, probes, core)
    mine, other = reduce_halves(keep, send)
    return finish(mine, other, snapshots, volumes, live_rows, core, probes.shape[0])


def solution(mesh):
    placed = (
        P(("cells", "sub"), None),
        P(("cells", "sub")),
        P(("cells", "sub")),
        P(None, ("cells", "sub")),
    )
    return jax.shard_map(
        per_device,
        mesh=mesh,
        in_specs=placed,
        out_specs=(P(("cells", "sub"), None), P(), P()),
        check_vma=False,
    )
```

```python
import functools
import jax
import jax.numpy as jnp
from jax import lax
from jax.experimental import pallas as pl
from jax.experimental.pallas import tpu as pltpu
from jax.sharding import PartitionSpec as P

HIGHEST = lax.Precision.HIGHEST
LANES = 128
BLOCK = 8
F32 = jnp.float32


def recip(value):
    guess = pl.reciprocal(value, approx=True)
    guess = guess * (2.0 - value * guess)
    return guess * (2.0 - value * guess)


def lanes_of(tile, column):
    return jnp.broadcast_to(tile[:, column : column + 1], (BLOCK, LANES))


def row_of(tile, index):
    return jnp.broadcast_to(tile[index : index + 1, :], (BLOCK, LANES))


def eliminate(work, factor_ref, linv_ref, order, panel):
    tiles = order // LANES
    sub_ids = lax.broadcasted_iota(jnp.int32, (BLOCK, LANES), 0)
    lane_ids = lax.broadcasted_iota(jnp.int32, (BLOCK, LANES), 1)
    zero = jnp.zeros((BLOCK, LANES), F32)
    one = jnp.ones((BLOCK, LANES), F32)

    def load(row, tile):
        return work[row : row + BLOCK, tile * LANES : (tile + 1) * LANES]

    for start in range(0, order, BLOCK):
        first = (start // panel) * panel
        last = first + panel
        home, offset = start // LANES, start % LANES
        in_block = (lane_ids >= offset) & (lane_ids < offset + BLOCK)
        own = [load(start, t) for t in range(tiles)]
        diag_tile = own[home]
        columns = [lanes_of(diag_tile, offset + c) for c in range(BLOCK)]
        entry = {(r, c): row_of(columns[c], r) for c in range(BLOCK) for r in range(c + 1)}
        rows = [[row_of(own[t], r) for t in range(tiles)] for r in range(BLOCK)]
        kept = [rows[r][home] for r in range(BLOCK)]
        for r in range(BLOCK):
            rows[r][home] = jnp.where(in_block, jnp.where(lane_ids == offset + r, one, zero), rows[r][home])
        ahead = start + BLOCK
        follows = ahead < last
        if follows:
            below = [load(ahead, t) for t in range(tiles)]
            below_columns = [lanes_of(below[home], offset + c) for c in range(BLOCK)]
            below[home] = jnp.where(in_block, zero, below[home])
        inverse_pivot, scaled = [], {}
        for i in range(BLOCK):
            inv = recip(entry[i, i])
            inverse_pivot.append(inv)
            for r in range(i + 1, BLOCK):
                scaled[r, i] = entry[i, r] * inv
            for r in range(i + 1, BLOCK):
                for c in range(r, BLOCK):
                    entry[r, c] = entry[r, c] - scaled[r, i] * entry[i, c]
            if follows:
                weight = below_columns[i] * inv
                for c in range(i + 1, BLOCK):
                    below_columns[c] = below_columns[c] - below_columns[i] * scaled[c, i]
                for t in range(tiles):
                    below[t] = below[t] - weight * rows[i][t]
            for r in range(i + 1, BLOCK):
                for t in range(tiles):
                    rows[r][t] = rows[r][t] - scaled[r, i] * rows[i][t]
                kept[r] = kept[r] - scaled[r, i] * kept[i]
        if follows:
            for t in range(tiles):
                work[ahead : ahead + BLOCK, t * LANES : (t + 1) * LANES] = below[t]
        roots = [jnp.sqrt(entry[i, i]) * inverse_pivot[i] for i in range(BLOCK)]

        def gather(parts):
            total = parts[0]
            for r in range(1, BLOCK):
                total = jnp.where(sub_ids == r, parts[r], total)
            return total

        root = gather(roots)
        for t in range(tiles):
            merged = gather([rows[r][t] for r in range(BLOCK)]) * root
            column_ids = lane_ids + t * LANES
            lower = jnp.where(column_ids <= start + sub_ids, merged, zero)
            if t == home:
                merged_kept = gather(kept) * root
                upper = jnp.where(in_block, merged_kept, merged)
            else:
                upper = merged
            upper = jnp.where(column_ids >= start + sub_ids, upper, zero)
            factor_ref[start : start + BLOCK, t * LANES : (t + 1) * LANES] = upper
            linv_ref[start : start + BLOCK, t * LANES : (t + 1) * LANES] = lower
        if ahead + BLOCK < last:
            solved = [None] * BLOCK
            for r in reversed(range(BLOCK)):
                solved[r] = [rows[r][t] * inverse_pivot[r] for t in range(tiles)]
                for c in range(r + 1, BLOCK):
                    for t in range(tiles):
                        solved[r][t] = solved[r][t] - scaled[c, r] * solved[c][t]
            for row in range(ahead + BLOCK, last, BLOCK):
                target = [load(row, t) for t in range(tiles)]
                source = target[home]
                target[home] = jnp.where(in_block, zero, source)
                for c in range(BLOCK):
                    weight = lanes_of(source, offset + c)
                    for t in range(tiles):
                        target[t] = target[t] - weight * solved[c][t]
                for t in range(tiles):
                    work[row : row + BLOCK, t * LANES : (t + 1) * LANES] = target[t]
        if ahead == last and last < order:
            left = factor_ref[first:last, last:]
            mixed = jnp.concatenate([linv_ref[first:last, :last], factor_ref[first:last, last:]], axis=1)
            product = lax.dot_general(
                left, mixed, (((0,), (0,)), ((), ())), precision=HIGHEST, preferred_element_type=F32
            )
            ids = lax.broadcasted_iota(jnp.int32, (order - last, order), 1)
            previous = jnp.where((ids >= first) & (ids < last), 0.0, work[last:, :])
            work[last:, :] = previous - product


def piece_rows(order, probes, count):
    total = (3 * (order // 2) + probes * 2) * (order // 2 // LANES)
    return -(-total // (count * BLOCK)) * BLOCK


def live_volumes(volumes_ref, live_ref, begin):
    ids = lax.broadcasted_iota(jnp.int32, (1, LANES), 1) + begin
    part = volumes_ref[pl.ds(begin, LANES)].reshape(1, LANES)
    return jnp.where(ids < live_ref[0], part, 0.0)


def sums_kernel(total_rows, snapshots_hbm, volumes_hbm, live_ref, probes_hbm, packed, snapshots_ref, volumes_ref, probes_ref, sems):
    copies = [
        pltpu.make_async_copy(source, target, sems.at[i])
        for i, (source, target) in enumerate(
            ((volumes_hbm, volumes_ref), (snapshots_hbm, snapshots_ref), (probes_hbm, probes_ref))
        )
    ]
    for copy in copies:
        copy.start()
    row_count, order = snapshots_ref.shape
    probes = probes_ref.shape[0]
    half = order // 2
    copies[0].wait()
    volume = jnp.concatenate([live_volumes(volumes_ref, live_ref, b) for b in range(0, row_count, LANES)], axis=1)
    copies[1].wait()
    snapshots = snapshots_ref[...]
    scaled = snapshots.T * (volume * (1.0 / total_rows))
    gram = jnp.dot(scaled, snapshots, precision=HIGHEST, preferred_element_type=F32)
    packed[:half, :] = gram[:half, :half]
    packed[half : 2 * half, :] = gram[:half, half:]
    packed[2 * half : 3 * half, :] = gram[half:, half:]
    copies[2].wait()
    probe_scaled = probes_ref[...] * (volume * (1.0 / total_rows**0.5))
    cross = jnp.dot(probe_scaled, snapshots, precision=HIGHEST, preferred_element_type=F32)
    packed[3 * half : 3 * half + probes, :] = cross[:, :half]
    packed[3 * half + probes : 3 * half + 2 * probes, :] = cross[:, half:]
    rest = packed.shape[0] - 3 * half - 2 * probes
    if rest > 0:
        packed[3 * half + 2 * probes :, :] = jnp.zeros((rest, half), F32)


def local_sums(count, snapshots, volumes, live_rows, probes):
    order = snapshots.shape[1]
    rows = piece_rows(order, probes.shape[0], count) * count
    hbm = pl.BlockSpec(memory_space=pltpu.HBM)
    whole = pl.BlockSpec(memory_space=pltpu.VMEM)
    scalar = pl.BlockSpec(memory_space=pltpu.SMEM)
    return pl.pallas_call(
        functools.partial(sums_kernel, snapshots.shape[0] * count),
        out_shape=jax.ShapeDtypeStruct((rows, order // 2), F32),
        in_specs=[hbm, hbm, scalar, hbm],
        out_specs=whole,
        scratch_shapes=[
            pltpu.VMEM(snapshots.shape, F32),
            pltpu.VMEM(volumes.shape, F32),
            pltpu.VMEM(probes.shape, F32),
            pltpu.SemaphoreType.DMA((3,)),
        ],
        compiler_params=pltpu.CompilerParams(vmem_limit_bytes=60 * 1024 * 1024),
    )(snapshots, volumes, live_rows, probes)


def finish_kernel(panel, packed, snapshots_ref, volumes_ref, live_ref, basis_ref, factor_ref, coef_ref, work, linv):
    row_count, order = snapshots_ref.shape
    probes = coef_ref.shape[0]
    half = order // 2
    work[:half, :half] = packed[:half, :]
    work[:half, half:] = packed[half : 2 * half, :]
    work[half:, half:] = packed[2 * half : 3 * half, :]
    work[half:, :half] = jnp.zeros((half, half), F32)
    eliminate(work, factor_ref, linv, order, panel)
    dims = (((1,), (1,)), ((), ()))
    inverse = linv[...]
    cross = jnp.concatenate(
        [packed[3 * half : 3 * half + probes, :], packed[3 * half + probes : 3 * half + 2 * probes, :]], axis=1
    )
    coef_ref[...] = lax.dot_general(cross, inverse, dims, precision=HIGHEST, preferred_element_type=F32)
    for begin in range(0, row_count, LANES):
        scale = jnp.sqrt(live_volumes(volumes_ref, live_ref, begin))
        scale = jnp.broadcast_to(scale, (LANES, LANES)).T
        weighted = snapshots_ref[begin : begin + LANES, :] * jnp.concatenate([scale] * (order // LANES), axis=1)
        basis_ref[begin : begin + LANES, :] = lax.dot_general(
            weighted, inverse, dims, precision=HIGHEST, preferred_element_type=F32
        )


def finish(packed, snapshots, volumes, live_rows, probes):
    row_count, order = snapshots.shape
    whole = pl.BlockSpec(memory_space=pltpu.VMEM)
    scalar = pl.BlockSpec(memory_space=pltpu.SMEM)
    return pl.pallas_call(
        functools.partial(finish_kernel, order // 2),
        out_shape=(
            jax.ShapeDtypeStruct((row_count, order), F32),
            jax.ShapeDtypeStruct((order, order), F32),
            jax.ShapeDtypeStruct((probes, order), F32),
        ),
        in_specs=[whole] * 3 + [scalar],
        out_specs=(whole,) * 3,
        scratch_shapes=[pltpu.VMEM((order, order), F32), pltpu.VMEM((order, order), F32)],
        compiler_params=pltpu.CompilerParams(vmem_limit_bytes=32 * 1024 * 1024),
    )(packed, snapshots, volumes, live_rows)


def sum_everywhere(packed):
    axes = ("cells", "sub")
    count = lax.axis_size("cells") * lax.axis_size("sub")
    pieces = packed.reshape(count, packed.shape[0] // count, packed.shape[1])
    mine = jnp.sum(lax.all_to_all(pieces, axes, 0, 0), axis=0)
    return lax.all_to_all(jnp.broadcast_to(mine, pieces.shape), axes, 0, 0).reshape(packed.shape)


def per_device(snapshots, volumes, live_rows, probes):
    count = lax.axis_size("cells") * lax.axis_size("sub")
    packed = local_sums(count, snapshots, volumes, live_rows, probes)
    return finish(sum_everywhere(packed), snapshots, volumes, live_rows, probes.shape[0])


def solution(mesh):
    placed = (
        P(("cells", "sub"), None),
        P(("cells", "sub")),
        P(("cells", "sub")),
        P(None, ("cells", "sub")),
    )
    return jax.shard_map(
        per_device,
        mesh=mesh,
        in_specs=placed,
        out_specs=(P(("cells", "sub"), None), P(), P()),
        check_vma=False,
    )
```

```python
import functools
import jax
import jax.numpy as jnp
from jax import lax
from jax.experimental import pallas as pl
from jax.experimental.pallas import tpu as pltpu
from jax.sharding import PartitionSpec as P

HIGHEST = lax.Precision.HIGHEST
LANES = 128
BLOCK = 8
F32 = jnp.float32


def recip(value):
    guess = pl.reciprocal(value, approx=True)
    guess = guess * (2.0 - value * guess)
    return guess * (2.0 - value * guess)


def lanes_of(tile, column):
    return jnp.broadcast_to(tile[:, column : column + 1], (BLOCK, LANES))


def row_of(tile, index):
    return jnp.broadcast_to(tile[index : index + 1, :], (BLOCK, LANES))


def eliminate(work, factor_ref, linv_ref, order, panel):
    tiles = order // LANES
    sub_ids = lax.broadcasted_iota(jnp.int32, (BLOCK, LANES), 0)
    lane_ids = lax.broadcasted_iota(jnp.int32, (BLOCK, LANES), 1)
    zero = jnp.zeros((BLOCK, LANES), F32)
    one = jnp.ones((BLOCK, LANES), F32)

    def load(row, tile):
        return work[row : row + BLOCK, tile * LANES : (tile + 1) * LANES]

    for start in range(0, order, BLOCK):
        first = (start // panel) * panel
        last = first + panel
        home, offset = start // LANES, start % LANES
        in_block = (lane_ids >= offset) & (lane_ids < offset + BLOCK)
        own = [load(start, t) for t in range(tiles)]
        diag_tile = own[home]
        columns = [lanes_of(diag_tile, offset + c) for c in range(BLOCK)]
        entry = {(r, c): row_of(columns[c], r) for c in range(BLOCK) for r in range(c + 1)}
        rows = [[row_of(own[t], r) for t in range(tiles)] for r in range(BLOCK)]
        kept = [rows[r][home] for r in range(BLOCK)]
        for r in range(BLOCK):
            rows[r][home] = jnp.where(in_block, jnp.where(lane_ids == offset + r, one, zero), rows[r][home])
        ahead = start + BLOCK
        follows = ahead < last
        if follows:
            below = [load(ahead, t) for t in range(tiles)]
            below_columns = [lanes_of(below[home], offset + c) for c in range(BLOCK)]
            below[home] = jnp.where(in_block, zero, below[home])
        inverse_pivot, scaled = [], {}
        for i in range(BLOCK):
            inv = recip(entry[i, i])
            inverse_pivot.append(inv)
            for r in range(i + 1, BLOCK):
                scaled[r, i] = entry[i, r] * inv
            for r in range(i + 1, BLOCK):
                for c in range(r, BLOCK):
                    entry[r, c] = entry[r, c] - scaled[r, i] * entry[i, c]
            if follows:
                weight = below_columns[i] * inv
                for c in range(i + 1, BLOCK):
                    below_columns[c] = below_columns[c] - below_columns[i] * scaled[c, i]
                for t in range(tiles):
                    below[t] = below[t] - weight * rows[i][t]
            for r in range(i + 1, BLOCK):
                for t in range(tiles):
                    rows[r][t] = rows[r][t] - scaled[r, i] * rows[i][t]
                kept[r] = kept[r] - scaled[r, i] * kept[i]
        if follows:
            for t in range(tiles):
                work[ahead : ahead + BLOCK, t * LANES : (t + 1) * LANES] = below[t]
        roots = [jnp.sqrt(entry[i, i]) * inverse_pivot[i] for i in range(BLOCK)]

        def gather(parts):
            total = parts[0]
            for r in range(1, BLOCK):
                total = jnp.where(sub_ids == r, parts[r], total)
            return total

        root = gather(roots)
        for t in range(tiles):
            merged = gather([rows[r][t] for r in range(BLOCK)]) * root
            column_ids = lane_ids + t * LANES
            lower = jnp.where(column_ids <= start + sub_ids, merged, zero)
            if t == home:
                merged_kept = gather(kept) * root
                upper = jnp.where(in_block, merged_kept, merged)
            else:
                upper = merged
            upper = jnp.where(column_ids >= start + sub_ids, upper, zero)
            factor_ref[start : start + BLOCK, t * LANES : (t + 1) * LANES] = upper
            linv_ref[start : start + BLOCK, t * LANES : (t + 1) * LANES] = lower
        if ahead + BLOCK < last:
            solved = [None] * BLOCK
            for r in reversed(range(BLOCK)):
                solved[r] = [rows[r][t] * inverse_pivot[r] for t in range(tiles)]
                for c in range(r + 1, BLOCK):
                    for t in range(tiles):
                        solved[r][t] = solved[r][t] - scaled[c, r] * solved[c][t]
            for row in range(ahead + BLOCK, last, BLOCK):
                target = [load(row, t) for t in range(tiles)]
                source = target[home]
                target[home] = jnp.where(in_block, zero, source)
                for c in range(BLOCK):
                    weight = lanes_of(source, offset + c)
                    for t in range(tiles):
                        target[t] = target[t] - weight * solved[c][t]
                for t in range(tiles):
                    work[row : row + BLOCK, t * LANES : (t + 1) * LANES] = target[t]
        if ahead == last and last < order:
            left = factor_ref[first:last, last:]
            mixed = jnp.concatenate([linv_ref[first:last, :last], factor_ref[first:last, last:]], axis=1)
            product = lax.dot_general(
                left, mixed, (((0,), (0,)), ((), ())), precision=HIGHEST, preferred_element_type=F32
            )
            ids = lax.broadcasted_iota(jnp.int32, (order - last, order), 1)
            previous = jnp.where((ids >= first) & (ids < last), 0.0, work[last:, :])
            work[last:, :] = previous - product


def piece_rows(order, probes, count):
    total = (3 * (order // 2) + probes * 2) * (order // 2 // LANES)
    return -(-total // (count * BLOCK)) * BLOCK


def live_volumes(volumes_ref, live_ref, begin):
    ids = lax.broadcasted_iota(jnp.int32, (1, LANES), 1) + begin
    part = volumes_ref[pl.ds(begin, LANES)].reshape(1, LANES)
    return jnp.where(ids < live_ref[0], part, 0.0)


def sums_kernel(total_rows, snapshots_hbm, volumes_hbm, live_ref, probes_hbm, packed, snapshots_ref, volumes_ref, probes_ref, sems):
    copies = [
        pltpu.make_async_copy(source, target, sems.at[i])
        for i, (source, target) in enumerate(
            ((volumes_hbm, volumes_ref), (snapshots_hbm, snapshots_ref), (probes_hbm, probes_ref))
        )
    ]
    for copy in copies:
        copy.start()
    row_count, order = snapshots_ref.shape
    probes = probes_ref.shape[0]
    half = order // 2
    copies[0].wait()
    volume = jnp.concatenate([live_volumes(volumes_ref, live_ref, b) for b in range(0, row_count, LANES)], axis=1)
    copies[1].wait()
    snapshots = snapshots_ref[...]
    scaled = snapshots.T * (volume * (1.0 / total_rows))
    gram = jnp.dot(scaled, snapshots, precision=HIGHEST, preferred_element_type=F32)
    packed[:half, :] = gram[:half, :half]
    packed[half : 2 * half, :] = gram[:half, half:]
    packed[2 * half : 3 * half, :] = gram[half:, half:]
    copies[2].wait()
    probe_scaled = probes_ref[...] * (volume * (1.0 / total_rows**0.5))
    cross = jnp.dot(probe_scaled, snapshots, precision=HIGHEST, preferred_element_type=F32)
    packed[3 * half : 3 * half + probes, :] = cross[:, :half]
    packed[3 * half + probes : 3 * half + 2 * probes, :] = cross[:, half:]
    rest = packed.shape[0] - 3 * half - 2 * probes
    if rest > 0:
        packed[3 * half + 2 * probes :, :] = jnp.zeros((rest, half), F32)


def local_sums(count, snapshots, volumes, live_rows, probes):
    order = snapshots.shape[1]
    rows = piece_rows(order, probes.shape[0], count) * count
    hbm = pl.BlockSpec(memory_space=pltpu.HBM)
    whole = pl.BlockSpec(memory_space=pltpu.VMEM)
    scalar = pl.BlockSpec(memory_space=pltpu.SMEM)
    return pl.pallas_call(
        functools.partial(sums_kernel, snapshots.shape[0] * count),
        out_shape=jax.ShapeDtypeStruct((rows, order // 2), F32),
        in_specs=[hbm, hbm, scalar, hbm],
        out_specs=whole,
        scratch_shapes=[
            pltpu.VMEM(snapshots.shape, F32),
            pltpu.VMEM(volumes.shape, F32),
            pltpu.VMEM(probes.shape, F32),
            pltpu.SemaphoreType.DMA((3,)),
        ],
        compiler_params=pltpu.CompilerParams(vmem_limit_bytes=60 * 1024 * 1024),
    )(snapshots, volumes, live_rows, probes)


def finish_kernel(panel, packed, snapshots_ref, volumes_ref, live_ref, basis_ref, factor_ref, coef_ref, work, linv):
    row_count, order = snapshots_ref.shape
    probes = coef_ref.shape[0]
    half = order // 2
    work[:half, :half] = packed[:half, :]
    work[:half, half:] = packed[half : 2 * half, :]
    work[half:, half:] = packed[2 * half : 3 * half, :]
    work[half:, :half] = jnp.zeros((half, half), F32)
    eliminate(work, factor_ref, linv, order, panel)
    dims = (((1,), (1,)), ((), ()))
    inverse = linv[...]
    cross = jnp.concatenate(
        [packed[3 * half : 3 * half + probes, :], packed[3 * half + probes : 3 * half + 2 * probes, :]], axis=1
    )
    coef_ref[...] = lax.dot_general(cross, inverse, dims, precision=HIGHEST, preferred_element_type=F32)
    for begin in range(0, row_count, LANES):
        scale = jnp.sqrt(live_volumes(volumes_ref, live_ref, begin))
        scale = jnp.broadcast_to(scale, (LANES, LANES)).T
        weighted = snapshots_ref[begin : begin + LANES, :] * jnp.concatenate([scale] * (order // LANES), axis=1)
        basis_ref[begin : begin + LANES, :] = lax.dot_general(
            weighted, inverse, dims, precision=HIGHEST, preferred_element_type=F32
        )


def finish(packed, snapshots, volumes, live_rows, probes):
    row_count, order = snapshots.shape
    whole = pl.BlockSpec(memory_space=pltpu.VMEM)
    scalar = pl.BlockSpec(memory_space=pltpu.SMEM)
    return pl.pallas_call(
        functools.partial(finish_kernel, order // 2),
        out_shape=(
            jax.ShapeDtypeStruct((row_count, order), F32),
            jax.ShapeDtypeStruct((order, order), F32),
            jax.ShapeDtypeStruct((probes, order), F32),
        ),
        in_specs=[whole] * 3 + [scalar],
        out_specs=(whole,) * 3,
        scratch_shapes=[pltpu.VMEM((order, order), F32), pltpu.VMEM((order, order), F32)],
        compiler_params=pltpu.CompilerParams(vmem_limit_bytes=32 * 1024 * 1024),
    )(packed, snapshots, volumes, live_rows)


def spread(pieces, groups):
    return lax.all_to_all(pieces, ("cells", "sub"), 0, 0, axis_index_groups=groups)


def sum_everywhere(packed):
    count = lax.axis_size("cells") * lax.axis_size("sub")
    near = min(count, 8)
    far = count // near
    inner = [[g * near + k for k in range(near)] for g in range(far)]
    outer = [[g * near + k for g in range(far)] for k in range(near)]
    rows, lanes = packed.shape
    mine = jnp.sum(spread(packed.reshape(near, rows // near, lanes), inner), axis=0)
    mine = jnp.sum(spread(jnp.broadcast_to(mine, (far,) + mine.shape), outer), axis=0)
    return spread(jnp.broadcast_to(mine, (near,) + mine.shape), inner).reshape(rows, lanes)


def per_device(snapshots, volumes, live_rows, probes):
    count = lax.axis_size("cells") * lax.axis_size("sub")
    packed = local_sums(count, snapshots, volumes, live_rows, probes)
    return finish(sum_everywhere(packed), snapshots, volumes, live_rows, probes.shape[0])


def solution(mesh):
    placed = (
        P(("cells", "sub"), None),
        P(("cells", "sub")),
        P(("cells", "sub")),
        P(None, ("cells", "sub")),
    )
    return jax.shard_map(
        per_device,
        mesh=mesh,
        in_specs=placed,
        out_specs=(P(("cells", "sub"), None), P(), P()),
        check_vma=False,
    )
```

```python
import functools
import jax
import jax.numpy as jnp
from jax import lax
from jax.experimental import pallas as pl
from jax.experimental.pallas import tpu as pltpu
from jax.sharding import PartitionSpec as P

HIGHEST = lax.Precision.HIGHEST
LANES = 128
BLOCK = 8
F32 = jnp.float32


def recip(value):
    guess = pl.reciprocal(value, approx=True)
    guess = guess * (2.0 - value * guess)
    return guess * (2.0 - value * guess)


def lanes_of(tile, column):
    return jnp.broadcast_to(tile[:, column : column + 1], (BLOCK, LANES))


def row_of(tile, index):
    return jnp.broadcast_to(tile[index : index + 1, :], (BLOCK, LANES))


def eliminate(work, factor_ref, linv_ref, order, panel):
    tiles = order // LANES
    sub_ids = lax.broadcasted_iota(jnp.int32, (BLOCK, LANES), 0)
    lane_ids = lax.broadcasted_iota(jnp.int32, (BLOCK, LANES), 1)
    zero = jnp.zeros((BLOCK, LANES), F32)
    one = jnp.ones((BLOCK, LANES), F32)

    def load(row, tile):
        return work[row : row + BLOCK, tile * LANES : (tile + 1) * LANES]

    for start in range(0, order, BLOCK):
        first = (start // panel) * panel
        last = first + panel
        home, offset = start // LANES, start % LANES
        in_block = (lane_ids >= offset) & (lane_ids < offset + BLOCK)
        own = [load(start, t) for t in range(tiles)]
        diag_tile = own[home]
        columns = [lanes_of(diag_tile, offset + c) for c in range(BLOCK)]
        entry = {(r, c): row_of(columns[c], r) for c in range(BLOCK) for r in range(c + 1)}
        rows = [[row_of(own[t], r) for t in range(tiles)] for r in range(BLOCK)]
        kept = [rows[r][home] for r in range(BLOCK)]
        for r in range(BLOCK):
            rows[r][home] = jnp.where(in_block, jnp.where(lane_ids == offset + r, one, zero), rows[r][home])
        ahead = start + BLOCK
        follows = ahead < last
        if follows:
            below = [load(ahead, t) for t in range(tiles)]
            below_columns = [lanes_of(below[home], offset + c) for c in range(BLOCK)]
            below[home] = jnp.where(in_block, zero, below[home])
        inverse_pivot, scaled = [], {}
        for i in range(BLOCK):
            inv = recip(entry[i, i])
            inverse_pivot.append(inv)
            for r in range(i + 1, BLOCK):
                scaled[r, i] = entry[i, r] * inv
            for r in range(i + 1, BLOCK):
                for c in range(r, BLOCK):
                    entry[r, c] = entry[r, c] - scaled[r, i] * entry[i, c]
            if follows:
                weight = below_columns[i] * inv
                for c in range(i + 1, BLOCK):
                    below_columns[c] = below_columns[c] - below_columns[i] * scaled[c, i]
                for t in range(tiles):
                    below[t] = below[t] - weight * rows[i][t]
            for r in range(i + 1, BLOCK):
                for t in range(tiles):
                    rows[r][t] = rows[r][t] - scaled[r, i] * rows[i][t]
                kept[r] = kept[r] - scaled[r, i] * kept[i]
        if follows:
            for t in range(tiles):
                work[ahead : ahead + BLOCK, t * LANES : (t + 1) * LANES] = below[t]
        roots = [jnp.sqrt(entry[i, i]) * inverse_pivot[i] for i in range(BLOCK)]

        def gather(parts):
            total = parts[0]
            for r in range(1, BLOCK):
                total = jnp.where(sub_ids == r, parts[r], total)
            return total

        root = gather(roots)
        for t in range(tiles):
            merged = gather([rows[r][t] for r in range(BLOCK)]) * root
            column_ids = lane_ids + t * LANES
            lower = jnp.where(column_ids <= start + sub_ids, merged, zero)
            if t == home:
                merged_kept = gather(kept) * root
                upper = jnp.where(in_block, merged_kept, merged)
            else:
                upper = merged
            upper = jnp.where(column_ids >= start + sub_ids, upper, zero)
            factor_ref[start : start + BLOCK, t * LANES : (t + 1) * LANES] = upper
            linv_ref[start : start + BLOCK, t * LANES : (t + 1) * LANES] = lower
        if ahead + BLOCK < last:
            solved = [None] * BLOCK
            for r in reversed(range(BLOCK)):
                solved[r] = [rows[r][t] * inverse_pivot[r] for t in range(tiles)]
                for c in range(r + 1, BLOCK):
                    for t in range(tiles):
                        solved[r][t] = solved[r][t] - scaled[c, r] * solved[c][t]
            for row in range(ahead + BLOCK, last, BLOCK):
                target = [load(row, t) for t in range(tiles)]
                source = target[home]
                target[home] = jnp.where(in_block, zero, source)
                for c in range(BLOCK):
                    weight = lanes_of(source, offset + c)
                    for t in range(tiles):
                        target[t] = target[t] - weight * solved[c][t]
                for t in range(tiles):
                    work[row : row + BLOCK, t * LANES : (t + 1) * LANES] = target[t]
        if ahead == last and last < order:
            left = factor_ref[first:last, last:]
            mixed = jnp.concatenate([linv_ref[first:last, :last], factor_ref[first:last, last:]], axis=1)
            product = lax.dot_general(
                left, mixed, (((0,), (0,)), ((), ())), precision=HIGHEST, preferred_element_type=F32
            )
            ids = lax.broadcasted_iota(jnp.int32, (order - last, order), 1)
            previous = jnp.where((ids >= first) & (ids < last), 0.0, work[last:, :])
            work[last:, :] = previous - product


def live_volumes(volumes_ref, live_ref, begin):
    ids = lax.broadcasted_iota(jnp.int32, (1, LANES), 1) + begin
    part = volumes_ref[pl.ds(begin, LANES)].reshape(1, LANES)
    return jnp.where(ids < live_ref[0], part, 0.0)


def sums_kernel(total_rows, snapshots_hbm, volumes_hbm, live_ref, probes_hbm, head_ref, tail_ref, snapshots_ref, volumes_ref, probes_ref, sems):
    copies = [
        pltpu.make_async_copy(source, target, sems.at[i])
        for i, (source, target) in enumerate(
            ((volumes_hbm, volumes_ref), (snapshots_hbm, snapshots_ref), (probes_hbm, probes_ref))
        )
    ]
    for copy in copies:
        copy.start()
    row_count, order = snapshots_ref.shape
    probes = probes_ref.shape[0]
    half = order // 2
    moved = head_ref.shape[0] - half
    copies[0].wait()
    volume = jnp.concatenate([live_volumes(volumes_ref, live_ref, b) for b in range(0, row_count, LANES)], axis=1)
    copies[1].wait()
    snapshots = snapshots_ref[...]
    scaled = snapshots.T * (volume * (1.0 / total_rows))
    gram = jnp.dot(scaled, snapshots, precision=HIGHEST, preferred_element_type=F32)
    row_ids = lax.broadcasted_iota(jnp.int32, (half, half), 0)
    column_ids = lax.broadcasted_iota(jnp.int32, (half, half), 1)
    second = gram[half:, half:]
    head_ref[:half, :half] = jnp.where(row_ids <= column_ids, gram[:half, :half], second)
    head_ref[:half, half:] = gram[:half, half:]
    diagonal = jnp.sum(jnp.where(row_ids == column_ids, second, 0.0), axis=0, keepdims=True)
    tail_ref[probes - moved :, :] = jnp.concatenate([jnp.broadcast_to(diagonal, (BLOCK, half))] * 2, axis=1)
    copies[2].wait()
    probe_scaled = probes_ref[...] * (volume * (1.0 / total_rows**0.5))
    cross = jnp.dot(probe_scaled, snapshots, precision=HIGHEST, preferred_element_type=F32)
    head_ref[half:, :] = cross[:moved, :]
    tail_ref[: probes - moved, :] = cross[moved:, :]


def local_sums(count, snapshots, volumes, live_rows, probes):
    order = snapshots.shape[1]
    moved = probes.shape[0] // 4
    hbm = pl.BlockSpec(memory_space=pltpu.HBM)
    whole = pl.BlockSpec(memory_space=pltpu.VMEM)
    scalar = pl.BlockSpec(memory_space=pltpu.SMEM)
    return pl.pallas_call(
        functools.partial(sums_kernel, snapshots.shape[0] * count),
        out_shape=(
            jax.ShapeDtypeStruct((order // 2 + moved, order), F32),
            jax.ShapeDtypeStruct((probes.shape[0] - moved + BLOCK, order), F32),
        ),
        in_specs=[hbm, hbm, scalar, hbm],
        out_specs=(whole, whole),
        scratch_shapes=[
            pltpu.VMEM(snapshots.shape, F32),
            pltpu.VMEM(volumes.shape, F32),
            pltpu.VMEM(probes.shape, F32),
            pltpu.SemaphoreType.DMA((3,)),
        ],
        compiler_params=pltpu.CompilerParams(vmem_limit_bytes=60 * 1024 * 1024),
    )(snapshots, volumes, live_rows, probes)


def finish_kernel(panel, head_mine, head_other, tail_mine, tail_other, snapshots_ref, volumes_ref, live_ref, core_ref, basis_ref, factor_ref, coef_ref, work, linv):
    row_count, order = snapshots_ref.shape
    probes = coef_ref.shape[0]
    half = order // 2
    own = core_ref[0] == 1
    head = jnp.where(own, head_mine[...], head_other[...])
    tail = jnp.where(own, tail_other[...], tail_mine[...])
    gram, diagonal = head[:half, :], tail[-1:, :half]
    cross = jnp.concatenate([head[half:, :], tail[:-BLOCK, :]], axis=0)
    row_ids = lax.broadcasted_iota(jnp.int32, (half, half), 0)
    column_ids = lax.broadcasted_iota(jnp.int32, (half, half), 1)
    square = gram[:, :half]
    turned = square.T
    work[:half, :half] = jnp.where(row_ids <= column_ids, square, turned)
    work[:half, half:] = gram[:, half:]
    second = jnp.where(row_ids > column_ids, square, turned)
    work[half:, half:] = jnp.where(row_ids == column_ids, diagonal, second)
    work[half:, :half] = jnp.zeros((half, half), F32)
    eliminate(work, factor_ref, linv, order, panel)
    dims = (((1,), (1,)), ((), ()))
    inverse = linv[...]
    coef_ref[...] = lax.dot_general(cross, inverse, dims, precision=HIGHEST, preferred_element_type=F32)
    for begin in range(0, row_count, LANES):
        scale = jnp.sqrt(live_volumes(volumes_ref, live_ref, begin))
        scale = jnp.broadcast_to(scale, (LANES, LANES)).T
        weighted = snapshots_ref[begin : begin + LANES, :] * jnp.concatenate([scale] * (order // LANES), axis=1)
        basis_ref[begin : begin + LANES, :] = lax.dot_general(
            weighted, inverse, dims, precision=HIGHEST, preferred_element_type=F32
        )


def finish(heads, tails, probes, snapshots, volumes, live_rows, core):
    row_count, order = snapshots.shape
    whole = pl.BlockSpec(memory_space=pltpu.VMEM)
    scalar = pl.BlockSpec(memory_space=pltpu.SMEM)
    return pl.pallas_call(
        functools.partial(finish_kernel, order // 2),
        out_shape=(
            jax.ShapeDtypeStruct((row_count, order), F32),
            jax.ShapeDtypeStruct((order, order), F32),
            jax.ShapeDtypeStruct((probes, order), F32),
        ),
        in_specs=[whole] * 6 + [scalar] * 2,
        out_specs=(whole,) * 3,
        scratch_shapes=[pltpu.VMEM((order, order), F32), pltpu.VMEM((order, order), F32)],
        compiler_params=pltpu.CompilerParams(vmem_limit_bytes=32 * 1024 * 1024),
    )(*heads, *tails, snapshots, volumes, live_rows, core)


def sum_parts(head, tail):
    count = lax.axis_size("cells") * lax.axis_size("sub")
    odd, even = range(1, count, 2), range(0, count, 2)

    def send(value, pairs):
        return lax.ppermute(value, ("cells", "sub"), pairs)

    def step(value, members, bit):
        return value + send(value, [(i, i ^ bit) for i in members])

    up, down = [(i, i + 1) for i in even], [(i, i - 1) for i in odd]
    head, tail = lax.optimization_barrier((head + send(head, up), tail + send(tail, down)))
    bits = [1 << k for k in range(1, count.bit_length() - 1)]
    split = len(bits) // 2
    for low, high in zip(bits[:split], bits[split : 2 * split]):
        head, tail = step(head, odd, high), step(tail, even, low)
        head, tail = step(head, odd, low), step(tail, even, high)
    for bit in bits[2 * split :]:
        head, tail = step(head, odd, bit), step(tail, even, bit)
    return (head, send(head, down)), (tail, send(tail, up))


def per_device(snapshots, volumes, live_rows, probes):
    count = lax.axis_size("cells") * lax.axis_size("sub")
    core = (lax.axis_index("sub") % 2).astype(jnp.int32).reshape(1)
    head, tail = local_sums(count, snapshots, volumes, live_rows, probes)
    heads, tails = sum_parts(head, tail)
    return finish(heads, tails, probes.shape[0], snapshots, volumes, live_rows, core)


def solution(mesh):
    placed = (
        P(("cells", "sub"), None),
        P(("cells", "sub")),
        P(("cells", "sub")),
        P(None, ("cells", "sub")),
    )
    return jax.shard_map(
        per_device,
        mesh=mesh,
        in_specs=placed,
        out_specs=(P(("cells", "sub"), None), P(), P()),
        check_vma=False,
    )
```

```python
import functools
import jax
import jax.numpy as jnp
from jax import lax
from jax.experimental import pallas as pl
from jax.experimental.pallas import tpu as pltpu
from jax.sharding import PartitionSpec as P

HIGHEST = lax.Precision.HIGHEST
LANES = 128
BLOCK = 8
AHEAD = 2
F32 = jnp.float32


def lanes_of(tile, column):
    return jnp.broadcast_to(tile[:, column : column + 1], tile.shape)


def row_of(tile, index):
    return jnp.broadcast_to(tile[index : index + 1, :], tile.shape)


def product(left, right, dims):
    return lax.dot_general(left, right, (dims, ((), ())), precision=HIGHEST, preferred_element_type=F32)


def eliminate(matrix):
    width = matrix.shape[1]
    count = width // BLOCK
    shape = (BLOCK, width)
    tiles = [matrix[k * BLOCK : (k + 1) * BLOCK, :] for k in range(count)]
    sub_ids = lax.broadcasted_iota(jnp.int32, shape, 0)
    lane_ids = lax.broadcasted_iota(jnp.int32, shape, 1)
    spread_ids = lane_ids - sub_ids

    def gather(parts):
        total = parts[0]
        for r in range(1, BLOCK):
            total = jnp.where(sub_ids == r, parts[r], total)
        return total

    upper_rows, lower_rows = [], []
    columns = [lanes_of(tiles[0], c) for c in range(BLOCK)]
    for block in range(count):
        offset = block * BLOCK
        in_block = (lane_ids >= offset) & (lane_ids < offset + BLOCK)
        own = tiles[block]
        entry = {(r, c): row_of(columns[c], r) for c in range(BLOCK) for r in range(c + 1)}
        kept = [row_of(own, r) for r in range(BLOCK)]
        own = jnp.where(in_block, jnp.where(spread_ids == offset, 1.0, 0.0), own)
        rows = [row_of(own, r) for r in range(BLOCK)]
        near = range(block + 1, min(block + 1 + AHEAD, count))
        weights = {k: [lanes_of(tiles[k], offset + c) for c in range(BLOCK)] for k in near}
        if block + 1 < count:
            columns = [lanes_of(tiles[block + 1], offset + BLOCK + c) for c in range(BLOCK)]
        for k in near:
            tiles[k] = jnp.where(in_block, 0.0, tiles[k])
        inverse, scaled = [], {}
        for i in range(BLOCK):
            inv = pl.reciprocal(entry[i, i], approx=True)
            inverse.append(inv)
            if i + 1 < BLOCK:
                square = entry[i, i + 1] * entry[i, i + 1]
                entry[i + 1, i + 1] = entry[i + 1, i + 1] - square * inv
            for r in range(i + 1, BLOCK):
                scaled[r, i] = entry[i, r] * inv
            for r in range(i + 1, BLOCK):
                for c in range(r, BLOCK):
                    if (r, c) != (i + 1, i + 1):
                        entry[r, c] = entry[r, c] - scaled[r, i] * entry[i, c]
            for k in near:
                here = weights[k][i]
                weight = here * inv
                if k == block + 1:
                    for c in range(BLOCK):
                        columns[c] = columns[c] - weight * row_of(here, c)
                for c in range(i + 1, BLOCK):
                    weights[k][c] = weights[k][c] - here * scaled[c, i]
                tiles[k] = tiles[k] - weight * rows[i]
            for r in range(i + 1, BLOCK):
                rows[r] = rows[r] - scaled[r, i] * rows[i]
                kept[r] = kept[r] - scaled[r, i] * kept[i]
        root = gather([lax.rsqrt(entry[i, i]) for i in range(BLOCK)])
        merged = gather(rows) * root
        diagonal = gather(kept) * root
        lower_rows.append(jnp.where(spread_ids <= offset, merged, 0.0))
        upper_rows.append(jnp.where(spread_ids >= offset, jnp.where(in_block, diagonal, merged), 0.0))
        if block + 1 + AHEAD < count:
            solved = [None] * BLOCK
            for r in reversed(range(BLOCK)):
                solved[r] = rows[r] * inverse[r]
                for c in range(r + 1, BLOCK):
                    solved[r] = solved[r] - scaled[c, r] * solved[c]
            for k in range(block + 1 + AHEAD, count):
                terms = [lanes_of(tiles[k], offset + c) * solved[c] for c in range(BLOCK)]
                while len(terms) > 1:
                    terms = [terms[t] + terms[t + 1] for t in range(0, len(terms), 2)]
                tiles[k] = jnp.where(in_block, 0.0, tiles[k]) - terms[0]
    return jnp.concatenate(upper_rows, axis=0), jnp.concatenate(lower_rows, axis=0)


def packed_rows(order, probes):
    return -(-(order // 2 + probes + 1) // (2 * BLOCK)) * 2 * BLOCK


def live_volumes(volumes_ref, live_ref, begin):
    ids = lax.broadcasted_iota(jnp.int32, (1, LANES), 1) + begin
    part = volumes_ref[pl.ds(begin, LANES)].reshape(1, LANES)
    return jnp.where(ids < live_ref[0], part, 0.0)


def sums_kernel(total_rows, snapshots_hbm, volumes_hbm, live_ref, probes_hbm, core_ref, keep_ref, send_ref, snapshots_ref, volumes_ref, probes_ref, packed, sems):
    copies = [
        pltpu.make_async_copy(source, target, sems.at[i])
        for i, (source, target) in enumerate(
            ((volumes_hbm, volumes_ref), (snapshots_hbm, snapshots_ref), (probes_hbm, probes_ref))
        )
    ]
    for copy in copies:
        copy.start()
    row_count, order = snapshots_ref.shape
    probes = probes_ref.shape[0]
    half = order // 2
    copies[0].wait()
    volume = jnp.concatenate([live_volumes(volumes_ref, live_ref, b) for b in range(0, row_count, LANES)], axis=1)
    copies[1].wait()
    snapshots = snapshots_ref[...]
    scaled = snapshots.T * (volume * (1.0 / total_rows))
    gram = product(scaled, snapshots, ((1,), (0,)))
    row_ids = lax.broadcasted_iota(jnp.int32, (half, half), 0)
    column_ids = lax.broadcasted_iota(jnp.int32, (half, half), 1)
    packed[:half, :half] = jnp.where(row_ids <= column_ids, gram[:half, :half], gram[half:, half:])
    packed[:half, half:] = gram[:half, half:]
    rest = packed.shape[0] - half - probes
    diagonal = jnp.sum(jnp.where(row_ids == column_ids, gram[half:, half:], 0.0), axis=0, keepdims=True)
    packed[half + probes :, :] = jnp.concatenate([jnp.broadcast_to(diagonal, (rest, half))] * 2, axis=1)
    copies[2].wait()
    probe_scaled = probes_ref[...] * (volume * (1.0 / total_rows**0.5))
    packed[half : half + probes, :] = product(probe_scaled, snapshots, ((1,), (0,)))
    middle = packed.shape[0] // 2
    low = core_ref[0] == 0

    @pl.when(low)
    def _():
        keep_ref[...] = packed[:middle, :]
        send_ref[...] = packed[middle:, :]

    @pl.when(jnp.logical_not(low))
    def _():
        keep_ref[...] = packed[middle:, :]
        send_ref[...] = packed[:middle, :]


def local_sums(total_rows, snapshots, volumes, live_rows, probes, core):
    order = snapshots.shape[1]
    size = packed_rows(order, probes.shape[0])
    hbm = pl.BlockSpec(memory_space=pltpu.HBM)
    whole = pl.BlockSpec(memory_space=pltpu.VMEM)
    scalar = pl.BlockSpec(memory_space=pltpu.SMEM)
    return pl.pallas_call(
        functools.partial(sums_kernel, total_rows),
        out_shape=(jax.ShapeDtypeStruct((size // 2, order), F32),) * 2,
        in_specs=[hbm, hbm, scalar, hbm, scalar],
        out_specs=(whole, whole),
        scratch_shapes=[
            pltpu.VMEM(snapshots.shape, F32),
            pltpu.VMEM(volumes.shape, F32),
            pltpu.VMEM(probes.shape, F32),
            pltpu.VMEM((size, order), F32),
            pltpu.SemaphoreType.DMA((3,)),
        ],
        compiler_params=pltpu.CompilerParams(vmem_limit_bytes=60 * 1024 * 1024),
    )(snapshots, volumes, live_rows, probes, core)


def finish_kernel(mine_ref, other_ref, snapshots_ref, volumes_ref, live_ref, core_ref, basis_ref, factor_ref, coef_ref):
    row_count, order = snapshots_ref.shape
    probes = coef_ref.shape[0]
    half = order // 2
    low = core_ref[0] == 0
    mine, other = mine_ref[...], other_ref[...]
    packed = jnp.concatenate([jnp.where(low, mine, other), jnp.where(low, other, mine)], axis=0)
    row_ids = lax.broadcasted_iota(jnp.int32, (half, half), 0)
    column_ids = lax.broadcasted_iota(jnp.int32, (half, half), 1)
    square = packed[:half, :half]
    turned = square.T
    cross = packed[half : half + probes, :]
    diagonal = packed[half + probes : half + probes + 1, :half]

    upper, inverse = eliminate(jnp.where(row_ids <= column_ids, square, turned))
    factor_ref[:half, :half] = upper
    factor_ref[half:, :half] = jnp.zeros((half, half), F32)
    beside = product(inverse, packed[:half, half:], ((1,), (0,)))
    factor_ref[:half, half:] = beside
    second = jnp.where(row_ids > column_ids, square, turned)
    second = jnp.where(row_ids == column_ids, diagonal, second) - product(beside, beside, ((0,), (0,)))

    def first_columns(block):
        left = product(block[:, :half], inverse, ((1,), (1,)))
        return left, block[:, half:] - product(left, beside, ((1,), (0,)))

    left, cross_rest = first_columns(cross)
    coef_ref[:, :half] = left
    rest = []
    for begin in range(0, row_count, LANES):
        scale = jnp.sqrt(live_volumes(volumes_ref, live_ref, begin))
        scale = jnp.broadcast_to(scale, (LANES, LANES)).T
        weighted = snapshots_ref[begin : begin + LANES, :] * jnp.concatenate([scale] * (order // LANES), axis=1)
        left, right = first_columns(weighted)
        basis_ref[begin : begin + LANES, :half] = left
        rest.append(right)

    upper, inverse_second = eliminate(second)
    factor_ref[half:, half:] = upper
    coef_ref[:, half:] = product(cross_rest, inverse_second, ((1,), (1,)))
    for begin in range(0, row_count, LANES):
        basis_ref[begin : begin + LANES, half:] = product(rest[begin // LANES], inverse_second, ((1,), (1,)))


def finish(mine, other, snapshots, volumes, live_rows, core, probes):
    row_count, order = snapshots.shape
    whole = pl.BlockSpec(memory_space=pltpu.VMEM)
    scalar = pl.BlockSpec(memory_space=pltpu.SMEM)
    return pl.pallas_call(
        finish_kernel,
        out_shape=(
            jax.ShapeDtypeStruct((row_count, order), F32),
            jax.ShapeDtypeStruct((order, order), F32),
            jax.ShapeDtypeStruct((probes, order), F32),
        ),
        in_specs=[whole] * 4 + [scalar] * 2,
        out_specs=(whole,) * 3,
        compiler_params=pltpu.CompilerParams(vmem_limit_bytes=32 * 1024 * 1024),
    )(mine, other, snapshots, volumes, live_rows, core)


def exchange(value, bits):
    count = lax.axis_size("cells") * lax.axis_size("sub")
    return lax.ppermute(value, ("cells", "sub"), [(i, i ^ bits[i % 2]) for i in range(count)])


def reduce_halves(keep, send):
    count = lax.axis_size("cells") * lax.axis_size("sub")
    bits = [1 << k for k in range(1, count.bit_length() - 1)]
    split = len(bits) // 2
    mine = keep + exchange(send, (1, 1))
    for first, second in zip(bits[:split], bits[split : 2 * split]):
        mine = mine + exchange(mine, (first, second))
        mine = mine + exchange(mine, (second, first))
    for bit in bits[2 * split :]:
        mine = mine + exchange(mine, (bit, bit))
    return mine, exchange(mine, (1, 1))


def per_device(snapshots, volumes, live_rows, probes):
    count = lax.axis_size("cells") * lax.axis_size("sub")
    core = (lax.axis_index("sub") % 2).astype(jnp.int32).reshape(1)
    keep, send = local_sums(snapshots.shape[0] * count, snapshots, volumes, live_rows, probes, core)
    mine, other = reduce_halves(keep, send)
    return finish(mine, other, snapshots, volumes, live_rows, core, probes.shape[0])


def solution(mesh):
    placed = (
        P(("cells", "sub"), None),
        P(("cells", "sub")),
        P(("cells", "sub")),
        P(None, ("cells", "sub")),
    )
    return jax.shard_map(
        per_device,
        mesh=mesh,
        in_specs=placed,
        out_specs=(P(("cells", "sub"), None), P(), P()),
        check_vma=False,
    )
```

```python
import functools
import jax
import jax.numpy as jnp
from jax import lax
from jax.experimental import pallas as pl
from jax.experimental.pallas import tpu as pltpu
from jax.sharding import PartitionSpec as P

HIGHEST = lax.Precision.HIGHEST
LANES = 128
BLOCK = 8
AHEAD = 2
F32 = jnp.float32


def lanes_of(tile, column):
    return jnp.broadcast_to(tile[:, column : column + 1], tile.shape)


def row_of(tile, index):
    return jnp.broadcast_to(tile[index : index + 1, :], tile.shape)


def product(left, right, dims):
    return lax.dot_general(left, right, (dims, ((), ())), precision=HIGHEST, preferred_element_type=F32)


def eliminate(matrix):
    width = matrix.shape[1]
    count = width // BLOCK
    shape = (BLOCK, width)
    tiles = [matrix[k * BLOCK : (k + 1) * BLOCK, :] for k in range(count)]
    sub_ids = lax.broadcasted_iota(jnp.int32, shape, 0)
    lane_ids = lax.broadcasted_iota(jnp.int32, shape, 1)
    spread_ids = lane_ids - sub_ids

    def gather(parts):
        total = parts[0]
        for r in range(1, BLOCK):
            total = jnp.where(sub_ids == r, parts[r], total)
        return total

    upper_rows, lower_rows = [], []
    columns = [lanes_of(tiles[0], c) for c in range(BLOCK)]
    for block in range(count):
        offset = block * BLOCK
        in_block = (lane_ids >= offset) & (lane_ids < offset + BLOCK)
        own = tiles[block]
        entry = {(r, c): row_of(columns[c], r) for c in range(BLOCK) for r in range(c + 1)}
        kept = [row_of(own, r) for r in range(BLOCK)]
        own = jnp.where(in_block, jnp.where(spread_ids == offset, 1.0, 0.0), own)
        rows = [row_of(own, r) for r in range(BLOCK)]
        near = range(block + 1, min(block + 1 + AHEAD, count))
        weights = {k: [lanes_of(tiles[k], offset + c) for c in range(BLOCK)] for k in near}
        if block + 1 < count:
            columns = [lanes_of(tiles[block + 1], offset + BLOCK + c) for c in range(BLOCK)]
        for k in near:
            tiles[k] = jnp.where(in_block, 0.0, tiles[k])
        inverse, scaled = [], {}
        for i in range(BLOCK):
            inv = pl.reciprocal(entry[i, i], approx=True)
            inverse.append(inv)
            if i + 1 < BLOCK:
                square = entry[i, i + 1] * entry[i, i + 1]
                entry[i + 1, i + 1] = entry[i + 1, i + 1] - square * inv
            for r in range(i + 1, BLOCK):
                scaled[r, i] = entry[i, r] * inv
            for r in range(i + 1, BLOCK):
                for c in range(r, BLOCK):
                    if (r, c) != (i + 1, i + 1):
                        entry[r, c] = entry[r, c] - scaled[r, i] * entry[i, c]
            for k in near:
                here = weights[k][i]
                weight = here * inv
                if k == block + 1:
                    for c in range(BLOCK):
                        columns[c] = columns[c] - weight * row_of(here, c)
                for c in range(i + 1, BLOCK):
                    weights[k][c] = weights[k][c] - here * scaled[c, i]
                tiles[k] = tiles[k] - weight * rows[i]
            for r in range(i + 1, BLOCK):
                rows[r] = rows[r] - scaled[r, i] * rows[i]
                kept[r] = kept[r] - scaled[r, i] * kept[i]
        root = gather([lax.rsqrt(entry[i, i]) for i in range(BLOCK)])
        merged = gather(rows) * root
        diagonal = gather(kept) * root
        lower_rows.append(jnp.where(spread_ids <= offset, merged, 0.0))
        upper_rows.append(jnp.where(spread_ids >= offset, jnp.where(in_block, diagonal, merged), 0.0))
        if block + 1 + AHEAD < count:
            solved = [None] * BLOCK
            for r in reversed(range(BLOCK)):
                solved[r] = rows[r] * inverse[r]
                for c in range(r + 1, BLOCK):
                    solved[r] = solved[r] - scaled[c, r] * solved[c]
            for k in range(block + 1 + AHEAD, count):
                terms = [lanes_of(tiles[k], offset + c) * solved[c] for c in range(BLOCK)]
                while len(terms) > 1:
                    terms = [terms[t] + terms[t + 1] for t in range(0, len(terms), 2)]
                tiles[k] = jnp.where(in_block, 0.0, tiles[k]) - terms[0]
    return jnp.concatenate(upper_rows, axis=0), jnp.concatenate(lower_rows, axis=0)


def packed_rows(order, probes):
    return -(-(order // 2 + probes + 1) // (2 * BLOCK)) * 2 * BLOCK


def live_volumes(volumes_ref, live_ref, begin):
    ids = lax.broadcasted_iota(jnp.int32, (1, LANES), 1) + begin
    part = volumes_ref[pl.ds(begin, LANES)].reshape(1, LANES)
    return jnp.where(ids < live_ref[0], part, 0.0)


def sums_kernel(total_rows, snapshots_hbm, volumes_hbm, live_ref, probes_hbm, first_ref, second_ref, snapshots_ref, volumes_ref, probes_ref, packed, sems):
    copies = [
        pltpu.make_async_copy(source, target, sems.at[i])
        for i, (source, target) in enumerate(
            ((volumes_hbm, volumes_ref), (snapshots_hbm, snapshots_ref), (probes_hbm, probes_ref))
        )
    ]
    for copy in copies:
        copy.start()
    row_count, order = snapshots_ref.shape
    probes = probes_ref.shape[0]
    half = order // 2
    copies[0].wait()
    volume = jnp.concatenate([live_volumes(volumes_ref, live_ref, b) for b in range(0, row_count, LANES)], axis=1)
    copies[1].wait()
    snapshots = snapshots_ref[...]
    scaled = snapshots.T * (volume * (1.0 / total_rows))
    gram = product(scaled, snapshots, ((1,), (0,)))
    row_ids = lax.broadcasted_iota(jnp.int32, (half, half), 0)
    column_ids = lax.broadcasted_iota(jnp.int32, (half, half), 1)
    packed[:half, :half] = jnp.where(row_ids <= column_ids, gram[:half, :half], gram[half:, half:])
    packed[:half, half:] = gram[:half, half:]
    rest = packed.shape[0] - half - probes
    diagonal = jnp.sum(jnp.where(row_ids == column_ids, gram[half:, half:], 0.0), axis=0, keepdims=True)
    packed[half + probes :, :] = jnp.concatenate([jnp.broadcast_to(diagonal, (rest, half))] * 2, axis=1)
    copies[2].wait()
    probe_scaled = probes_ref[...] * (volume * (1.0 / total_rows**0.5))
    packed[half : half + probes, :] = product(probe_scaled, snapshots, ((1,), (0,)))
    middle = packed.shape[0] // 2
    first_ref[...] = packed[:middle, :]
    second_ref[...] = packed[middle:, :]


def local_sums(total_rows, snapshots, volumes, live_rows, probes):
    order = snapshots.shape[1]
    size = packed_rows(order, probes.shape[0])
    hbm = pl.BlockSpec(memory_space=pltpu.HBM)
    whole = pl.BlockSpec(memory_space=pltpu.VMEM)
    scalar = pl.BlockSpec(memory_space=pltpu.SMEM)
    return pl.pallas_call(
        functools.partial(sums_kernel, total_rows),
        out_shape=(jax.ShapeDtypeStruct((size // 2, order), F32),) * 2,
        in_specs=[hbm, hbm, scalar, hbm],
        out_specs=(whole, whole),
        scratch_shapes=[
            pltpu.VMEM(snapshots.shape, F32),
            pltpu.VMEM(volumes.shape, F32),
            pltpu.VMEM(probes.shape, F32),
            pltpu.VMEM((size, order), F32),
            pltpu.SemaphoreType.DMA((3,)),
        ],
        compiler_params=pltpu.CompilerParams(vmem_limit_bytes=54950 * 1024),
    )(snapshots, volumes, live_rows, probes)


def finish_kernel(first_own, first_other, second_own, second_other, snapshots_ref, volumes_ref, live_ref, core_ref, basis_ref, factor_ref, coef_ref):
    row_count, order = snapshots_ref.shape
    probes = coef_ref.shape[0]
    half = order // 2
    own = core_ref[0] == 1
    first = jnp.where(own, first_own[...], first_other[...])
    packed = jnp.concatenate([first, jnp.where(own, second_own[...], second_other[...])], axis=0)
    row_ids = lax.broadcasted_iota(jnp.int32, (half, half), 0)
    column_ids = lax.broadcasted_iota(jnp.int32, (half, half), 1)
    square = packed[:half, :half]
    turned = square.T
    cross = packed[half : half + probes, :]
    diagonal = packed[half + probes : half + probes + 1, :half]

    upper, inverse = eliminate(jnp.where(row_ids <= column_ids, square, turned))
    factor_ref[:half, :half] = upper
    factor_ref[half:, :half] = jnp.zeros((half, half), F32)
    beside = product(inverse, packed[:half, half:], ((1,), (0,)))
    factor_ref[:half, half:] = beside
    second = jnp.where(row_ids > column_ids, square, turned)
    second = jnp.where(row_ids == column_ids, diagonal, second) - product(beside, beside, ((0,), (0,)))

    def first_columns(block):
        left = product(block[:, :half], inverse, ((1,), (1,)))
        return left, block[:, half:] - product(left, beside, ((1,), (0,)))

    left, cross_rest = first_columns(cross)
    coef_ref[:, :half] = left
    rest = []
    for begin in range(0, row_count, LANES):
        scale = jnp.sqrt(live_volumes(volumes_ref, live_ref, begin))
        scale = jnp.broadcast_to(scale, (LANES, LANES)).T
        weighted = snapshots_ref[begin : begin + LANES, :] * jnp.concatenate([scale] * (order // LANES), axis=1)
        left, right = first_columns(weighted)
        basis_ref[begin : begin + LANES, :half] = left
        rest.append(right)

    upper, inverse_second = eliminate(second)
    factor_ref[half:, half:] = upper
    coef_ref[:, half:] = product(cross_rest, inverse_second, ((1,), (1,)))
    for begin in range(0, row_count, LANES):
        basis_ref[begin : begin + LANES, half:] = product(rest[begin // LANES], inverse_second, ((1,), (1,)))


def finish(firsts, seconds, snapshots, volumes, live_rows, core, probes):
    row_count, order = snapshots.shape
    whole = pl.BlockSpec(memory_space=pltpu.VMEM)
    scalar = pl.BlockSpec(memory_space=pltpu.SMEM)
    return pl.pallas_call(
        finish_kernel,
        out_shape=(
            jax.ShapeDtypeStruct((row_count, order), F32),
            jax.ShapeDtypeStruct((order, order), F32),
            jax.ShapeDtypeStruct((probes, order), F32),
        ),
        in_specs=[whole] * 6 + [scalar] * 2,
        out_specs=(whole,) * 3,
        compiler_params=pltpu.CompilerParams(vmem_limit_bytes=32 * 1024 * 1024),
    )(*firsts, *seconds, snapshots, volumes, live_rows, core)


def sum_chunks(first, second):
    count = lax.axis_size("cells") * lax.axis_size("sub")

    def swap(value, bit):
        return lax.ppermute(value, ("cells", "sub"), [(i, i ^ bit if i % 2 or bit == 1 else i) for i in range(count)])

    def after(value, other):
        return lax.optimization_barrier((value, other))[0]

    bits = [1 << k for k in range(1, count.bit_length() - 1)]
    split = len(bits) // 2
    orders = [], []
    for low, high in zip(bits[:split], bits[split : 2 * split]):
        orders[0].extend((low, high))
        orders[1].extend((high, low))
    for order in orders:
        order.extend(bits[2 * split :])
    if len(bits) > 1:
        orders[1][orders[1].index(bits[-1])] = bits[-1] ^ bits[-2]
    got_first, got_second = swap(first, 1), swap(second, 1)
    for bit_first, bit_second in zip(*orders):
        first = first + after(got_first, second)
        got_first = swap(first, bit_first)
        second = second + after(got_second, first)
        got_second = swap(second, bit_second)
    first = first + after(got_first, second)
    other_first = swap(first, 1)
    second = second + after(got_second, first)
    return (first, other_first), (second, swap(second, 1))


def per_device(snapshots, volumes, live_rows, probes):
    count = lax.axis_size("cells") * lax.axis_size("sub")
    core = (lax.axis_index("sub") % 2).astype(jnp.int32).reshape(1)
    first, second = local_sums(snapshots.shape[0] * count, snapshots, volumes, live_rows, probes)
    firsts, seconds = sum_chunks(first, second)
    return finish(firsts, seconds, snapshots, volumes, live_rows, core, probes.shape[0])


def solution(mesh):
    placed = (
        P(("cells", "sub"), None),
        P(("cells", "sub")),
        P(("cells", "sub")),
        P(None, ("cells", "sub")),
    )
    return jax.shard_map(
        per_device,
        mesh=mesh,
        in_specs=placed,
        out_specs=(P(("cells", "sub"), None), P(), P()),
        check_vma=False,
    )
```

```python
import functools
import jax
import jax.numpy as jnp
from jax import lax
from jax.experimental import pallas as pl
from jax.experimental.pallas import tpu as pltpu
from jax.sharding import PartitionSpec as P

HIGHEST = lax.Precision.HIGHEST
LANES = 128
BLOCK = 8
AHEAD = 2
F32 = jnp.float32


def lanes_of(tile, column):
    return jnp.broadcast_to(tile[:, column : column + 1], tile.shape)


def row_of(tile, index):
    return jnp.broadcast_to(tile[index : index + 1, :], tile.shape)


def product(left, right, dims):
    return lax.dot_general(left, right, (dims, ((), ())), precision=HIGHEST, preferred_element_type=F32)


def eliminate(matrix):
    width = matrix.shape[1]
    count = width // BLOCK
    shape = (BLOCK, width)
    tiles = [matrix[k * BLOCK : (k + 1) * BLOCK, :] for k in range(count)]
    sub_ids = lax.broadcasted_iota(jnp.int32, shape, 0)
    lane_ids = lax.broadcasted_iota(jnp.int32, shape, 1)
    spread_ids = lane_ids - sub_ids

    def gather(parts):
        total = parts[0]
        for r in range(1, BLOCK):
            total = jnp.where(sub_ids == r, parts[r], total)
        return total

    upper_rows, lower_rows = [], []
    columns = [lanes_of(tiles[0], c) for c in range(BLOCK)]
    for block in range(count):
        offset = block * BLOCK
        in_block = (lane_ids >= offset) & (lane_ids < offset + BLOCK)
        own = tiles[block]
        entry = {(r, c): row_of(columns[c], r) for c in range(BLOCK) for r in range(c + 1)}
        kept = [row_of(own, r) for r in range(BLOCK)]
        own = jnp.where(in_block, jnp.where(spread_ids == offset, 1.0, 0.0), own)
        rows = [row_of(own, r) for r in range(BLOCK)]
        near = range(block + 1, min(block + 1 + AHEAD, count))
        weights = {k: [lanes_of(tiles[k], offset + c) for c in range(BLOCK)] for k in near}
        if block + 1 < count:
            columns = [lanes_of(tiles[block + 1], offset + BLOCK + c) for c in range(BLOCK)]
        for k in near:
            tiles[k] = jnp.where(in_block, 0.0, tiles[k])
        inverse, scaled = [], {}
        for i in range(BLOCK):
            inv = pl.reciprocal(entry[i, i], approx=True)
            inverse.append(inv)
            if i + 1 < BLOCK:
                square = entry[i, i + 1] * entry[i, i + 1]
                entry[i + 1, i + 1] = entry[i + 1, i + 1] - square * inv
            for r in range(i + 1, BLOCK):
                scaled[r, i] = entry[i, r] * inv
            for r in range(i + 1, BLOCK):
                for c in range(r, BLOCK):
                    if (r, c) != (i + 1, i + 1):
                        entry[r, c] = entry[r, c] - scaled[r, i] * entry[i, c]
            for k in near:
                here = weights[k][i]
                weight = here * inv
                if k == block + 1:
                    for c in range(BLOCK):
                        columns[c] = columns[c] - weight * row_of(here, c)
                for c in range(i + 1, BLOCK):
                    weights[k][c] = weights[k][c] - here * scaled[c, i]
                tiles[k] = tiles[k] - weight * rows[i]
            for r in range(i + 1, BLOCK):
                rows[r] = rows[r] - scaled[r, i] * rows[i]
                kept[r] = kept[r] - scaled[r, i] * kept[i]
        root = gather([lax.rsqrt(entry[i, i]) for i in range(BLOCK)])
        merged = gather(rows) * root
        diagonal = gather(kept) * root
        lower_rows.append(jnp.where(spread_ids <= offset, merged, 0.0))
        upper_rows.append(jnp.where(spread_ids >= offset, jnp.where(in_block, diagonal, merged), 0.0))
        if block + 1 + AHEAD < count:
            solved = [None] * BLOCK
            for r in reversed(range(BLOCK)):
                solved[r] = rows[r] * inverse[r]
                for c in range(r + 1, BLOCK):
                    solved[r] = solved[r] - scaled[c, r] * solved[c]
            for k in range(block + 1 + AHEAD, count):
                terms = [lanes_of(tiles[k], offset + c) * solved[c] for c in range(BLOCK)]
                while len(terms) > 1:
                    terms = [terms[t] + terms[t + 1] for t in range(0, len(terms), 2)]
                tiles[k] = jnp.where(in_block, 0.0, tiles[k]) - terms[0]
    return jnp.concatenate(upper_rows, axis=0), jnp.concatenate(lower_rows, axis=0)


def packed_rows(order, probes):
    return -(-(order // 2 + probes + 1) // (2 * BLOCK)) * 2 * BLOCK


def live_volumes(volumes_ref, live_ref, begin):
    ids = lax.broadcasted_iota(jnp.int32, (1, LANES), 1) + begin
    part = volumes_ref[pl.ds(begin, LANES)].reshape(1, LANES)
    return jnp.where(ids < live_ref[0], part, 0.0)


def sums_kernel(total_rows, snapshots_hbm, volumes_hbm, live_ref, probes_hbm, part_ref, keep_ref, send_ref, snapshots_ref, volumes_ref, probes_ref, packed, sems):
    copies = [
        pltpu.make_async_copy(source, target, sems.at[i])
        for i, (source, target) in enumerate(
            ((volumes_hbm, volumes_ref), (snapshots_hbm, snapshots_ref), (probes_hbm, probes_ref))
        )
    ]
    for copy in copies:
        copy.start()
    row_count, order = snapshots_ref.shape
    probes = probes_ref.shape[0]
    half = order // 2
    copies[0].wait()
    volume = jnp.concatenate([live_volumes(volumes_ref, live_ref, b) for b in range(0, row_count, LANES)], axis=1)
    copies[1].wait()
    snapshots = snapshots_ref[...]
    scaled = snapshots.T * (volume * (1.0 / total_rows))
    gram = product(scaled, snapshots, ((1,), (0,)))
    row_ids = lax.broadcasted_iota(jnp.int32, (half, half), 0)
    column_ids = lax.broadcasted_iota(jnp.int32, (half, half), 1)
    packed[:half, :half] = jnp.where(row_ids <= column_ids, gram[:half, :half], gram[half:, half:])
    packed[:half, half:] = gram[:half, half:]
    rest = packed.shape[0] - half - probes
    diagonal = jnp.sum(jnp.where(row_ids == column_ids, gram[half:, half:], 0.0), axis=0, keepdims=True)
    packed[half + probes :, :] = jnp.concatenate([jnp.broadcast_to(diagonal, (rest, half))] * 2, axis=1)
    copies[2].wait()
    probe_scaled = probes_ref[...] * (volume * (1.0 / total_rows**0.5))
    packed[half : half + probes, :] = product(probe_scaled, snapshots, ((1,), (0,)))
    middle = packed.shape[0] // 2
    low = part_ref[0] == 0

    @pl.when(low)
    def _():
        keep_ref[...] = packed[:middle, :]
        send_ref[...] = packed[middle:, :]

    @pl.when(jnp.logical_not(low))
    def _():
        keep_ref[...] = packed[middle:, :]
        send_ref[...] = packed[:middle, :]


def local_sums(total_rows, snapshots, volumes, live_rows, probes, part):
    order = snapshots.shape[1]
    size = packed_rows(order, probes.shape[0])
    hbm = pl.BlockSpec(memory_space=pltpu.HBM)
    whole = pl.BlockSpec(memory_space=pltpu.VMEM)
    scalar = pl.BlockSpec(memory_space=pltpu.SMEM)
    return pl.pallas_call(
        functools.partial(sums_kernel, total_rows),
        out_shape=(jax.ShapeDtypeStruct((size // 2, order), F32),) * 2,
        in_specs=[hbm, hbm, scalar, hbm, scalar],
        out_specs=(whole, whole),
        scratch_shapes=[
            pltpu.VMEM(snapshots.shape, F32),
            pltpu.VMEM(volumes.shape, F32),
            pltpu.VMEM(probes.shape, F32),
            pltpu.VMEM((size, order), F32),
            pltpu.SemaphoreType.DMA((3,)),
        ],
        compiler_params=pltpu.CompilerParams(vmem_limit_bytes=54950 * 1024),
    )(snapshots, volumes, live_rows, probes, part)


def finish_kernel(mine_ref, other_ref, snapshots_ref, volumes_ref, live_ref, part_ref, basis_ref, factor_ref, coef_ref):
    row_count, order = snapshots_ref.shape
    probes = coef_ref.shape[0]
    half = order // 2
    low = part_ref[0] == 0
    mine, other = mine_ref[...], other_ref[...]
    packed = jnp.concatenate([jnp.where(low, mine, other), jnp.where(low, other, mine)], axis=0)
    row_ids = lax.broadcasted_iota(jnp.int32, (half, half), 0)
    column_ids = lax.broadcasted_iota(jnp.int32, (half, half), 1)
    square = packed[:half, :half]
    turned = square.T
    cross = packed[half : half + probes, :]
    diagonal = packed[half + probes : half + probes + 1, :half]

    upper, inverse = eliminate(jnp.where(row_ids <= column_ids, square, turned))
    factor_ref[:half, :half] = upper
    factor_ref[half:, :half] = jnp.zeros((half, half), F32)
    beside = product(inverse, packed[:half, half:], ((1,), (0,)))
    factor_ref[:half, half:] = beside
    second = jnp.where(row_ids > column_ids, square, turned)
    second = jnp.where(row_ids == column_ids, diagonal, second) - product(beside, beside, ((0,), (0,)))

    def first_columns(block):
        left = product(block[:, :half], inverse, ((1,), (1,)))
        return left, block[:, half:] - product(left, beside, ((1,), (0,)))

    left, cross_rest = first_columns(cross)
    coef_ref[:, :half] = left
    rest = []
    for begin in range(0, row_count, LANES):
        scale = jnp.sqrt(live_volumes(volumes_ref, live_ref, begin))
        scale = jnp.broadcast_to(scale, (LANES, LANES)).T
        weighted = snapshots_ref[begin : begin + LANES, :] * jnp.concatenate([scale] * (order // LANES), axis=1)
        left, right = first_columns(weighted)
        basis_ref[begin : begin + LANES, :half] = left
        rest.append(right)

    upper, inverse_second = eliminate(second)
    factor_ref[half:, half:] = upper
    coef_ref[:, half:] = product(cross_rest, inverse_second, ((1,), (1,)))
    for begin in range(0, row_count, LANES):
        basis_ref[begin : begin + LANES, half:] = product(rest[begin // LANES], inverse_second, ((1,), (1,)))


def finish(mine, other, snapshots, volumes, live_rows, part, probes):
    row_count, order = snapshots.shape
    whole = pl.BlockSpec(memory_space=pltpu.VMEM)
    scalar = pl.BlockSpec(memory_space=pltpu.SMEM)
    return pl.pallas_call(
        finish_kernel,
        out_shape=(
            jax.ShapeDtypeStruct((row_count, order), F32),
            jax.ShapeDtypeStruct((order, order), F32),
            jax.ShapeDtypeStruct((probes, order), F32),
        ),
        in_specs=[whole] * 4 + [scalar] * 2,
        out_specs=(whole,) * 3,
        compiler_params=pltpu.CompilerParams(vmem_limit_bytes=32 * 1024 * 1024),
    )(mine, other, snapshots, volumes, live_rows, part)


def exchange(value, bits):
    count = lax.axis_size("cells") * lax.axis_size("sub")
    pairs = [(i, i ^ 1 ^ bits[bin(i).count("1") % 2]) for i in range(count)]
    return lax.ppermute(value, ("cells", "sub"), pairs)


def reduce_halves(keep, send):
    count = lax.axis_size("cells") * lax.axis_size("sub")
    bits = [1 << k for k in range(1, count.bit_length() - 1)]
    split = len(bits) // 2
    mine = keep + exchange(send, (0, 0))
    for first, second in zip(bits[:split], bits[split : 2 * split]):
        mine = mine + exchange(mine, (first, second))
        mine = mine + exchange(mine, (second, first))
    for bit in bits[2 * split :]:
        mine = mine + exchange(mine, (bit, bit))
    return mine, exchange(mine, (0, 0))


def per_device(snapshots, volumes, live_rows, probes):
    count = lax.axis_size("cells") * lax.axis_size("sub")
    index = lax.axis_index("cells") * lax.axis_size("sub") + lax.axis_index("sub")
    part = (lax.population_count(index.astype(jnp.int32)) % 2).reshape(1)
    keep, send = local_sums(snapshots.shape[0] * count, snapshots, volumes, live_rows, probes, part)
    mine, other = reduce_halves(keep, send)
    return finish(mine, other, snapshots, volumes, live_rows, part, probes.shape[0])


def solution(mesh):
    placed = (
        P(("cells", "sub"), None),
        P(("cells", "sub")),
        P(("cells", "sub")),
        P(None, ("cells", "sub")),
    )
    return jax.shard_map(
        per_device,
        mesh=mesh,
        in_specs=placed,
        out_specs=(P(("cells", "sub"), None), P(), P()),
        check_vma=False,
    )
```

```python
import functools
import jax
import jax.numpy as jnp
from jax import lax
from jax.experimental import pallas as pl
from jax.experimental.pallas import tpu as pltpu
from jax.sharding import PartitionSpec as P

HIGHEST = lax.Precision.HIGHEST
LANES = 128
BLOCK = 8
AHEAD = 2
F32 = jnp.float32


def lanes_of(tile, column):
    return jnp.broadcast_to(tile[:, column : column + 1], tile.shape)


def row_of(tile, index):
    return jnp.broadcast_to(tile[index : index + 1, :], tile.shape)


def product(left, right, dims):
    return lax.dot_general(left, right, (dims, ((), ())), precision=HIGHEST, preferred_element_type=F32)


def eliminate(matrix):
    width = matrix.shape[1]
    count = width // BLOCK
    shape = (BLOCK, width)
    tiles = [matrix[k * BLOCK : (k + 1) * BLOCK, :] for k in range(count)]
    sub_ids = lax.broadcasted_iota(jnp.int32, shape, 0)
    lane_ids = lax.broadcasted_iota(jnp.int32, shape, 1)
    spread_ids = lane_ids - sub_ids

    def gather(parts):
        total = parts[0]
        for r in range(1, BLOCK):
            total = jnp.where(sub_ids == r, parts[r], total)
        return total

    lower_rows = []
    following = [lanes_of(tiles[0], c) for c in range(BLOCK)]
    for block in range(count):
        offset = block * BLOCK
        in_block = (lane_ids >= offset) & (lane_ids < offset + BLOCK)
        columns = following
        own = jnp.where(in_block, jnp.where(spread_ids == offset, 1.0, 0.0), tiles[block])
        rows = [row_of(own, r) for r in range(BLOCK)]
        near = range(block + 1, min(block + 1 + AHEAD, count))
        weights = {k: [lanes_of(tiles[k], offset + c) for c in range(BLOCK)] for k in near}
        if block + 1 < count:
            following = [lanes_of(tiles[block + 1], offset + BLOCK + c) for c in range(BLOCK)]
        for k in near:
            tiles[k] = jnp.where(in_block, 0.0, tiles[k])
        pivots, inverse, scaled = [row_of(columns[0], 0)], [], {}
        for i in range(BLOCK):
            inv = pl.reciprocal(pivots[i], approx=True)
            inverse.append(inv)
            beside = {c: row_of(columns[c], i) for c in range(i + 1, BLOCK)}
            if i + 1 < BLOCK:
                square = beside[i + 1] * beside[i + 1]
                pivots.append(row_of(columns[i + 1], i + 1) - square * inv)
            for c in range(i + 1, BLOCK):
                scaled[c, i] = beside[c] * inv
                columns[c] = columns[c] - columns[i] * scaled[c, i]
            for k in near:
                here = weights[k][i]
                weight = here * inv
                if k == block + 1:
                    for c in range(BLOCK):
                        following[c] = following[c] - weight * row_of(here, c)
                for c in range(i + 1, BLOCK):
                    weights[k][c] = weights[k][c] - here * scaled[c, i]
                tiles[k] = tiles[k] - weight * rows[i]
            for r in range(i + 1, BLOCK):
                rows[r] = rows[r] - scaled[r, i] * rows[i]
        merged = gather(rows) * lax.rsqrt(gather(pivots))
        lower_rows.append(jnp.where(spread_ids <= offset, merged, 0.0))
        if block + 1 + AHEAD < count:
            solved = [None] * BLOCK
            for r in reversed(range(BLOCK)):
                solved[r] = rows[r] * inverse[r]
                for c in range(r + 1, BLOCK):
                    solved[r] = solved[r] - scaled[c, r] * solved[c]
            for k in range(block + 1 + AHEAD, count):
                terms = [lanes_of(tiles[k], offset + c) * solved[c] for c in range(BLOCK)]
                while len(terms) > 1:
                    terms = [terms[t] + terms[t + 1] for t in range(0, len(terms), 2)]
                tiles[k] = jnp.where(in_block, 0.0, tiles[k]) - terms[0]
    return jnp.concatenate(lower_rows, axis=0)


def packed_rows(order, probes):
    return -(-(order // 2 + probes + 1) // (2 * BLOCK)) * 2 * BLOCK


def live_volumes(volumes_ref, live_ref, begin):
    ids = lax.broadcasted_iota(jnp.int32, (1, LANES), 1) + begin
    part = volumes_ref[pl.ds(begin, LANES)].reshape(1, LANES)
    return jnp.where(ids < live_ref[0], part, 0.0)


def sums_kernel(total_rows, snapshots_hbm, volumes_hbm, live_ref, probes_hbm, part_ref, keep_ref, send_ref, snapshots_ref, volumes_ref, probes_ref, packed, sems):
    copies = [
        pltpu.make_async_copy(source, target, sems.at[i])
        for i, (source, target) in enumerate(
            ((volumes_hbm, volumes_ref), (snapshots_hbm, snapshots_ref), (probes_hbm, probes_ref))
        )
    ]
    for copy in copies:
        copy.start()
    row_count, order = snapshots_ref.shape
    probes = probes_ref.shape[0]
    half = order // 2
    copies[0].wait()
    volume = jnp.concatenate([live_volumes(volumes_ref, live_ref, b) for b in range(0, row_count, LANES)], axis=1)
    copies[1].wait()
    snapshots = snapshots_ref[...]
    scaled = snapshots.T * (volume * (1.0 / total_rows))
    gram = product(scaled, snapshots, ((1,), (0,)))
    row_ids = lax.broadcasted_iota(jnp.int32, (half, half), 0)
    column_ids = lax.broadcasted_iota(jnp.int32, (half, half), 1)
    packed[:half, :half] = jnp.where(row_ids <= column_ids, gram[:half, :half], gram[half:, half:])
    packed[:half, half:] = gram[:half, half:]
    rest = packed.shape[0] - half - probes
    diagonal = jnp.sum(jnp.where(row_ids == column_ids, gram[half:, half:], 0.0), axis=0, keepdims=True)
    packed[half + probes :, :] = jnp.concatenate([jnp.broadcast_to(diagonal, (rest, half))] * 2, axis=1)
    copies[2].wait()
    probe_scaled = probes_ref[...] * (volume * (1.0 / total_rows**0.5))
    packed[half : half + probes, :] = product(probe_scaled, snapshots, ((1,), (0,)))
    middle = packed.shape[0] // 2
    low = part_ref[0] == 0

    @pl.when(low)
    def _():
        keep_ref[...] = packed[:middle, :]
        send_ref[...] = packed[middle:, :]

    @pl.when(jnp.logical_not(low))
    def _():
        keep_ref[...] = packed[middle:, :]
        send_ref[...] = packed[:middle, :]


def local_sums(total_rows, snapshots, volumes, live_rows, probes, part):
    order = snapshots.shape[1]
    size = packed_rows(order, probes.shape[0])
    hbm = pl.BlockSpec(memory_space=pltpu.HBM)
    whole = pl.BlockSpec(memory_space=pltpu.VMEM)
    scalar = pl.BlockSpec(memory_space=pltpu.SMEM)
    return pl.pallas_call(
        functools.partial(sums_kernel, total_rows),
        out_shape=(jax.ShapeDtypeStruct((size // 2, order), F32),) * 2,
        in_specs=[hbm, hbm, scalar, hbm, scalar],
        out_specs=(whole, whole),
        scratch_shapes=[
            pltpu.VMEM(snapshots.shape, F32),
            pltpu.VMEM(volumes.shape, F32),
            pltpu.VMEM(probes.shape, F32),
            pltpu.VMEM((size, order), F32),
            pltpu.SemaphoreType.DMA((3,)),
        ],
        compiler_params=pltpu.CompilerParams(vmem_limit_bytes=24 * 1024 * 1024),
    )(*(pltpu.with_memory_space_constraint(x, pltpu.HBM) for x in (snapshots, volumes)), live_rows, pltpu.with_memory_space_constraint(probes, pltpu.HBM), part)


def weigh_kernel(snapshots_ref, volumes_ref, live_ref, weighted_ref):
    row_count, order = snapshots_ref.shape
    for begin in range(0, row_count, LANES):
        scale = jnp.sqrt(live_volumes(volumes_ref, live_ref, begin))
        scale = jnp.broadcast_to(scale, (LANES, LANES)).T
        rows = pl.ds(begin, LANES)
        weighted_ref[rows, :] = snapshots_ref[rows, :] * jnp.concatenate([scale] * (order // LANES), axis=1)


def weigh(snapshots, volumes, live_rows):
    whole = pl.BlockSpec(memory_space=pltpu.VMEM)
    scalar = pl.BlockSpec(memory_space=pltpu.SMEM)
    return pl.pallas_call(
        weigh_kernel,
        out_shape=jax.ShapeDtypeStruct(snapshots.shape, F32),
        in_specs=[whole, whole, scalar],
        out_specs=whole,
        compiler_params=pltpu.CompilerParams(vmem_limit_bytes=24 * 1024 * 1024),
        cost_estimate=pl.CostEstimate(flops=snapshots.size, bytes_accessed=8 * snapshots.size, transcendentals=0),
    )(snapshots, volumes, live_rows)


def finish_kernel(mine_ref, other_ref, weighted_ref, part_ref, basis_ref, factor_ref, coef_ref):
    order = weighted_ref.shape[1]
    probes = coef_ref.shape[0]
    half = order // 2
    low = part_ref[0] == 0
    mine, other = mine_ref[...], other_ref[...]
    packed = jnp.concatenate([jnp.where(low, mine, other), jnp.where(low, other, mine)], axis=0)
    row_ids = lax.broadcasted_iota(jnp.int32, (half, half), 0)
    column_ids = lax.broadcasted_iota(jnp.int32, (half, half), 1)
    in_upper = row_ids <= column_ids
    square = packed[:half, :half]
    turned = square.T
    cross = packed[half : half + probes, :]
    diagonal = packed[half + probes : half + probes + 1, :half]

    first = jnp.where(in_upper, square, turned)
    inverse = eliminate(first)
    beside = product(inverse, packed[:half, half:], ((1,), (0,)))
    second = jnp.where(row_ids > column_ids, square, turned)
    second = jnp.where(row_ids == column_ids, diagonal, second) - product(beside, beside, ((0,), (0,)))
    factor_ref[:half, :half] = jnp.where(in_upper, product(inverse, first, ((1,), (0,))), 0.0)
    factor_ref[:half, half:] = beside
    factor_ref[half:, :half] = jnp.zeros((half, half), F32)

    left = product(cross[:, :half], inverse, ((1,), (1,)))
    coef_ref[:, :half] = left
    cross_rest = cross[:, half:] - product(left, beside, ((1,), (0,)))
    left = product(weighted_ref[:, :half], inverse, ((1,), (1,)))
    basis_ref[:, :half] = left
    rest = weighted_ref[:, half:] - product(left, beside, ((1,), (0,)))

    inverse_second = eliminate(second)
    coef_ref[:, half:] = product(cross_rest, inverse_second, ((1,), (1,)))
    basis_ref[:, half:] = product(rest, inverse_second, ((1,), (1,)))
    factor_ref[half:, half:] = jnp.where(in_upper, product(inverse_second, second, ((1,), (0,))), 0.0)


def finish(mine, other, weighted, part, probes):
    row_count, order = weighted.shape
    whole = pl.BlockSpec(memory_space=pltpu.VMEM)
    return pl.pallas_call(
        finish_kernel,
        out_shape=(
            jax.ShapeDtypeStruct((row_count, order), F32),
            jax.ShapeDtypeStruct((order, order), F32),
            jax.ShapeDtypeStruct((probes, order), F32),
        ),
        in_specs=[whole] * 3 + [pl.BlockSpec(memory_space=pltpu.SMEM)],
        out_specs=(whole,) * 3,
        compiler_params=pltpu.CompilerParams(vmem_limit_bytes=32 * 1024 * 1024),
    )(mine, other, weighted, part)


def exchange(value, bits):
    count = lax.axis_size("cells") * lax.axis_size("sub")
    pairs = [(i, i ^ 1 ^ bits[bin(i).count("1") % 2]) for i in range(count)]
    return lax.ppermute(value, ("cells", "sub"), pairs)


def reduce_halves(keep, send):
    count = lax.axis_size("cells") * lax.axis_size("sub")
    bits = [1 << k for k in range(1, count.bit_length() - 1)]
    split = len(bits) // 2
    mine = keep + exchange(send, (0, 0))
    for first, second in zip(bits[:split], bits[split : 2 * split]):
        mine = mine + exchange(mine, (first, second))
        mine = mine + exchange(mine, (second, first))
    for bit in bits[2 * split :]:
        mine = mine + exchange(mine, (bit, bit))
    return mine, exchange(mine, (0, 0))


def per_device(snapshots, volumes, live_rows, probes):
    count = lax.axis_size("cells") * lax.axis_size("sub")
    index = lax.axis_index("cells") * lax.axis_size("sub") + lax.axis_index("sub")
    part = (lax.population_count(index.astype(jnp.int32)) % 2).reshape(1)
    keep, send = local_sums(snapshots.shape[0] * count, snapshots, volumes, live_rows, probes, part)
    mine, other = reduce_halves(keep, send)
    return finish(mine, other, weigh(snapshots, volumes, live_rows), part, probes.shape[0])


def solution(mesh):
    placed = (
        P(("cells", "sub"), None),
        P(("cells", "sub")),
        P(("cells", "sub")),
        P(None, ("cells", "sub")),
    )
    return jax.shard_map(
        per_device,
        mesh=mesh,
        in_specs=placed,
        out_specs=(P(("cells", "sub"), None), P(), P()),
        check_vma=False,
    )
```

```python
import functools
import jax
import jax.numpy as jnp
from jax import lax
from jax.experimental import pallas as pl
from jax.experimental.pallas import tpu as pltpu
from jax.sharding import PartitionSpec as P

HIGHEST = lax.Precision.HIGHEST
LANES = 128
BLOCK = 8
AHEAD = 2
F32 = jnp.float32


def lanes_of(tile, column):
    return jnp.broadcast_to(tile[:, column : column + 1], tile.shape)


def row_of(tile, index):
    return jnp.broadcast_to(tile[index : index + 1, :], tile.shape)


def product(left, right, dims):
    return lax.dot_general(left, right, (dims, ((), ())), precision=HIGHEST, preferred_element_type=F32)


def eliminate(matrix):
    width = matrix.shape[1]
    count = width // BLOCK
    shape = (BLOCK, width)
    tiles = [matrix[k * BLOCK : (k + 1) * BLOCK, :] for k in range(count)]
    sub_ids = lax.broadcasted_iota(jnp.int32, shape, 0)
    lane_ids = lax.broadcasted_iota(jnp.int32, shape, 1)
    spread_ids = lane_ids - sub_ids

    def gather(parts):
        total = parts[0]
        for r in range(1, BLOCK):
            total = jnp.where(sub_ids == r, parts[r], total)
        return total

    lower_rows = []
    following = [lanes_of(tiles[0], c) for c in range(BLOCK)]
    for block in range(count):
        offset = block * BLOCK
        in_block = (lane_ids >= offset) & (lane_ids < offset + BLOCK)
        columns = following
        own = jnp.where(in_block, jnp.where(spread_ids == offset, 1.0, 0.0), tiles[block])
        rows = [row_of(own, r) for r in range(BLOCK)]
        near = range(block + 1, min(block + 1 + AHEAD, count))
        weights = {k: [lanes_of(tiles[k], offset + c) for c in range(BLOCK)] for k in near}
        if block + 1 < count:
            following = [lanes_of(tiles[block + 1], offset + BLOCK + c) for c in range(BLOCK)]
        for k in near:
            tiles[k] = jnp.where(in_block, 0.0, tiles[k])
        pivots, inverse, scaled = [row_of(columns[0], 0)], [], {}
        for i in range(BLOCK):
            inv = pl.reciprocal(pivots[i], approx=True)
            inverse.append(inv)
            beside = {c: row_of(columns[c], i) for c in range(i + 1, BLOCK)}
            if i + 1 < BLOCK:
                square = beside[i + 1] * beside[i + 1]
                pivots.append(row_of(columns[i + 1], i + 1) - square * inv)
            for c in range(i + 1, BLOCK):
                scaled[c, i] = beside[c] * inv
                columns[c] = columns[c] - columns[i] * scaled[c, i]
            for k in near:
                here = weights[k][i]
                weight = here * inv
                if k == block + 1:
                    for c in range(BLOCK):
                        following[c] = following[c] - weight * row_of(here, c)
                for c in range(i + 1, BLOCK):
                    weights[k][c] = weights[k][c] - here * scaled[c, i]
                tiles[k] = tiles[k] - weight * rows[i]
            for r in range(i + 1, BLOCK):
                rows[r] = rows[r] - scaled[r, i] * rows[i]
        merged = gather(rows) * lax.rsqrt(gather(pivots))
        lower_rows.append(jnp.where(spread_ids <= offset, merged, 0.0))
        if block + 1 + AHEAD < count:
            solved = [None] * BLOCK
            for r in reversed(range(BLOCK)):
                solved[r] = rows[r] * inverse[r]
                for c in range(r + 1, BLOCK):
                    solved[r] = solved[r] - scaled[c, r] * solved[c]
            for k in range(block + 1 + AHEAD, count):
                terms = [lanes_of(tiles[k], offset + c) * solved[c] for c in range(BLOCK)]
                while len(terms) > 1:
                    terms = [terms[t] + terms[t + 1] for t in range(0, len(terms), 2)]
                tiles[k] = jnp.where(in_block, 0.0, tiles[k]) - terms[0]
    return jnp.concatenate(lower_rows, axis=0)


def packed_rows(order, probes):
    return -(-(order // 2 + probes + 1) // (2 * BLOCK)) * 2 * BLOCK


def live_volumes(volumes_ref, live_ref, begin):
    ids = lax.broadcasted_iota(jnp.int32, (1, LANES), 1) + begin
    part = volumes_ref[pl.ds(begin, LANES)].reshape(1, LANES)
    return jnp.where(ids < live_ref[0], part, 0.0)


def sums_kernel(total_rows, snapshots_hbm, volumes_hbm, live_ref, probes_hbm, part_ref, keep_ref, send_ref, snapshots_ref, volumes_ref, probes_ref, packed, sems):
    copies = [
        pltpu.make_async_copy(source, target, sems.at[i])
        for i, (source, target) in enumerate(
            ((volumes_hbm, volumes_ref), (snapshots_hbm, snapshots_ref), (probes_hbm, probes_ref))
        )
    ]
    for copy in copies:
        copy.start()
    row_count, order = snapshots_ref.shape
    probes = probes_ref.shape[0]
    half = order // 2
    copies[0].wait()
    volume = jnp.concatenate([live_volumes(volumes_ref, live_ref, b) for b in range(0, row_count, LANES)], axis=1)
    copies[1].wait()
    snapshots = snapshots_ref[...]
    scaled = snapshots.T * (volume * (1.0 / total_rows))
    gram = product(scaled, snapshots, ((1,), (0,)))
    row_ids = lax.broadcasted_iota(jnp.int32, (half, half), 0)
    column_ids = lax.broadcasted_iota(jnp.int32, (half, half), 1)
    packed[:half, :half] = jnp.where(row_ids <= column_ids, gram[:half, :half], gram[half:, half:])
    packed[:half, half:] = gram[:half, half:]
    rest = packed.shape[0] - half - probes
    diagonal = jnp.sum(jnp.where(row_ids == column_ids, gram[half:, half:], 0.0), axis=0, keepdims=True)
    packed[half + probes :, :] = jnp.concatenate([jnp.broadcast_to(diagonal, (rest, half))] * 2, axis=1)
    copies[2].wait()
    probe_scaled = probes_ref[...] * (volume * (1.0 / total_rows**0.5))
    packed[half : half + probes, :] = product(probe_scaled, snapshots, ((1,), (0,)))
    middle = packed.shape[0] // 2
    low = part_ref[0] == 0

    @pl.when(low)
    def _():
        keep_ref[...] = packed[:middle, :]
        send_ref[...] = packed[middle:, :]

    @pl.when(jnp.logical_not(low))
    def _():
        keep_ref[...] = packed[middle:, :]
        send_ref[...] = packed[:middle, :]


def local_sums(total_rows, snapshots, volumes, live_rows, probes, part):
    order = snapshots.shape[1]
    size = packed_rows(order, probes.shape[0])
    hbm = pl.BlockSpec(memory_space=pltpu.HBM)
    whole = pl.BlockSpec(memory_space=pltpu.VMEM)
    scalar = pl.BlockSpec(memory_space=pltpu.SMEM)
    return pl.pallas_call(
        functools.partial(sums_kernel, total_rows),
        out_shape=(jax.ShapeDtypeStruct((size // 2, order), F32),) * 2,
        in_specs=[hbm, hbm, scalar, hbm, scalar],
        out_specs=(whole, whole),
        scratch_shapes=[
            pltpu.VMEM(snapshots.shape, F32),
            pltpu.VMEM(volumes.shape, F32),
            pltpu.VMEM(probes.shape, F32),
            pltpu.VMEM((size, order), F32),
            pltpu.SemaphoreType.DMA((3,)),
        ],
        compiler_params=pltpu.CompilerParams(vmem_limit_bytes=24 * 1024 * 1024),
    )(*(pltpu.with_memory_space_constraint(x, pltpu.HBM) for x in (snapshots, volumes)), live_rows, pltpu.with_memory_space_constraint(probes, pltpu.HBM), part)


def weigh_kernel(snapshots_ref, volumes_ref, live_ref, weighted_ref):
    row_count, order = snapshots_ref.shape
    for begin in range(0, row_count, LANES):
        scale = jnp.sqrt(live_volumes(volumes_ref, live_ref, begin))
        scale = jnp.broadcast_to(scale, (LANES, LANES)).T
        rows = pl.ds(begin, LANES)
        weighted_ref[rows, :] = snapshots_ref[rows, :] * jnp.concatenate([scale] * (order // LANES), axis=1)


def weigh(snapshots, volumes, live_rows):
    whole = pl.BlockSpec(memory_space=pltpu.VMEM)
    scalar = pl.BlockSpec(memory_space=pltpu.SMEM)
    return pl.pallas_call(
        weigh_kernel,
        out_shape=jax.ShapeDtypeStruct(snapshots.shape, F32),
        in_specs=[whole, whole, scalar],
        out_specs=whole,
        compiler_params=pltpu.CompilerParams(vmem_limit_bytes=24 * 1024 * 1024),
        cost_estimate=pl.CostEstimate(flops=snapshots.size, bytes_accessed=8 * snapshots.size, transcendentals=0),
    )(snapshots, volumes, live_rows)


def finish_kernel(mine_ref, other_ref, weighted_ref, part_ref, basis_ref, factor_ref, coef_ref):
    order = weighted_ref.shape[1]
    probes = coef_ref.shape[0]
    half = order // 2
    low = part_ref[0] == 0
    mine, other = mine_ref[...], other_ref[...]
    packed = jnp.concatenate([jnp.where(low, mine, other), jnp.where(low, other, mine)], axis=0)
    row_ids = lax.broadcasted_iota(jnp.int32, (half, half), 0)
    column_ids = lax.broadcasted_iota(jnp.int32, (half, half), 1)
    in_upper = row_ids <= column_ids
    square = packed[:half, :half]
    turned = square.T
    cross = packed[half : half + probes, :]
    diagonal = packed[half + probes : half + probes + 1, :half]

    first = jnp.where(in_upper, square, turned)
    inverse = eliminate(first)
    beside = product(inverse, packed[:half, half:], ((1,), (0,)))
    second = jnp.where(row_ids > column_ids, square, turned)
    second = jnp.where(row_ids == column_ids, diagonal, second) - product(beside, beside, ((0,), (0,)))
    factor_ref[:half, :half] = jnp.where(in_upper, product(inverse, first, ((1,), (0,))), 0.0)
    factor_ref[:half, half:] = beside
    factor_ref[half:, :half] = jnp.zeros((half, half), F32)

    left = product(cross[:, :half], inverse, ((1,), (1,)))
    coef_ref[:, :half] = left
    cross_rest = cross[:, half:] - product(left, beside, ((1,), (0,)))
    left = product(weighted_ref[:, :half], inverse, ((1,), (1,)))
    basis_ref[:, :half] = left
    rest = weighted_ref[:, half:] - product(left, beside, ((1,), (0,)))

    inverse_second = eliminate(second)
    coef_ref[:, half:] = product(cross_rest, inverse_second, ((1,), (1,)))
    basis_ref[:, half:] = product(rest, inverse_second, ((1,), (1,)))
    factor_ref[half:, half:] = jnp.where(in_upper, product(inverse_second, second, ((1,), (0,))), 0.0)


def finish(mine, other, weighted, part, probes):
    row_count, order = weighted.shape
    whole = pl.BlockSpec(memory_space=pltpu.VMEM)
    return pl.pallas_call(
        finish_kernel,
        out_shape=(
            jax.ShapeDtypeStruct((row_count, order), F32),
            jax.ShapeDtypeStruct((order, order), F32),
            jax.ShapeDtypeStruct((probes, order), F32),
        ),
        in_specs=[whole] * 3 + [pl.BlockSpec(memory_space=pltpu.SMEM)],
        out_specs=(whole,) * 3,
        compiler_params=pltpu.CompilerParams(vmem_limit_bytes=32 * 1024 * 1024),
    )(mine, other, weighted, part)


def exchange(value, masks):
    count = lax.axis_size("cells") * lax.axis_size("sub")
    pairs = [(i, i ^ masks[bin(i).count("1") % 2]) for i in range(count)]
    return lax.ppermute(value, ("cells", "sub"), pairs)


def reduce_halves(keep, send):
    count = lax.axis_size("cells") * lax.axis_size("sub")
    bits = [1 << k for k in range(1, count.bit_length() - 1)]
    phases = [bits[k : k + 2] for k in range(0, len(bits) - 1, 2)]
    split = len(phases) // 2
    mine = keep + exchange(send, (1, 1))
    for even, odd in zip(phases, phases[split:] + phases[:split]):
        near = exchange(mine, (even[0] ^ 1, odd[0] ^ 1))
        far = exchange(mine, (even[1] ^ 1, odd[1] ^ 1))
        across = exchange(mine, (even[0] ^ even[1], odd[0] ^ odd[1]))
        mine = (mine + near) + (far + across)
    for bit in bits[2 * len(phases) :]:
        mine = mine + exchange(mine, (bit ^ 1, bit ^ 1))
    return mine, exchange(mine, (1, 1))


def per_device(snapshots, volumes, live_rows, probes):
    count = lax.axis_size("cells") * lax.axis_size("sub")
    index = lax.axis_index("cells") * lax.axis_size("sub") + lax.axis_index("sub")
    part = (lax.population_count(index.astype(jnp.int32)) % 2).reshape(1)
    keep, send = local_sums(snapshots.shape[0] * count, snapshots, volumes, live_rows, probes, part)
    mine, other = reduce_halves(keep, send)
    return finish(mine, other, weigh(snapshots, volumes, live_rows), part, probes.shape[0])


def solution(mesh):
    placed = (
        P(("cells", "sub"), None),
        P(("cells", "sub")),
        P(("cells", "sub")),
        P(None, ("cells", "sub")),
    )
    return jax.shard_map(
        per_device,
        mesh=mesh,
        in_specs=placed,
        out_specs=(P(("cells", "sub"), None), P(), P()),
        check_vma=False,
    )
```

```python
import functools
import jax
import jax.numpy as jnp
from jax import lax
from jax.experimental import pallas as pl
from jax.experimental.pallas import tpu as pltpu
from jax.sharding import PartitionSpec as P

HIGHEST = lax.Precision.HIGHEST
LANES = 128
BLOCK = 8
AHEAD = 2
F32 = jnp.float32


def lanes_of(tile, column):
    return jnp.broadcast_to(tile[:, column : column + 1], tile.shape)


def row_of(tile, index):
    return jnp.broadcast_to(tile[index : index + 1, :], tile.shape)


def product(left, right, dims):
    return lax.dot_general(left, right, (dims, ((), ())), precision=HIGHEST, preferred_element_type=F32)


def eliminate(matrix):
    width = matrix.shape[1]
    count = width // BLOCK
    shape = (BLOCK, width)
    tiles = [matrix[k * BLOCK : (k + 1) * BLOCK, :] for k in range(count)]
    sub_ids = lax.broadcasted_iota(jnp.int32, shape, 0)
    lane_ids = lax.broadcasted_iota(jnp.int32, shape, 1)
    spread_ids = lane_ids - sub_ids

    def gather(parts):
        total = parts[0]
        for r in range(1, BLOCK):
            total = jnp.where(sub_ids == r, parts[r], total)
        return total

    lower_rows = []
    following = [lanes_of(tiles[0], c) for c in range(BLOCK)]
    for block in range(count):
        offset = block * BLOCK
        in_block = (lane_ids >= offset) & (lane_ids < offset + BLOCK)
        columns = following
        before = tiles[block]
        own = jnp.where(in_block, jnp.where(spread_ids == offset, 1.0, 0.0), before)
        rows = [row_of(own, r) for r in range(BLOCK)]
        near = range(block + 1, min(block + 1 + AHEAD, count))
        weights = {k: [lanes_of(tiles[k], offset + c) for c in range(BLOCK)] for k in near}
        if block + 1 < count:
            following = [lanes_of(tiles[block + 1], offset + BLOCK + c) for c in range(BLOCK)]
        for k in near:
            tiles[k] = jnp.where(in_block, 0.0, tiles[k])
        pivots, inverse, scaled = [row_of(columns[0], 0)], [], {}
        for i in range(BLOCK):
            inv = pl.reciprocal(pivots[i], approx=True)
            inverse.append(inv)
            beside = {c: row_of(columns[c], i) for c in range(i + 1, BLOCK)}
            if i + 1 < BLOCK:
                square = beside[i + 1] * beside[i + 1]
                pivots.append(row_of(columns[i + 1], i + 1) - square * inv)
            for c in range(i + 1, BLOCK):
                scaled[c, i] = beside[c] * inv
                columns[c] = columns[c] - columns[i] * scaled[c, i]
            for k in near:
                here = weights[k][i]
                weight = here * inv
                if k == block + 1:
                    for c in range(BLOCK):
                        following[c] = following[c] - weight * row_of(here, c)
                for c in range(i + 1, BLOCK):
                    weights[k][c] = weights[k][c] - here * scaled[c, i]
                tiles[k] = tiles[k] - weight * rows[i]
            for r in range(i + 1, BLOCK):
                rows[r] = rows[r] - scaled[r, i] * rows[i]
        merged = gather(rows) * lax.rsqrt(gather(pivots))
        lower_rows.append(jnp.where(spread_ids <= offset, merged, 0.0))
        if block + 1 + AHEAD < count:
            solved = [None] * BLOCK
            for r in reversed(range(BLOCK)):
                solved[r] = rows[r] * inverse[r]
                for c in range(r + 1, BLOCK):
                    solved[r] = solved[r] - scaled[c, r] * solved[c]
            update = product(before, gather(solved), ((0,), (0,)))
            for k in range(block + 1 + AHEAD, count):
                tiles[k] = jnp.where(in_block, 0.0, tiles[k]) - update[k * BLOCK : (k + 1) * BLOCK, :]
    return jnp.concatenate(lower_rows, axis=0)


def packed_rows(order, probes):
    return -(-(order // 2 + probes + 1) // (2 * BLOCK)) * 2 * BLOCK


def live_volumes(volumes_ref, live_ref, begin):
    ids = lax.broadcasted_iota(jnp.int32, (1, LANES), 1) + begin
    part = volumes_ref[pl.ds(begin, LANES)].reshape(1, LANES)
    return jnp.where(ids < live_ref[0], part, 0.0)


def sums_kernel(total_rows, snapshots_hbm, volumes_hbm, live_ref, probes_hbm, part_ref, keep_ref, send_ref, scale_ref, snapshots_ref, volumes_ref, probes_ref, packed, sems):
    copies = [
        pltpu.make_async_copy(source, target, sems.at[i])
        for i, (source, target) in enumerate(
            ((volumes_hbm, volumes_ref), (snapshots_hbm, snapshots_ref), (probes_hbm, probes_ref))
        )
    ]
    for copy in copies:
        copy.start()
    row_count, order = snapshots_ref.shape
    probes = probes_ref.shape[0]
    half = order // 2
    copies[0].wait()
    volume = jnp.concatenate([live_volumes(volumes_ref, live_ref, b) for b in range(0, row_count, LANES)], axis=1)
    scale_ref[...] = jnp.sqrt(volume)
    copies[1].wait()
    snapshots = snapshots_ref[...]
    scaled = snapshots.T * (volume * (1.0 / total_rows))
    gram = product(scaled, snapshots, ((1,), (0,)))
    row_ids = lax.broadcasted_iota(jnp.int32, (half, half), 0)
    column_ids = lax.broadcasted_iota(jnp.int32, (half, half), 1)
    packed[:half, :half] = jnp.where(row_ids <= column_ids, gram[:half, :half], gram[half:, half:])
    packed[:half, half:] = gram[:half, half:]
    rest = packed.shape[0] - half - probes
    diagonal = jnp.sum(jnp.where(row_ids == column_ids, gram[half:, half:], 0.0), axis=0, keepdims=True)
    packed[half + probes :, :] = jnp.concatenate([jnp.broadcast_to(diagonal, (rest, half))] * 2, axis=1)
    copies[2].wait()
    probe_scaled = probes_ref[...] * (volume * (1.0 / total_rows**0.5))
    packed[half : half + probes, :] = product(probe_scaled, snapshots, ((1,), (0,)))
    middle = packed.shape[0] // 2
    low = part_ref[0] == 0

    @pl.when(low)
    def _():
        keep_ref[...] = packed[:middle, :]
        send_ref[...] = packed[middle:, :]

    @pl.when(jnp.logical_not(low))
    def _():
        keep_ref[...] = packed[middle:, :]
        send_ref[...] = packed[:middle, :]


def hold(array):
    return pltpu.with_memory_space_constraint(array, pltpu.HBM)


def local_sums(total_rows, snapshots, volumes, live_rows, probes, part):
    order = snapshots.shape[1]
    size = packed_rows(order, probes.shape[0])
    hbm = pl.BlockSpec(memory_space=pltpu.HBM)
    whole = pl.BlockSpec(memory_space=pltpu.VMEM)
    scalar = pl.BlockSpec(memory_space=pltpu.SMEM)
    return pl.pallas_call(
        functools.partial(sums_kernel, total_rows),
        out_shape=(jax.ShapeDtypeStruct((size // 2, order), F32),) * 2 + (jax.ShapeDtypeStruct((1, volumes.shape[0]), F32),),
        in_specs=[hbm, hbm, scalar, hbm, scalar],
        out_specs=(whole, whole, whole),
        scratch_shapes=[
            pltpu.VMEM(snapshots.shape, F32),
            pltpu.VMEM(volumes.shape, F32),
            pltpu.VMEM(probes.shape, F32),
            pltpu.VMEM((size, order), F32),
            pltpu.SemaphoreType.DMA((3,)),
        ],
        compiler_params=pltpu.CompilerParams(vmem_limit_bytes=24 * 1024 * 1024),
    )(hold(snapshots), hold(volumes), live_rows, hold(probes), part)


def weigh_kernel(snapshots_ref, scale_ref, weighted_ref):
    row_count, order = snapshots_ref.shape
    for begin in range(0, row_count, LANES):
        rows = pl.ds(begin, LANES)
        scale = jnp.broadcast_to(scale_ref[:, rows], (LANES, LANES)).T
        weighted_ref[rows, :] = snapshots_ref[rows, :] * jnp.concatenate([scale] * (order // LANES), axis=1)


def weigh(snapshots, scale):
    whole = pl.BlockSpec(memory_space=pltpu.VMEM)
    return pl.pallas_call(
        weigh_kernel,
        out_shape=jax.ShapeDtypeStruct(snapshots.shape, F32),
        in_specs=[whole, whole],
        out_specs=whole,
        compiler_params=pltpu.CompilerParams(vmem_limit_bytes=24 * 1024 * 1024),
        cost_estimate=pl.CostEstimate(flops=snapshots.size, bytes_accessed=8 * snapshots.size, transcendentals=0),
    )(snapshots, scale)


def finish_kernel(mine_ref, other_ref, weighted_ref, part_ref, basis_ref, factor_ref, coef_ref):
    order = weighted_ref.shape[1]
    probes = coef_ref.shape[0]
    half = order // 2
    low = part_ref[0] == 0
    mine, other = mine_ref[...], other_ref[...]
    packed = jnp.concatenate([jnp.where(low, mine, other), jnp.where(low, other, mine)], axis=0)
    row_ids = lax.broadcasted_iota(jnp.int32, (half, half), 0)
    column_ids = lax.broadcasted_iota(jnp.int32, (half, half), 1)
    in_upper = row_ids <= column_ids
    square = packed[:half, :half]
    turned = square.T
    cross = packed[half : half + probes, :]
    diagonal = packed[half + probes : half + probes + 1, :half]

    first = jnp.where(in_upper, square, turned)
    inverse = eliminate(first)
    beside = product(inverse, packed[:half, half:], ((1,), (0,)))
    second = jnp.where(row_ids > column_ids, square, turned)
    second = jnp.where(row_ids == column_ids, diagonal, second) - product(beside, beside, ((0,), (0,)))
    factor_ref[:half, :half] = jnp.where(in_upper, product(inverse, first, ((1,), (0,))), 0.0)
    factor_ref[:half, half:] = beside
    factor_ref[half:, :half] = jnp.zeros((half, half), F32)

    left = product(cross[:, :half], inverse, ((1,), (1,)))
    coef_ref[:, :half] = left
    cross_rest = cross[:, half:] - product(left, beside, ((1,), (0,)))
    left = product(weighted_ref[:, :half], inverse, ((1,), (1,)))
    basis_ref[:, :half] = left
    rest = weighted_ref[:, half:] - product(left, beside, ((1,), (0,)))

    inverse_second = eliminate(second)
    coef_ref[:, half:] = product(cross_rest, inverse_second, ((1,), (1,)))
    basis_ref[:, half:] = product(rest, inverse_second, ((1,), (1,)))
    factor_ref[half:, half:] = jnp.where(in_upper, product(inverse_second, second, ((1,), (0,))), 0.0)


def finish(mine, other, weighted, part, probes):
    row_count, order = weighted.shape
    whole = pl.BlockSpec(memory_space=pltpu.VMEM)
    return pl.pallas_call(
        finish_kernel,
        out_shape=(
            jax.ShapeDtypeStruct((row_count, order), F32),
            jax.ShapeDtypeStruct((order, order), F32),
            jax.ShapeDtypeStruct((probes, order), F32),
        ),
        in_specs=[whole] * 3 + [pl.BlockSpec(memory_space=pltpu.SMEM)],
        out_specs=(whole,) * 3,
        compiler_params=pltpu.CompilerParams(vmem_limit_bytes=32 * 1024 * 1024),
    )(mine, other, weighted, part)


def exchange(value, masks):
    count = lax.axis_size("cells") * lax.axis_size("sub")
    pairs = [(i, i ^ masks[bin(i).count("1") % 2]) for i in range(count)]
    return lax.ppermute(value, ("cells", "sub"), pairs)


def reduce_halves(keep, send):
    count = lax.axis_size("cells") * lax.axis_size("sub")
    bits = [1 << k for k in range(1, count.bit_length() - 1)]
    phases = [bits[k : k + 2] for k in range(0, len(bits) - 1, 2)]
    split = len(phases) // 2
    mine = keep + exchange(send, (1, 1))
    for even, odd in zip(phases, phases[split:] + phases[:split]):
        near = exchange(mine, (even[0] ^ 1, odd[0] ^ 1))
        far = exchange(mine, (even[1] ^ 1, odd[1] ^ 1))
        across = exchange(mine, (even[0] ^ even[1], odd[0] ^ odd[1]))
        mine = (mine + near) + (far + across)
    for bit in bits[2 * len(phases) :]:
        mine = mine + exchange(mine, (bit ^ 1, bit ^ 1))
    return mine, exchange(mine, (1, 1))


def per_device(snapshots, volumes, live_rows, probes):
    count = lax.axis_size("cells") * lax.axis_size("sub")
    index = lax.axis_index("cells") * lax.axis_size("sub") + lax.axis_index("sub")
    part = (lax.population_count(index.astype(jnp.int32)) % 2).reshape(1)
    keep, send, scale = local_sums(snapshots.shape[0] * count, snapshots, volumes, live_rows, probes, part)
    mine, other = reduce_halves(keep, send)
    return finish(mine, other, weigh(snapshots, scale), part, probes.shape[0])


def solution(mesh):
    placed = (
        P(("cells", "sub"), None),
        P(("cells", "sub")),
        P(("cells", "sub")),
        P(None, ("cells", "sub")),
    )
    return jax.shard_map(
        per_device,
        mesh=mesh,
        in_specs=placed,
        out_specs=(P(("cells", "sub"), None), P(), P()),
        check_vma=False,
    )
```

```python
import functools
import jax
import jax.numpy as jnp
from jax import lax
from jax.experimental import pallas as pl
from jax.experimental.pallas import tpu as pltpu
from jax.sharding import PartitionSpec as P

HIGHEST = lax.Precision.HIGHEST
LANES = 128
BLOCK = 8
AHEAD = 2
F32 = jnp.float32


def lanes_of(tile, column):
    return jnp.broadcast_to(tile[:, column : column + 1], tile.shape)


def row_of(tile, index):
    return jnp.broadcast_to(tile[index : index + 1, :], tile.shape)


def product(left, right, dims):
    return lax.dot_general(left, right, (dims, ((), ())), precision=HIGHEST, preferred_element_type=F32)


def eliminate(matrix, tasks=()):
    width = matrix.shape[1]
    count = width // BLOCK
    shape = (BLOCK, width)
    tiles = [matrix[k * BLOCK : (k + 1) * BLOCK, :] for k in range(count)]
    sub_ids = lax.broadcasted_iota(jnp.int32, shape, 0)
    lane_ids = lax.broadcasted_iota(jnp.int32, shape, 1)
    spread_ids = lane_ids - sub_ids

    def gather(parts):
        total = parts[0]
        for r in range(1, BLOCK):
            total = jnp.where(sub_ids == r, parts[r], total)
        return total

    tasks = iter(tasks)
    lower_rows = []
    following = [lanes_of(tiles[0], c) for c in range(BLOCK)]
    for block in range(count):
        offset = block * BLOCK
        in_block = (lane_ids >= offset) & (lane_ids < offset + BLOCK)
        columns = following
        own = jnp.where(in_block, jnp.where(spread_ids == offset, 1.0, 0.0), tiles[block])
        rows = [row_of(own, r) for r in range(BLOCK)]
        near = range(block + 1, min(block + 1 + AHEAD, count))
        weights = {k: [lanes_of(tiles[k], offset + c) for c in range(BLOCK)] for k in near}
        if block + 1 < count:
            following = [lanes_of(tiles[block + 1], offset + BLOCK + c) for c in range(BLOCK)]
        for k in near:
            tiles[k] = jnp.where(in_block, 0.0, tiles[k])
        pivots, inverse, scaled = [row_of(columns[0], 0)], [], {}
        for i in range(BLOCK):
            inv = pl.reciprocal(pivots[i], approx=True)
            inverse.append(inv)
            beside = {c: row_of(columns[c], i) for c in range(i + 1, BLOCK)}
            if i + 1 < BLOCK:
                square = beside[i + 1] * beside[i + 1]
                pivots.append(row_of(columns[i + 1], i + 1) - square * inv)
            for c in range(i + 1, BLOCK):
                scaled[c, i] = beside[c] * inv
                columns[c] = columns[c] - columns[i] * scaled[c, i]
            for k in near:
                here = weights[k][i]
                weight = here * inv
                if k == block + 1:
                    for c in range(BLOCK):
                        following[c] = following[c] - weight * row_of(here, c)
                for c in range(i + 1, BLOCK):
                    weights[k][c] = weights[k][c] - here * scaled[c, i]
                tiles[k] = tiles[k] - weight * rows[i]
            for r in range(i + 1, BLOCK):
                rows[r] = rows[r] - scaled[r, i] * rows[i]
        merged = gather(rows) * lax.rsqrt(gather(pivots))
        lower_rows.append(jnp.where(spread_ids <= offset, merged, 0.0))
        if block + 1 + AHEAD < count:
            solved = [None] * BLOCK
            for r in reversed(range(BLOCK)):
                solved[r] = rows[r] * inverse[r]
                for c in range(r + 1, BLOCK):
                    solved[r] = solved[r] - scaled[c, r] * solved[c]
            for k in range(block + 1 + AHEAD, count):
                terms = [lanes_of(tiles[k], offset + c) * solved[c] for c in range(BLOCK)]
                while len(terms) > 1:
                    terms = [terms[t] + terms[t + 1] for t in range(0, len(terms), 2)]
                tiles[k] = jnp.where(in_block, 0.0, tiles[k]) - terms[0]
        for task in tasks:
            task()
            break
    for task in tasks:
        task()
    return jnp.concatenate(lower_rows, axis=0)


def packed_rows(order, probes):
    return -(-(order // 2 + probes + 1) // (2 * BLOCK)) * 2 * BLOCK


def live_volumes(volumes_ref, live_ref, begin):
    ids = lax.broadcasted_iota(jnp.int32, (1, LANES), 1) + begin
    part = volumes_ref[pl.ds(begin, LANES)].reshape(1, LANES)
    return jnp.where(ids < live_ref[0], part, 0.0)


def sums_kernel(total_rows, snapshots_hbm, volumes_hbm, live_ref, probes_hbm, part_ref, keep_ref, send_ref, scale_ref, snapshots_ref, volumes_ref, probes_ref, packed, sems):
    copies = [
        pltpu.make_async_copy(source, target, sems.at[i])
        for i, (source, target) in enumerate(
            ((volumes_hbm, volumes_ref), (snapshots_hbm, snapshots_ref), (probes_hbm, probes_ref))
        )
    ]
    for copy in copies:
        copy.start()
    row_count, order = snapshots_ref.shape
    probes = probes_ref.shape[0]
    half = order // 2
    copies[0].wait()
    volume = jnp.concatenate([live_volumes(volumes_ref, live_ref, b) for b in range(0, row_count, LANES)], axis=1)
    scale_ref[...] = jnp.sqrt(volume)
    copies[1].wait()
    snapshots = snapshots_ref[...]
    scaled = snapshots.T * (volume * (1.0 / total_rows))
    gram = product(scaled, snapshots, ((1,), (0,)))
    row_ids = lax.broadcasted_iota(jnp.int32, (half, half), 0)
    column_ids = lax.broadcasted_iota(jnp.int32, (half, half), 1)
    packed[:half, :half] = jnp.where(row_ids <= column_ids, gram[:half, :half], gram[half:, half:])
    packed[:half, half:] = gram[:half, half:]
    rest = packed.shape[0] - half - probes
    diagonal = jnp.sum(jnp.where(row_ids == column_ids, gram[half:, half:], 0.0), axis=0, keepdims=True)
    packed[half + probes :, :] = jnp.concatenate([jnp.broadcast_to(diagonal, (rest, half))] * 2, axis=1)
    copies[2].wait()
    probe_scaled = probes_ref[...] * (volume * (1.0 / total_rows**0.5))
    packed[half : half + probes, :] = product(probe_scaled, snapshots, ((1,), (0,)))
    middle = packed.shape[0] // 2
    low = part_ref[0] == 0

    @pl.when(low)
    def _():
        keep_ref[...] = packed[:middle, :]
        send_ref[...] = packed[middle:, :]

    @pl.when(jnp.logical_not(low))
    def _():
        keep_ref[...] = packed[middle:, :]
        send_ref[...] = packed[:middle, :]


def hold(array):
    return pltpu.with_memory_space_constraint(array, pltpu.HBM)


def local_sums(total_rows, snapshots, volumes, live_rows, probes, part):
    order = snapshots.shape[1]
    size = packed_rows(order, probes.shape[0])
    hbm = pl.BlockSpec(memory_space=pltpu.HBM)
    whole = pl.BlockSpec(memory_space=pltpu.VMEM)
    scalar = pl.BlockSpec(memory_space=pltpu.SMEM)
    return pl.pallas_call(
        functools.partial(sums_kernel, total_rows),
        out_shape=(jax.ShapeDtypeStruct((size // 2, order), F32),) * 2 + (jax.ShapeDtypeStruct((1, volumes.shape[0]), F32),),
        in_specs=[hbm, hbm, scalar, hbm, scalar],
        out_specs=(whole, whole, whole),
        scratch_shapes=[
            pltpu.VMEM(snapshots.shape, F32),
            pltpu.VMEM(volumes.shape, F32),
            pltpu.VMEM(probes.shape, F32),
            pltpu.VMEM((size, order), F32),
            pltpu.SemaphoreType.DMA((3,)),
        ],
        compiler_params=pltpu.CompilerParams(vmem_limit_bytes=24 * 1024 * 1024),
    )(hold(snapshots), hold(volumes), live_rows, hold(probes), part)


def weigh_kernel(snapshots_ref, scale_ref, weighted_ref):
    row_count, order = snapshots_ref.shape
    for begin in range(0, row_count, LANES):
        rows = pl.ds(begin, LANES)
        scale = jnp.broadcast_to(scale_ref[:, rows], (LANES, LANES)).T
        weighted_ref[rows, :] = snapshots_ref[rows, :] * jnp.concatenate([scale] * (order // LANES), axis=1)


def weigh(snapshots, scale):
    whole = pl.BlockSpec(memory_space=pltpu.VMEM)
    return pl.pallas_call(
        weigh_kernel,
        out_shape=jax.ShapeDtypeStruct(snapshots.shape, F32),
        in_specs=[whole, whole],
        out_specs=whole,
        compiler_params=pltpu.CompilerParams(vmem_limit_bytes=24 * 1024 * 1024),
        cost_estimate=pl.CostEstimate(flops=snapshots.size, bytes_accessed=8 * snapshots.size, transcendentals=0),
    )(snapshots, scale)


def finish_kernel(mine_ref, other_ref, weighted_ref, part_ref, basis_hbm, factor_hbm, coef_hbm, basis_ref, factor_ref, coef_ref, rest_ref, sems):
    row_count, order = weighted_ref.shape
    probes = coef_ref.shape[0]
    half = order // 2
    chunks = [pl.ds(begin, LANES) for begin in range(0, row_count, LANES)]
    left, right = pl.ds(0, half), pl.ds(half, half)
    copies = []

    def write(source, target, place):
        copy = pltpu.make_async_copy(source.at[place], target.at[place], sems.at[len(copies)])
        copy.start()
        copies.append(copy)

    low = part_ref[0] == 0
    mine, other = mine_ref[...], other_ref[...]
    packed = jnp.concatenate([jnp.where(low, mine, other), jnp.where(low, other, mine)], axis=0)
    row_ids = lax.broadcasted_iota(jnp.int32, (half, half), 0)
    column_ids = lax.broadcasted_iota(jnp.int32, (half, half), 1)
    in_upper = row_ids <= column_ids
    square = packed[:half, :half]
    turned = square.T
    cross = packed[half : half + probes, :]
    diagonal = packed[half + probes : half + probes + 1, :half]

    first = jnp.where(in_upper, square, turned)
    inverse = eliminate(first)
    beside = product(inverse, packed[:half, half:], ((1,), (0,)))
    second = jnp.where(row_ids > column_ids, square, turned)
    second = jnp.where(row_ids == column_ids, diagonal, second) - product(beside, beside, ((0,), (0,)))

    def basis_left(rows):
        def task():
            basis_ref[rows, left] = product(weighted_ref[rows, left], inverse, ((1,), (1,)))
            write(basis_ref, basis_hbm, (rows, left))

        return task

    def basis_rest(rows):
        def task():
            rest_ref[rows, :] = weighted_ref[rows, right] - product(basis_ref[rows, left], beside, ((1,), (0,)))

        return task

    def coef_left():
        coef_ref[:, left] = product(cross[:, :half], inverse, ((1,), (1,)))

    def coef_rest():
        coef_ref[:, right] = cross[:, half:] - product(coef_ref[:, left], beside, ((1,), (0,)))

    def factor_top():
        top = pl.ds(0, half)
        factor_ref[top, left] = jnp.where(in_upper, product(inverse, first, ((1,), (0,))), 0.0)
        factor_ref[top, right] = beside
        write(factor_ref, factor_hbm, (top, pl.ds(0, order)))

    tasks = [task(rows) for task in (basis_left, basis_rest) for rows in chunks]
    inverse_second = eliminate(second, tasks + [coef_left, coef_rest, factor_top])
    for rows in chunks:
        basis_ref[rows, right] = product(rest_ref[rows, :], inverse_second, ((1,), (1,)))
        write(basis_ref, basis_hbm, (rows, right))
    bottom = pl.ds(half, half)
    factor_ref[bottom, left] = jnp.zeros((half, half), F32)
    factor_ref[bottom, right] = jnp.where(in_upper, product(inverse_second, second, ((1,), (0,))), 0.0)
    write(factor_ref, factor_hbm, (bottom, pl.ds(0, order)))
    coef_ref[:, right] = product(coef_ref[:, right], inverse_second, ((1,), (1,)))
    write(coef_ref, coef_hbm, (pl.ds(0, probes), pl.ds(0, order)))
    for copy in copies:
        copy.wait()


def finish(mine, other, weighted, part, probes):
    row_count, order = weighted.shape
    whole = pl.BlockSpec(memory_space=pltpu.VMEM)
    shapes = (row_count, order), (order, order), (probes, order)
    return pl.pallas_call(
        finish_kernel,
        out_shape=tuple(jax.ShapeDtypeStruct(shape, F32) for shape in shapes),
        in_specs=[whole] * 3 + [pl.BlockSpec(memory_space=pltpu.SMEM)],
        out_specs=(pl.BlockSpec(memory_space=pltpu.HBM),) * 3,
        scratch_shapes=[
            *(pltpu.VMEM(shape, F32) for shape in shapes),
            pltpu.VMEM((row_count, order // 2), F32),
            pltpu.SemaphoreType.DMA((2 * (row_count // LANES) + 3,)),
        ],
        compiler_params=pltpu.CompilerParams(vmem_limit_bytes=32 * 1024 * 1024),
    )(mine, other, weighted, part)


def exchange(value, masks):
    count = lax.axis_size("cells") * lax.axis_size("sub")
    pairs = [(i, i ^ masks[bin(i).count("1") % 2]) for i in range(count)]
    return lax.ppermute(value, ("cells", "sub"), pairs)


def reduce_halves(keep, send):
    count = lax.axis_size("cells") * lax.axis_size("sub")
    bits = [1 << k for k in range(1, count.bit_length() - 1)]
    phases = [bits[k : k + 2] for k in range(0, len(bits) - 1, 2)]
    split = len(phases) // 2
    mine = keep + exchange(send, (1, 1))
    for even, odd in zip(phases, phases[split:] + phases[:split]):
        near = exchange(mine, (even[0] ^ 1, odd[0] ^ 1))
        far = exchange(mine, (even[1] ^ 1, odd[1] ^ 1))
        across = exchange(mine, (even[0] ^ even[1], odd[0] ^ odd[1]))
        mine = (mine + near) + (far + across)
    for bit in bits[2 * len(phases) :]:
        mine = mine + exchange(mine, (bit ^ 1, bit ^ 1))
    return mine, exchange(mine, (1, 1))


def per_device(snapshots, volumes, live_rows, probes):
    count = lax.axis_size("cells") * lax.axis_size("sub")
    index = lax.axis_index("cells") * lax.axis_size("sub") + lax.axis_index("sub")
    part = (lax.population_count(index.astype(jnp.int32)) % 2).reshape(1)
    keep, send, scale = local_sums(snapshots.shape[0] * count, snapshots, volumes, live_rows, probes, part)
    mine, other = reduce_halves(keep, send)
    return finish(mine, other, weigh(snapshots, scale), part, probes.shape[0])


def solution(mesh):
    placed = (
        P(("cells", "sub"), None),
        P(("cells", "sub")),
        P(("cells", "sub")),
        P(None, ("cells", "sub")),
    )
    return jax.shard_map(
        per_device,
        mesh=mesh,
        in_specs=placed,
        out_specs=(P(("cells", "sub"), None), P(), P()),
        check_vma=False,
    )
```

```python
import functools
import jax
import jax.numpy as jnp
from jax import lax
from jax.experimental import pallas as pl
from jax.experimental.pallas import tpu as pltpu
from jax.sharding import PartitionSpec as P

HIGHEST = lax.Precision.HIGHEST
LANES = 128
BLOCK = 8
AHEAD = 2
F32 = jnp.float32


def lanes_of(tile, column):
    return jnp.broadcast_to(tile[:, column : column + 1], tile.shape)


def row_of(tile, index):
    return jnp.broadcast_to(tile[index : index + 1, :], tile.shape)


def product(left, right, dims):
    return lax.dot_general(left, right, (dims, ((), ())), precision=HIGHEST, preferred_element_type=F32)


def eliminate(matrix):
    width = matrix.shape[1]
    count = width // BLOCK
    shape = (BLOCK, width)
    tiles = [matrix[k * BLOCK : (k + 1) * BLOCK, :] for k in range(count)]
    sub_ids = lax.broadcasted_iota(jnp.int32, shape, 0)
    lane_ids = lax.broadcasted_iota(jnp.int32, shape, 1)
    spread_ids = lane_ids - sub_ids

    def gather(parts):
        total = parts[0]
        for r in range(1, BLOCK):
            total = jnp.where(sub_ids == r, parts[r], total)
        return total

    lower_rows = []
    following = [lanes_of(tiles[0], c) for c in range(BLOCK)]
    carried = [lanes_of(tiles[1], c) for c in range(BLOCK)]
    for block in range(count):
        offset = block * BLOCK
        in_block = (lane_ids >= offset) & (lane_ids < offset + BLOCK)
        columns = following
        own = jnp.where(in_block, jnp.where(spread_ids == offset, 1.0, 0.0), tiles[block])
        rows = [row_of(own, r) for r in range(BLOCK)]
        near = range(block + 1, min(block + 1 + AHEAD, count))
        weights = {k: [lanes_of(tiles[k], offset + c) for c in range(BLOCK)] for k in near if k > block + 1}
        weights[block + 1] = carried
        bases = {k: [lanes_of(tiles[k], offset + BLOCK + c) for c in range(BLOCK)] for k in near if k <= block + 2}
        changes = {k: [None] * BLOCK for k in bases}
        for k in near:
            tiles[k] = jnp.where(in_block, 0.0, tiles[k])
        pivots, inverse, scaled = [row_of(columns[0], 0)], [], {}
        for i in range(BLOCK):
            inv = pl.reciprocal(pivots[i], approx=True)
            inverse.append(inv)
            beside = {c: row_of(columns[c], i) for c in range(i + 1, BLOCK)}
            if i + 1 < BLOCK:
                square = beside[i + 1] * beside[i + 1]
                pivots.append(row_of(columns[i + 1], i + 1) - square * inv)
            for c in range(i + 1, BLOCK):
                scaled[c, i] = beside[c] * inv
                columns[c] = columns[c] - columns[i] * scaled[c, i]
            for k in near:
                here = weights[k][i]
                weight = here * inv
                if k == block + 1:
                    splats = [row_of(here, c) for c in range(BLOCK)]
                if k in changes:
                    for c in range(BLOCK):
                        change = weight * splats[c]
                        changes[k][c] = change if i == 0 else changes[k][c] + change
                for c in range(i + 1, BLOCK):
                    weights[k][c] = weights[k][c] - here * scaled[c, i]
                tiles[k] = tiles[k] - weight * rows[i]
            for r in range(i + 1, BLOCK):
                rows[r] = rows[r] - scaled[r, i] * rows[i]
        updated = {k: [base - change for base, change in zip(bases[k], changes[k])] for k in bases}
        following, carried = updated.get(block + 1), updated.get(block + 2)
        merged = gather(rows) * lax.rsqrt(gather(pivots))
        lower_rows.append(jnp.where(spread_ids <= offset, merged, 0.0))
        if block + 1 + AHEAD < count:
            solved = [None] * BLOCK
            for r in reversed(range(BLOCK)):
                solved[r] = rows[r] * inverse[r]
                for c in range(r + 1, BLOCK):
                    solved[r] = solved[r] - scaled[c, r] * solved[c]
            for k in range(block + 1 + AHEAD, count):
                terms = [lanes_of(tiles[k], offset + c) * solved[c] for c in range(BLOCK)]
                while len(terms) > 1:
                    terms = [terms[t] + terms[t + 1] for t in range(0, len(terms), 2)]
                tiles[k] = jnp.where(in_block, 0.0, tiles[k]) - terms[0]
    return jnp.concatenate(lower_rows, axis=0)


def packed_rows(order, probes):
    return -(-(order // 2 + probes + 1) // (2 * BLOCK)) * 2 * BLOCK


def live_volumes(volumes_ref, live_ref, begin):
    ids = lax.broadcasted_iota(jnp.int32, (1, LANES), 1) + begin
    part = volumes_ref[pl.ds(begin, LANES)].reshape(1, LANES)
    return jnp.where(ids < live_ref[0], part, 0.0)


def sums_kernel(total_rows, snapshots_hbm, volumes_hbm, live_ref, probes_hbm, part_ref, keep_ref, send_ref, scale_ref, snapshots_ref, volumes_ref, probes_ref, packed, sems):
    copies = [
        pltpu.make_async_copy(source, target, sems.at[i])
        for i, (source, target) in enumerate(
            ((volumes_hbm, volumes_ref), (snapshots_hbm, snapshots_ref), (probes_hbm, probes_ref))
        )
    ]
    for copy in copies:
        copy.start()
    row_count, order = snapshots_ref.shape
    probes = probes_ref.shape[0]
    half = order // 2
    copies[0].wait()
    volume = jnp.concatenate([live_volumes(volumes_ref, live_ref, b) for b in range(0, row_count, LANES)], axis=1)
    scale_ref[...] = jnp.sqrt(volume)
    copies[1].wait()
    snapshots = snapshots_ref[...]
    scaled = snapshots.T * (volume * (1.0 / total_rows))
    gram = product(scaled, snapshots, ((1,), (0,)))
    row_ids = lax.broadcasted_iota(jnp.int32, (half, half), 0)
    column_ids = lax.broadcasted_iota(jnp.int32, (half, half), 1)
    packed[:half, :half] = jnp.where(row_ids <= column_ids, gram[:half, :half], gram[half:, half:])
    packed[:half, half:] = gram[:half, half:]
    rest = packed.shape[0] - half - probes
    diagonal = jnp.sum(jnp.where(row_ids == column_ids, gram[half:, half:], 0.0), axis=0, keepdims=True)
    packed[half + probes :, :] = jnp.concatenate([jnp.broadcast_to(diagonal, (rest, half))] * 2, axis=1)
    copies[2].wait()
    probe_scaled = probes_ref[...] * (volume * (1.0 / total_rows**0.5))
    packed[half : half + probes, :] = product(probe_scaled, snapshots, ((1,), (0,)))
    middle = packed.shape[0] // 2
    low = part_ref[0] == 0

    @pl.when(low)
    def _():
        keep_ref[...] = packed[:middle, :]
        send_ref[...] = packed[middle:, :]

    @pl.when(jnp.logical_not(low))
    def _():
        keep_ref[...] = packed[middle:, :]
        send_ref[...] = packed[:middle, :]


def hold(array):
    return pltpu.with_memory_space_constraint(array, pltpu.HBM)


def local_sums(total_rows, snapshots, volumes, live_rows, probes, part):
    order = snapshots.shape[1]
    size = packed_rows(order, probes.shape[0])
    hbm = pl.BlockSpec(memory_space=pltpu.HBM)
    whole = pl.BlockSpec(memory_space=pltpu.VMEM)
    scalar = pl.BlockSpec(memory_space=pltpu.SMEM)
    return pl.pallas_call(
        functools.partial(sums_kernel, total_rows),
        out_shape=(jax.ShapeDtypeStruct((size // 2, order), F32),) * 2 + (jax.ShapeDtypeStruct((1, volumes.shape[0]), F32),),
        in_specs=[hbm, hbm, scalar, hbm, scalar],
        out_specs=(whole, whole, whole),
        scratch_shapes=[
            pltpu.VMEM(snapshots.shape, F32),
            pltpu.VMEM(volumes.shape, F32),
            pltpu.VMEM(probes.shape, F32),
            pltpu.VMEM((size, order), F32),
            pltpu.SemaphoreType.DMA((3,)),
        ],
        compiler_params=pltpu.CompilerParams(vmem_limit_bytes=24 * 1024 * 1024),
    )(hold(snapshots), hold(volumes), live_rows, hold(probes), part)


def weigh_kernel(snapshots_ref, scale_ref, weighted_ref):
    row_count, order = snapshots_ref.shape
    for begin in range(0, row_count, LANES):
        rows = pl.ds(begin, LANES)
        scale = jnp.broadcast_to(scale_ref[:, rows], (LANES, LANES)).T
        weighted_ref[rows, :] = snapshots_ref[rows, :] * jnp.concatenate([scale] * (order // LANES), axis=1)


def weigh(snapshots, scale):
    whole = pl.BlockSpec(memory_space=pltpu.VMEM)
    return pl.pallas_call(
        weigh_kernel,
        out_shape=jax.ShapeDtypeStruct(snapshots.shape, F32),
        in_specs=[whole, whole],
        out_specs=whole,
        compiler_params=pltpu.CompilerParams(vmem_limit_bytes=24 * 1024 * 1024),
        cost_estimate=pl.CostEstimate(flops=snapshots.size, bytes_accessed=8 * snapshots.size, transcendentals=0),
    )(snapshots, scale)


def finish_kernel(mine_ref, other_ref, weighted_ref, part_ref, basis_ref, factor_ref, coef_ref):
    order = weighted_ref.shape[1]
    probes = coef_ref.shape[0]
    half = order // 2
    low = part_ref[0] == 0
    mine, other = mine_ref[...], other_ref[...]
    packed = jnp.concatenate([jnp.where(low, mine, other), jnp.where(low, other, mine)], axis=0)
    row_ids = lax.broadcasted_iota(jnp.int32, (half, half), 0)
    column_ids = lax.broadcasted_iota(jnp.int32, (half, half), 1)
    in_upper = row_ids <= column_ids
    square = packed[:half, :half]
    turned = square.T
    cross = packed[half : half + probes, :]
    diagonal = packed[half + probes : half + probes + 1, :half]

    first = jnp.where(in_upper, square, turned)
    inverse = eliminate(first)
    beside = product(inverse, packed[:half, half:], ((1,), (0,)))
    second = jnp.where(row_ids > column_ids, square, turned)
    second = jnp.where(row_ids == column_ids, diagonal, second) - product(beside, beside, ((0,), (0,)))
    factor_ref[:half, :half] = jnp.where(in_upper, product(inverse, first, ((1,), (0,))), 0.0)
    factor_ref[:half, half:] = beside
    factor_ref[half:, :half] = jnp.zeros((half, half), F32)

    left = product(cross[:, :half], inverse, ((1,), (1,)))
    coef_ref[:, :half] = left
    cross_rest = cross[:, half:] - product(left, beside, ((1,), (0,)))
    left = product(weighted_ref[:, :half], inverse, ((1,), (1,)))
    basis_ref[:, :half] = left
    rest = weighted_ref[:, half:] - product(left, beside, ((1,), (0,)))

    inverse_second = eliminate(second)
    coef_ref[:, half:] = product(cross_rest, inverse_second, ((1,), (1,)))
    basis_ref[:, half:] = product(rest, inverse_second, ((1,), (1,)))
    factor_ref[half:, half:] = jnp.where(in_upper, product(inverse_second, second, ((1,), (0,))), 0.0)


def finish(mine, other, weighted, part, probes):
    row_count, order = weighted.shape
    whole = pl.BlockSpec(memory_space=pltpu.VMEM)
    return pl.pallas_call(
        finish_kernel,
        out_shape=(
            jax.ShapeDtypeStruct((row_count, order), F32),
            jax.ShapeDtypeStruct((order, order), F32),
            jax.ShapeDtypeStruct((probes, order), F32),
        ),
        in_specs=[whole] * 3 + [pl.BlockSpec(memory_space=pltpu.SMEM)],
        out_specs=(whole,) * 3,
        compiler_params=pltpu.CompilerParams(vmem_limit_bytes=32 * 1024 * 1024),
    )(mine, other, weighted, part)


def exchange(value, masks):
    count = lax.axis_size("cells") * lax.axis_size("sub")
    pairs = [(i, i ^ masks[bin(i).count("1") % 2]) for i in range(count)]
    return lax.ppermute(value, ("cells", "sub"), pairs)


def reduce_halves(keep, send):
    count = lax.axis_size("cells") * lax.axis_size("sub")
    bits = [1 << k for k in range(1, count.bit_length() - 1)]
    phases = [bits[k : k + 2] for k in range(0, len(bits) - 1, 2)]
    split = len(phases) // 2
    mine = keep + exchange(send, (1, 1))
    for even, odd in zip(phases, phases[split:] + phases[:split]):
        near = exchange(mine, (even[0] ^ 1, odd[0] ^ 1))
        far = exchange(mine, (even[1] ^ 1, odd[1] ^ 1))
        across = exchange(mine, (even[0] ^ even[1], odd[0] ^ odd[1]))
        mine = (mine + near) + (far + across)
    for bit in bits[2 * len(phases) :]:
        mine = mine + exchange(mine, (bit ^ 1, bit ^ 1))
    return mine, exchange(mine, (1, 1))


def per_device(snapshots, volumes, live_rows, probes):
    count = lax.axis_size("cells") * lax.axis_size("sub")
    index = lax.axis_index("cells") * lax.axis_size("sub") + lax.axis_index("sub")
    part = (lax.population_count(index.astype(jnp.int32)) % 2).reshape(1)
    keep, send, scale = local_sums(snapshots.shape[0] * count, snapshots, volumes, live_rows, probes, part)
    mine, other = reduce_halves(keep, send)
    return finish(mine, other, weigh(snapshots, scale), part, probes.shape[0])


def solution(mesh):
    placed = (
        P(("cells", "sub"), None),
        P(("cells", "sub")),
        P(("cells", "sub")),
        P(None, ("cells", "sub")),
    )
    return jax.shard_map(
        per_device,
        mesh=mesh,
        in_specs=placed,
        out_specs=(P(("cells", "sub"), None), P(), P()),
        check_vma=False,
    )
```

```python
import functools
import jax
import jax.numpy as jnp
from jax import lax
from jax.experimental import pallas as pl
from jax.experimental.pallas import tpu as pltpu
from jax.sharding import PartitionSpec as P

HIGHEST = lax.Precision.HIGHEST
LANES = 128
BLOCK = 8
AHEAD = 2
F32 = jnp.float32


def lanes_of(tile, column):
    return jnp.broadcast_to(tile[:, column : column + 1], tile.shape)


def row_of(tile, index):
    return jnp.broadcast_to(tile[index : index + 1, :], tile.shape)


def product(left, right, dims):
    return lax.dot_general(left, right, (dims, ((), ())), precision=HIGHEST, preferred_element_type=F32)


def eliminate(matrix):
    width = matrix.shape[1]
    count = width // BLOCK
    shape = (BLOCK, width)
    tiles = [matrix[k * BLOCK : (k + 1) * BLOCK, :] for k in range(count)]
    sub_ids = lax.broadcasted_iota(jnp.int32, shape, 0)
    lane_ids = lax.broadcasted_iota(jnp.int32, shape, 1)
    spread_ids = lane_ids - sub_ids

    def gather(parts):
        total = parts[0]
        for r in range(1, BLOCK):
            total = jnp.where(sub_ids == r, parts[r], total)
        return total

    lower_rows = []
    following = [lanes_of(tiles[0], c) for c in range(BLOCK)]
    carried = [lanes_of(tiles[1], c) for c in range(BLOCK)]
    for block in range(count):
        offset = block * BLOCK
        in_block = (lane_ids >= offset) & (lane_ids < offset + BLOCK)
        columns = following
        own = jnp.where(in_block, jnp.where(spread_ids == offset, 1.0, 0.0), tiles[block])
        rows = [row_of(own, r) for r in range(BLOCK)]
        near = range(block + 1, min(block + 1 + AHEAD, count))
        weights = {k: [lanes_of(tiles[k], offset + c) for c in range(BLOCK)] for k in near if k > block + 1}
        weights[block + 1] = carried
        bases = {k: [lanes_of(tiles[k], offset + BLOCK + c) for c in range(BLOCK)] for k in near if k <= block + 2}
        changes = {k: [None] * BLOCK for k in bases}
        for k in near:
            tiles[k] = jnp.where(in_block, 0.0, tiles[k])
        pivots, inverse, scaled = [row_of(columns[0], 0)], [], {}
        for i in range(BLOCK):
            inv = pl.reciprocal(pivots[i], approx=True)
            inverse.append(inv)
            beside = {c: row_of(columns[c], i) for c in range(i + 1, BLOCK)}
            if i + 1 < BLOCK:
                square = beside[i + 1] * beside[i + 1]
                pivots.append(row_of(columns[i + 1], i + 1) - square * inv)
            for c in range(i + 1, BLOCK):
                scaled[c, i] = beside[c] * inv
                columns[c] = columns[c] - columns[i] * scaled[c, i]
            for k in near:
                here = weights[k][i]
                weight = here * inv
                if k == block + 1:
                    splats = [row_of(here, c) for c in range(BLOCK)]
                if k in changes:
                    for c in range(BLOCK):
                        change = weight * splats[c]
                        changes[k][c] = change if i == 0 else changes[k][c] + change
                for c in range(i + 1, BLOCK):
                    weights[k][c] = weights[k][c] - here * scaled[c, i]
                tiles[k] = tiles[k] - weight * rows[i]
            for r in range(i + 1, BLOCK):
                rows[r] = rows[r] - scaled[r, i] * rows[i]
        updated = {k: [base - change for base, change in zip(bases[k], changes[k])] for k in bases}
        following, carried = updated.get(block + 1), updated.get(block + 2)
        merged = gather(rows) * lax.rsqrt(gather(pivots))
        lower_rows.append(jnp.where(spread_ids <= offset, merged, 0.0))
        if block + 1 + AHEAD < count:
            solved = [None] * BLOCK
            for r in reversed(range(BLOCK)):
                solved[r] = rows[r] * inverse[r]
                for c in range(r + 1, BLOCK):
                    solved[r] = solved[r] - scaled[c, r] * solved[c]
            for k in range(block + 1 + AHEAD, count):
                terms = [lanes_of(tiles[k], offset + c) * solved[c] for c in range(BLOCK)]
                while len(terms) > 1:
                    terms = [terms[t] + terms[t + 1] for t in range(0, len(terms), 2)]
                tiles[k] = jnp.where(in_block, 0.0, tiles[k]) - terms[0]
    return jnp.concatenate(lower_rows, axis=0)


def packed_rows(order, probes):
    return -(-(order // 2 + probes + 1) // (2 * BLOCK)) * 2 * BLOCK


def own_part():
    bits = lax.axis_index("cells") ^ lax.axis_index("sub")
    for shift in (16, 8, 4, 2, 1):
        bits = bits ^ (bits >> shift)
    return bits & 1


def live_volumes(volumes_ref, live_ref, begin):
    ids = lax.broadcasted_iota(jnp.int32, (1, LANES), 1) + begin
    part = volumes_ref[pl.ds(begin, LANES)].reshape(1, LANES)
    return jnp.where(ids < live_ref[0], part, 0.0)


def sums_kernel(total_rows, snapshots_hbm, volumes_hbm, live_ref, probes_hbm, keep_ref, send_ref, scale_ref, snapshots_ref, volumes_ref, probes_ref, packed, sems):
    copies = [
        pltpu.make_async_copy(source, target, sems.at[i])
        for i, (source, target) in enumerate(
            ((volumes_hbm, volumes_ref), (snapshots_hbm, snapshots_ref), (probes_hbm, probes_ref))
        )
    ]
    for copy in copies:
        copy.start()
    row_count, order = snapshots_ref.shape
    probes = probes_ref.shape[0]
    half = order // 2
    copies[0].wait()
    volume = jnp.concatenate([live_volumes(volumes_ref, live_ref, b) for b in range(0, row_count, LANES)], axis=1)
    scale_ref[...] = jnp.sqrt(volume)
    copies[1].wait()
    snapshots = snapshots_ref[...]
    scaled = snapshots.T * (volume * (1.0 / total_rows))
    gram = product(scaled, snapshots, ((1,), (0,)))
    row_ids = lax.broadcasted_iota(jnp.int32, (half, half), 0)
    column_ids = lax.broadcasted_iota(jnp.int32, (half, half), 1)
    packed[:half, :half] = jnp.where(row_ids <= column_ids, gram[:half, :half], gram[half:, half:])
    packed[:half, half:] = gram[:half, half:]
    rest = packed.shape[0] - half - probes
    diagonal = jnp.sum(jnp.where(row_ids == column_ids, gram[half:, half:], 0.0), axis=0, keepdims=True)
    packed[half + probes :, :] = jnp.concatenate([jnp.broadcast_to(diagonal, (rest, half))] * 2, axis=1)
    copies[2].wait()
    probe_scaled = probes_ref[...] * (volume * (1.0 / total_rows**0.5))
    packed[half : half + probes, :] = product(probe_scaled, snapshots, ((1,), (0,)))
    middle = packed.shape[0] // 2
    low = own_part() == 0

    @pl.when(low)
    def _():
        keep_ref[...] = packed[:middle, :]
        send_ref[...] = packed[middle:, :]

    @pl.when(jnp.logical_not(low))
    def _():
        keep_ref[...] = packed[middle:, :]
        send_ref[...] = packed[:middle, :]


def hold(array):
    return pltpu.with_memory_space_constraint(array, pltpu.HBM)


def local_sums(total_rows, snapshots, volumes, live_rows, probes):
    order = snapshots.shape[1]
    size = packed_rows(order, probes.shape[0])
    hbm = pl.BlockSpec(memory_space=pltpu.HBM)
    whole = pl.BlockSpec(memory_space=pltpu.VMEM)
    return pl.pallas_call(
        functools.partial(sums_kernel, total_rows),
        out_shape=(jax.ShapeDtypeStruct((size // 2, order), F32),) * 2 + (jax.ShapeDtypeStruct((1, volumes.shape[0]), F32),),
        in_specs=[hbm, hbm, pl.BlockSpec(memory_space=pltpu.SMEM), hbm],
        out_specs=(whole, whole, whole),
        scratch_shapes=[
            pltpu.VMEM(snapshots.shape, F32),
            pltpu.VMEM(volumes.shape, F32),
            pltpu.VMEM(probes.shape, F32),
            pltpu.VMEM((size, order), F32),
            pltpu.SemaphoreType.DMA((3,)),
        ],
        compiler_params=pltpu.CompilerParams(vmem_limit_bytes=24 * 1024 * 1024),
    )(hold(snapshots), hold(volumes), live_rows, hold(probes))


def weigh_kernel(snapshots_ref, scale_ref, weighted_ref):
    row_count, order = snapshots_ref.shape
    for begin in range(0, row_count, LANES):
        rows = pl.ds(begin, LANES)
        scale = jnp.broadcast_to(scale_ref[:, rows], (LANES, LANES)).T
        weighted_ref[rows, :] = snapshots_ref[rows, :] * jnp.concatenate([scale] * (order // LANES), axis=1)


def weigh(snapshots, scale):
    whole = pl.BlockSpec(memory_space=pltpu.VMEM)
    return pl.pallas_call(
        weigh_kernel,
        out_shape=jax.ShapeDtypeStruct(snapshots.shape, F32),
        in_specs=[whole, whole],
        out_specs=whole,
        compiler_params=pltpu.CompilerParams(vmem_limit_bytes=24 * 1024 * 1024),
        cost_estimate=pl.CostEstimate(flops=snapshots.size, bytes_accessed=8 * snapshots.size, transcendentals=0),
    )(snapshots, scale)


def finish_kernel(mine_ref, other_ref, weighted_ref, basis_ref, factor_ref, coef_ref):
    order = weighted_ref.shape[1]
    probes = coef_ref.shape[0]
    half = order // 2
    low = own_part() == 0
    mine, other = mine_ref[...], other_ref[...]
    packed = jnp.concatenate([jnp.where(low, mine, other), jnp.where(low, other, mine)], axis=0)
    row_ids = lax.broadcasted_iota(jnp.int32, (half, half), 0)
    column_ids = lax.broadcasted_iota(jnp.int32, (half, half), 1)
    in_upper = row_ids <= column_ids
    square = packed[:half, :half]
    turned = square.T
    cross = packed[half : half + probes, :]
    diagonal = packed[half + probes : half + probes + 1, :half]

    first = jnp.where(in_upper, square, turned)
    inverse = eliminate(first)
    beside = product(inverse, packed[:half, half:], ((1,), (0,)))
    second = jnp.where(row_ids > column_ids, square, turned)
    second = jnp.where(row_ids == column_ids, diagonal, second) - product(beside, beside, ((0,), (0,)))
    factor_ref[:half, :half] = jnp.where(in_upper, product(inverse, first, ((1,), (0,))), 0.0)
    factor_ref[:half, half:] = beside
    factor_ref[half:, :half] = jnp.zeros((half, half), F32)

    left = product(cross[:, :half], inverse, ((1,), (1,)))
    coef_ref[:, :half] = left
    cross_rest = cross[:, half:] - product(left, beside, ((1,), (0,)))
    left = product(weighted_ref[:, :half], inverse, ((1,), (1,)))
    basis_ref[:, :half] = left
    rest = weighted_ref[:, half:] - product(left, beside, ((1,), (0,)))

    inverse_second = eliminate(second)
    coef_ref[:, half:] = product(cross_rest, inverse_second, ((1,), (1,)))
    basis_ref[:, half:] = product(rest, inverse_second, ((1,), (1,)))
    factor_ref[half:, half:] = jnp.where(in_upper, product(inverse_second, second, ((1,), (0,))), 0.0)


def finish(mine, other, weighted, probes):
    row_count, order = weighted.shape
    whole = pl.BlockSpec(memory_space=pltpu.VMEM)
    return pl.pallas_call(
        finish_kernel,
        out_shape=(
            jax.ShapeDtypeStruct((row_count, order), F32),
            jax.ShapeDtypeStruct((order, order), F32),
            jax.ShapeDtypeStruct((probes, order), F32),
        ),
        in_specs=[whole] * 3,
        out_specs=(whole,) * 3,
        compiler_params=pltpu.CompilerParams(vmem_limit_bytes=32 * 1024 * 1024),
    )(mine, other, weighted)


def exchange(value, masks):
    count = lax.axis_size("cells") * lax.axis_size("sub")
    pairs = [(i, i ^ masks[bin(i).count("1") % 2]) for i in range(count)]
    return lax.ppermute(value, ("cells", "sub"), pairs)


def reduce_halves(keep, send):
    count = lax.axis_size("cells") * lax.axis_size("sub")
    bits = [1 << k for k in range(1, count.bit_length() - 1)]
    phases = [bits[k : k + 2] for k in range(0, len(bits) - 1, 2)]
    split = len(phases) // 2
    mine = keep + exchange(send, (1, 1))
    for even, odd in zip(phases, phases[split:] + phases[:split]):
        near = exchange(mine, (even[0] ^ 1, odd[0] ^ 1))
        far = exchange(mine, (even[1] ^ 1, odd[1] ^ 1))
        across = exchange(mine, (even[0] ^ even[1], odd[0] ^ odd[1]))
        mine = (mine + near) + (far + across)
    for bit in bits[2 * len(phases) :]:
        mine = mine + exchange(mine, (bit ^ 1, bit ^ 1))
    return mine, exchange(mine, (1, 1))


def per_device(snapshots, volumes, live_rows, probes):
    count = lax.axis_size("cells") * lax.axis_size("sub")
    keep, send, scale = local_sums(snapshots.shape[0] * count, snapshots, volumes, live_rows, probes)
    mine, other = reduce_halves(keep, send)
    return finish(mine, other, weigh(snapshots, scale), probes.shape[0])


def solution(mesh):
    placed = (
        P(("cells", "sub"), None),
        P(("cells", "sub")),
        P(("cells", "sub")),
        P(None, ("cells", "sub")),
    )
    return jax.shard_map(
        per_device,
        mesh=mesh,
        in_specs=placed,
        out_specs=(P(("cells", "sub"), None), P(), P()),
        check_vma=False,
    )
```

```python
import functools
import jax
import jax.numpy as jnp
from jax import lax
from jax.experimental import pallas as pl
from jax.experimental.pallas import tpu as pltpu
from jax.sharding import PartitionSpec as P

HIGHEST = lax.Precision.HIGHEST
LANES = 128
BLOCK = 8
AHEAD = 2
F32 = jnp.float32


def lanes_of(tile, column):
    return jnp.broadcast_to(tile[:, column : column + 1], tile.shape)


def row_of(tile, index):
    return jnp.broadcast_to(tile[index : index + 1, :], tile.shape)


def product(left, right, dims):
    return lax.dot_general(left, right, (dims, ((), ())), precision=HIGHEST, preferred_element_type=F32)


def eliminate(matrix):
    width = matrix.shape[1]
    count = width // BLOCK
    shape = (BLOCK, width)
    tiles = [matrix[k * BLOCK : (k + 1) * BLOCK, :] for k in range(count)]
    sub_ids = lax.broadcasted_iota(jnp.int32, shape, 0)
    lane_ids = lax.broadcasted_iota(jnp.int32, shape, 1)
    spread_ids = lane_ids - sub_ids

    def gather(parts):
        total = parts[0]
        for r in range(1, BLOCK):
            total = jnp.where(sub_ids == r, parts[r], total)
        return total

    lower_rows = []
    following = [lanes_of(tiles[0], c) for c in range(BLOCK)]
    carried = [lanes_of(tiles[1], c) for c in range(BLOCK)]
    for block in range(count):
        offset = block * BLOCK
        in_block = (lane_ids >= offset) & (lane_ids < offset + BLOCK)
        columns = following
        own = jnp.where(in_block, jnp.where(spread_ids == offset, 1.0, 0.0), tiles[block])
        rows = [row_of(own, r) for r in range(BLOCK)]
        near = range(block + 1, min(block + 1 + AHEAD, count))
        weights = {k: [lanes_of(tiles[k], offset + c) for c in range(BLOCK)] for k in near if k > block + 1}
        weights[block + 1] = carried
        bases = {k: [lanes_of(tiles[k], offset + BLOCK + c) for c in range(BLOCK)] for k in near if k <= block + 2}
        changes = {k: [None] * BLOCK for k in bases}
        for k in near:
            tiles[k] = jnp.where(in_block, 0.0, tiles[k])
        pivots, inverse, scaled = [row_of(columns[0], 0)], [], {}
        for i in range(BLOCK):
            inv = pl.reciprocal(pivots[i], approx=True)
            inverse.append(inv)
            beside = {c: row_of(columns[c], i) for c in range(i + 1, BLOCK)}
            if i + 1 < BLOCK:
                square = beside[i + 1] * beside[i + 1]
                pivots.append(row_of(columns[i + 1], i + 1) - square * inv)
            for c in range(i + 1, BLOCK):
                scaled[c, i] = beside[c] * inv
                columns[c] = columns[c] - columns[i] * scaled[c, i]
            for k in near:
                here = weights[k][i]
                weight = here * inv
                if k == block + 1:
                    splats = [row_of(here, c) for c in range(BLOCK)]
                if k in changes:
                    for c in range(BLOCK):
                        change = weight * splats[c]
                        changes[k][c] = change if i == 0 else changes[k][c] + change
                for c in range(i + 1, BLOCK):
                    weights[k][c] = weights[k][c] - here * scaled[c, i]
                tiles[k] = tiles[k] - weight * rows[i]
            for r in range(i + 1, BLOCK):
                rows[r] = rows[r] - scaled[r, i] * rows[i]
        updated = {k: [base - change for base, change in zip(bases[k], changes[k])] for k in bases}
        following, carried = updated.get(block + 1), updated.get(block + 2)
        merged = gather(rows) * lax.rsqrt(gather(pivots))
        lower_rows.append(jnp.where(spread_ids <= offset, merged, 0.0))
        if block + 1 + AHEAD < count:
            solved = [None] * BLOCK
            for r in reversed(range(BLOCK)):
                solved[r] = rows[r] * inverse[r]
                for c in range(r + 1, BLOCK):
                    solved[r] = solved[r] - scaled[c, r] * solved[c]
            for k in range(block + 1 + AHEAD, count):
                terms = [lanes_of(tiles[k], offset + c) * solved[c] for c in range(BLOCK)]
                while len(terms) > 1:
                    terms = [terms[t] + terms[t + 1] for t in range(0, len(terms), 2)]
                tiles[k] = jnp.where(in_block, 0.0, tiles[k]) - terms[0]
    return jnp.concatenate(lower_rows, axis=0)


def packed_rows(order, probes):
    return -(-(order // 2 + probes + 1) // (2 * BLOCK)) * 2 * BLOCK


def own_part():
    bits = lax.axis_index("cells") ^ lax.axis_index("sub")
    for shift in (16, 8, 4, 2, 1):
        bits = bits ^ (bits >> shift)
    return bits & 1


def live_volumes(volumes_ref, live_ref, begin):
    ids = lax.broadcasted_iota(jnp.int32, (1, LANES), 1) + begin
    part = volumes_ref[pl.ds(begin, LANES)].reshape(1, LANES)
    return jnp.where(ids < live_ref[0], part, 0.0)


def sums_kernel(total_rows, snapshots_hbm, volumes_hbm, live_ref, probes_hbm, keep_ref, send_ref, scale_ref, snapshots_ref, volumes_ref, probes_ref, packed, sems):
    row_count, order = snapshots_ref.shape
    parts = [pl.ds(begin, LANES) for begin in range(0, row_count, LANES)]
    transfers = [(volumes_hbm, volumes_ref), *((snapshots_hbm.at[rows], snapshots_ref.at[rows]) for rows in parts)]
    transfers.append((probes_hbm, probes_ref))
    copies = [pltpu.make_async_copy(source, target, sems.at[i]) for i, (source, target) in enumerate(transfers)]
    for copy in copies:
        copy.start()
    probes = probes_ref.shape[0]
    half = order // 2
    copies[0].wait()
    volume = jnp.concatenate([live_volumes(volumes_ref, live_ref, b) for b in range(0, row_count, LANES)], axis=1)
    scale_ref[...] = jnp.sqrt(volume)
    weight = volume * (1.0 / total_rows)
    gram = jnp.zeros((order, order), F32)
    group = 2
    for begin in range(0, len(parts), group):
        for copy in copies[1 + begin : 1 + min(begin + group, len(parts))]:
            copy.wait()
        rows = slice(begin * LANES, min((begin + group) * LANES, row_count))
        block = snapshots_ref[rows, :]
        gram = gram + product(block.T * weight[:, rows], block, ((1,), (0,)))
    row_ids = lax.broadcasted_iota(jnp.int32, (half, half), 0)
    column_ids = lax.broadcasted_iota(jnp.int32, (half, half), 1)
    packed[:half, :half] = jnp.where(row_ids <= column_ids, gram[:half, :half], gram[half:, half:])
    packed[:half, half:] = gram[:half, half:]
    rest = packed.shape[0] - half - probes
    diagonal = jnp.sum(jnp.where(row_ids == column_ids, gram[half:, half:], 0.0), axis=0, keepdims=True)
    packed[half + probes :, :] = jnp.concatenate([jnp.broadcast_to(diagonal, (rest, half))] * 2, axis=1)
    copies[-1].wait()
    probe_scaled = probes_ref[...] * (volume * (1.0 / total_rows**0.5))
    packed[half : half + probes, :] = product(probe_scaled, snapshots_ref[...], ((1,), (0,)))
    middle = packed.shape[0] // 2
    low = own_part() == 0

    @pl.when(low)
    def _():
        keep_ref[...] = packed[:middle, :]
        send_ref[...] = packed[middle:, :]

    @pl.when(jnp.logical_not(low))
    def _():
        keep_ref[...] = packed[middle:, :]
        send_ref[...] = packed[:middle, :]


def hold(array):
    return pltpu.with_memory_space_constraint(array, pltpu.HBM)


def local_sums(total_rows, snapshots, volumes, live_rows, probes):
    order = snapshots.shape[1]
    size = packed_rows(order, probes.shape[0])
    hbm = pl.BlockSpec(memory_space=pltpu.HBM)
    whole = pl.BlockSpec(memory_space=pltpu.VMEM)
    return pl.pallas_call(
        functools.partial(sums_kernel, total_rows),
        out_shape=(jax.ShapeDtypeStruct((size // 2, order), F32),) * 2 + (jax.ShapeDtypeStruct((1, volumes.shape[0]), F32),),
        in_specs=[hbm, hbm, pl.BlockSpec(memory_space=pltpu.SMEM), hbm],
        out_specs=(whole, whole, whole),
        scratch_shapes=[
            pltpu.VMEM(snapshots.shape, F32),
            pltpu.VMEM(volumes.shape, F32),
            pltpu.VMEM(probes.shape, F32),
            pltpu.VMEM((size, order), F32),
            pltpu.SemaphoreType.DMA((2 + snapshots.shape[0] // LANES,)),
        ],
        compiler_params=pltpu.CompilerParams(vmem_limit_bytes=24 * 1024 * 1024),
    )(hold(snapshots), hold(volumes), live_rows, hold(probes))


def weigh_kernel(snapshots_ref, scale_ref, weighted_ref):
    row_count, order = snapshots_ref.shape
    for begin in range(0, row_count, LANES):
        rows = pl.ds(begin, LANES)
        scale = jnp.broadcast_to(scale_ref[:, rows], (LANES, LANES)).T
        weighted_ref[rows, :] = snapshots_ref[rows, :] * jnp.concatenate([scale] * (order // LANES), axis=1)


def weigh(snapshots, scale):
    whole = pl.BlockSpec(memory_space=pltpu.VMEM)
    return pl.pallas_call(
        weigh_kernel,
        out_shape=jax.ShapeDtypeStruct(snapshots.shape, F32),
        in_specs=[whole, whole],
        out_specs=whole,
        compiler_params=pltpu.CompilerParams(vmem_limit_bytes=24 * 1024 * 1024),
        cost_estimate=pl.CostEstimate(flops=snapshots.size, bytes_accessed=8 * snapshots.size, transcendentals=0),
    )(snapshots, scale)


def finish_kernel(mine_ref, other_ref, weighted_ref, basis_hbm, factor_hbm, coef_hbm, basis_ref, factor_ref, coef_ref, sems):
    row_count, order = weighted_ref.shape
    probes = coef_ref.shape[0]
    half = order // 2
    copies = []

    def write(source, target, rows, columns):
        copy = pltpu.make_async_copy(source.at[rows, columns], target.at[rows, columns], sems.at[len(copies)])
        copy.start()
        copies.append(copy)

    low = own_part() == 0
    mine, other = mine_ref[...], other_ref[...]
    packed = jnp.concatenate([jnp.where(low, mine, other), jnp.where(low, other, mine)], axis=0)
    row_ids = lax.broadcasted_iota(jnp.int32, (half, half), 0)
    column_ids = lax.broadcasted_iota(jnp.int32, (half, half), 1)
    in_upper = row_ids <= column_ids
    square = packed[:half, :half]
    turned = square.T
    cross = packed[half : half + probes, :]
    diagonal = packed[half + probes : half + probes + 1, :half]

    first = jnp.where(in_upper, square, turned)
    inverse = eliminate(first)
    beside = product(inverse, packed[:half, half:], ((1,), (0,)))
    second = jnp.where(row_ids > column_ids, square, turned)
    second = jnp.where(row_ids == column_ids, diagonal, second) - product(beside, beside, ((0,), (0,)))
    factor_ref[:half, :half] = jnp.where(in_upper, product(inverse, first, ((1,), (0,))), 0.0)
    factor_ref[:half, half:] = beside
    factor_ref[half:, :half] = jnp.zeros((half, half), F32)
    left = product(weighted_ref[:, :half], inverse, ((1,), (1,)))
    basis_ref[:, :half] = left
    write(basis_ref, basis_hbm, pl.ds(0, row_count), pl.ds(0, half))
    write(factor_ref, factor_hbm, pl.ds(0, half), pl.ds(0, order))
    rest = weighted_ref[:, half:] - product(left, beside, ((1,), (0,)))
    left = product(cross[:, :half], inverse, ((1,), (1,)))
    coef_ref[:, :half] = left
    cross_rest = cross[:, half:] - product(left, beside, ((1,), (0,)))

    inverse_second = eliminate(second)
    for begin in range(0, row_count, LANES):
        rows = pl.ds(begin, LANES)
        basis_ref[rows, half:] = product(rest[begin : begin + LANES, :], inverse_second, ((1,), (1,)))
        write(basis_ref, basis_hbm, rows, pl.ds(half, half))
    factor_ref[half:, half:] = jnp.where(in_upper, product(inverse_second, second, ((1,), (0,))), 0.0)
    write(factor_ref, factor_hbm, pl.ds(half, half), pl.ds(0, order))
    coef_ref[:, half:] = product(cross_rest, inverse_second, ((1,), (1,)))
    write(coef_ref, coef_hbm, pl.ds(0, probes), pl.ds(0, order))
    for copy in copies:
        copy.wait()


def finish(mine, other, weighted, probes):
    row_count, order = weighted.shape
    whole = pl.BlockSpec(memory_space=pltpu.VMEM)
    shapes = (row_count, order), (order, order), (probes, order)
    return pl.pallas_call(
        finish_kernel,
        out_shape=tuple(jax.ShapeDtypeStruct(shape, F32) for shape in shapes),
        in_specs=[whole] * 3,
        out_specs=(pl.BlockSpec(memory_space=pltpu.HBM),) * 3,
        scratch_shapes=[
            *(pltpu.VMEM(shape, F32) for shape in shapes),
            pltpu.SemaphoreType.DMA((row_count // LANES + 4,)),
        ],
        compiler_params=pltpu.CompilerParams(vmem_limit_bytes=32 * 1024 * 1024),
    )(mine, other, weighted)


def exchange(value, masks):
    count = lax.axis_size("cells") * lax.axis_size("sub")
    pairs = [(i, i ^ masks[bin(i).count("1") % 2]) for i in range(count)]
    return lax.ppermute(value, ("cells", "sub"), pairs)


def reduce_halves(keep, send):
    count = lax.axis_size("cells") * lax.axis_size("sub")
    bits = [1 << k for k in range(1, count.bit_length() - 1)]
    phases = [bits[k : k + 2] for k in range(0, len(bits) - 1, 2)]
    split = len(phases) // 2
    mine = keep + exchange(send, (1, 1))
    for even, odd in zip(phases, phases[split:] + phases[:split]):
        near = exchange(mine, (even[0] ^ 1, odd[0] ^ 1))
        far = exchange(mine, (even[1] ^ 1, odd[1] ^ 1))
        across = exchange(mine, (even[0] ^ even[1], odd[0] ^ odd[1]))
        mine = (mine + near) + (far + across)
    for bit in bits[2 * len(phases) :]:
        mine = mine + exchange(mine, (bit ^ 1, bit ^ 1))
    return mine, exchange(mine, (1, 1))


def per_device(snapshots, volumes, live_rows, probes):
    count = lax.axis_size("cells") * lax.axis_size("sub")
    keep, send, scale = local_sums(snapshots.shape[0] * count, snapshots, volumes, live_rows, probes)
    mine, other = reduce_halves(keep, send)
    return finish(mine, other, weigh(snapshots, scale), probes.shape[0])


def solution(mesh):
    placed = (
        P(("cells", "sub"), None),
        P(("cells", "sub")),
        P(("cells", "sub")),
        P(None, ("cells", "sub")),
    )
    return jax.shard_map(
        per_device,
        mesh=mesh,
        in_specs=placed,
        out_specs=(P(("cells", "sub"), None), P(), P()),
        check_vma=False,
    )
```

```python
import functools
import jax
import jax.numpy as jnp
from jax import lax
from jax.experimental import pallas as pl
from jax.experimental.pallas import tpu as pltpu
from jax.sharding import PartitionSpec as P

HIGHEST = lax.Precision.HIGHEST
LANES = 128
BLOCK = 8
AHEAD = 2
F32 = jnp.float32


def lanes_of(tile, column):
    return jnp.broadcast_to(tile[:, column : column + 1], tile.shape)


def row_of(tile, index):
    return jnp.broadcast_to(tile[index : index + 1, :], tile.shape)


def product(left, right, dims):
    return lax.dot_general(left, right, (dims, ((), ())), precision=HIGHEST, preferred_element_type=F32)


def eliminate(matrix):
    width = matrix.shape[1]
    count = width // BLOCK
    shape = (BLOCK, width)
    tiles = [matrix[k * BLOCK : (k + 1) * BLOCK, :] for k in range(count)]
    sub_ids = lax.broadcasted_iota(jnp.int32, shape, 0)
    lane_ids = lax.broadcasted_iota(jnp.int32, shape, 1)
    spread_ids = lane_ids - sub_ids

    def gather(parts):
        total = parts[0]
        for r in range(1, BLOCK):
            total = jnp.where(sub_ids == r, parts[r], total)
        return total

    lower_rows = []
    following = [lanes_of(tiles[0], c) for c in range(BLOCK)]
    carried = [lanes_of(tiles[1], c) for c in range(BLOCK)]
    for block in range(count):
        offset = block * BLOCK
        in_block = (lane_ids >= offset) & (lane_ids < offset + BLOCK)
        columns = following
        own = jnp.where(in_block, jnp.where(spread_ids == offset, 1.0, 0.0), tiles[block])
        rows = [row_of(own, r) for r in range(BLOCK)]
        near = range(block + 1, min(block + 1 + AHEAD, count))
        weights = {k: [lanes_of(tiles[k], offset + c) for c in range(BLOCK)] for k in near if k > block + 1}
        weights[block + 1] = carried
        bases = {k: [lanes_of(tiles[k], offset + BLOCK + c) for c in range(BLOCK)] for k in near if k <= block + 2}
        changes = {k: [None] * BLOCK for k in bases}
        for k in near:
            tiles[k] = jnp.where(in_block, 0.0, tiles[k])
        pivots, inverse, scaled = [row_of(columns[0], 0)], [], {}
        for i in range(BLOCK):
            inv = pl.reciprocal(pivots[i], approx=True)
            inverse.append(inv)
            beside = {c: row_of(columns[c], i) for c in range(i + 1, BLOCK)}
            if i + 1 < BLOCK:
                square = beside[i + 1] * beside[i + 1]
                pivots.append(row_of(columns[i + 1], i + 1) - square * inv)
            for c in range(i + 1, BLOCK):
                scaled[c, i] = beside[c] * inv
                columns[c] = columns[c] - columns[i] * scaled[c, i]
            for k in near:
                here = weights[k][i]
                weight = here * inv
                if k == block + 1:
                    splats = [row_of(here, c) for c in range(BLOCK)]
                if k in changes:
                    for c in range(BLOCK):
                        change = weight * splats[c]
                        changes[k][c] = change if i == 0 else changes[k][c] + change
                for c in range(i + 1, BLOCK):
                    weights[k][c] = weights[k][c] - here * scaled[c, i]
                tiles[k] = tiles[k] - weight * rows[i]
            for r in range(i + 1, BLOCK):
                rows[r] = rows[r] - scaled[r, i] * rows[i]
        updated = {k: [base - change for base, change in zip(bases[k], changes[k])] for k in bases}
        following, carried = updated.get(block + 1), updated.get(block + 2)
        merged = gather(rows) * lax.rsqrt(gather(pivots))
        lower_rows.append(jnp.where(spread_ids <= offset, merged, 0.0))
        if block + 1 + AHEAD < count:
            solved = [None] * BLOCK
            for r in reversed(range(BLOCK)):
                solved[r] = rows[r] * inverse[r]
                for c in range(r + 1, BLOCK):
                    solved[r] = solved[r] - scaled[c, r] * solved[c]
            for k in range(block + 1 + AHEAD, count):
                terms = [lanes_of(tiles[k], offset + c) * solved[c] for c in range(BLOCK)]
                while len(terms) > 1:
                    terms = [terms[t] + terms[t + 1] for t in range(0, len(terms), 2)]
                tiles[k] = jnp.where(in_block, 0.0, tiles[k]) - terms[0]
    return jnp.concatenate(lower_rows, axis=0)


def packed_rows(order, probes):
    return -(-(order // 2 + probes + 1) // (2 * BLOCK)) * 2 * BLOCK


def chip_bits():
    count = lax.axis_size("cells") * lax.axis_size("sub")
    bits = [1 << k for k in range(1, count.bit_length() - 1)]
    whole = len(bits) // 2 * 2
    return [bits[k : k + 2] for k in range(0, whole, 2)], bits[whole:]


def part_mask():
    return 1 + sum(pair[0] for pair in chip_bits()[0])


def own_part():
    bits = (lax.axis_index("cells") * lax.axis_size("sub") + lax.axis_index("sub")) & part_mask()
    for shift in (16, 8, 4, 2, 1):
        bits = bits ^ (bits >> shift)
    return bits & 1


def live_volumes(volumes_ref, live_ref, begin):
    ids = lax.broadcasted_iota(jnp.int32, (1, LANES), 1) + begin
    part = volumes_ref[pl.ds(begin, LANES)].reshape(1, LANES)
    return jnp.where(ids < live_ref[0], part, 0.0)


def sums_kernel(total_rows, snapshots_hbm, volumes_hbm, live_ref, probes_hbm, keep_ref, send_ref, scale_ref, snapshots_ref, volumes_ref, probes_ref, packed, sems):
    copies = [
        pltpu.make_async_copy(source, target, sems.at[i])
        for i, (source, target) in enumerate(
            ((volumes_hbm, volumes_ref), (snapshots_hbm, snapshots_ref), (probes_hbm, probes_ref))
        )
    ]
    for copy in copies:
        copy.start()
    row_count, order = snapshots_ref.shape
    probes = probes_ref.shape[0]
    half = order // 2
    copies[0].wait()
    volume = jnp.concatenate([live_volumes(volumes_ref, live_ref, b) for b in range(0, row_count, LANES)], axis=1)
    scale_ref[...] = jnp.sqrt(volume)
    copies[1].wait()
    snapshots = snapshots_ref[...]
    scaled = snapshots.T * (volume * (1.0 / total_rows))
    gram = product(scaled, snapshots, ((1,), (0,)))
    row_ids = lax.broadcasted_iota(jnp.int32, (half, half), 0)
    column_ids = lax.broadcasted_iota(jnp.int32, (half, half), 1)
    packed[:half, :half] = jnp.where(row_ids <= column_ids, gram[:half, :half], gram[half:, half:])
    packed[:half, half:] = gram[:half, half:]
    rest = packed.shape[0] - half - probes
    diagonal = jnp.sum(jnp.where(row_ids == column_ids, gram[half:, half:], 0.0), axis=0, keepdims=True)
    packed[half + probes :, :] = jnp.concatenate([jnp.broadcast_to(diagonal, (rest, half))] * 2, axis=1)
    copies[2].wait()
    probe_scaled = probes_ref[...] * (volume * (1.0 / total_rows**0.5))
    packed[half : half + probes, :] = product(probe_scaled, snapshots, ((1,), (0,)))
    middle = packed.shape[0] // 2
    low = own_part() == 0

    @pl.when(low)
    def _():
        keep_ref[...] = packed[:middle, :]
        send_ref[...] = packed[middle:, :]

    @pl.when(jnp.logical_not(low))
    def _():
        keep_ref[...] = packed[middle:, :]
        send_ref[...] = packed[:middle, :]


def hold(array):
    return pltpu.with_memory_space_constraint(array, pltpu.HBM)


def local_sums(total_rows, snapshots, volumes, live_rows, probes):
    order = snapshots.shape[1]
    size = packed_rows(order, probes.shape[0])
    hbm = pl.BlockSpec(memory_space=pltpu.HBM)
    whole = pl.BlockSpec(memory_space=pltpu.VMEM)
    return pl.pallas_call(
        functools.partial(sums_kernel, total_rows),
        out_shape=(jax.ShapeDtypeStruct((size // 2, order), F32),) * 2 + (jax.ShapeDtypeStruct((1, volumes.shape[0]), F32),),
        in_specs=[hbm, hbm, pl.BlockSpec(memory_space=pltpu.SMEM), hbm],
        out_specs=(whole, whole, whole),
        scratch_shapes=[
            pltpu.VMEM(snapshots.shape, F32),
            pltpu.VMEM(volumes.shape, F32),
            pltpu.VMEM(probes.shape, F32),
            pltpu.VMEM((size, order), F32),
            pltpu.SemaphoreType.DMA((3,)),
        ],
        compiler_params=pltpu.CompilerParams(vmem_limit_bytes=24 * 1024 * 1024),
    )(hold(snapshots), hold(volumes), live_rows, hold(probes))


def weigh_kernel(snapshots_ref, scale_ref, weighted_ref):
    row_count, order = snapshots_ref.shape
    for begin in range(0, row_count, LANES):
        rows = pl.ds(begin, LANES)
        scale = jnp.broadcast_to(scale_ref[:, rows], (LANES, LANES)).T
        weighted_ref[rows, :] = snapshots_ref[rows, :] * jnp.concatenate([scale] * (order // LANES), axis=1)


def weigh(snapshots, scale):
    whole = pl.BlockSpec(memory_space=pltpu.VMEM)
    return pl.pallas_call(
        weigh_kernel,
        out_shape=jax.ShapeDtypeStruct(snapshots.shape, F32),
        in_specs=[whole, whole],
        out_specs=whole,
        compiler_params=pltpu.CompilerParams(vmem_limit_bytes=24 * 1024 * 1024),
        cost_estimate=pl.CostEstimate(flops=snapshots.size, bytes_accessed=8 * snapshots.size, transcendentals=0),
    )(snapshots, scale)


def finish_kernel(mine_ref, other_ref, weighted_ref, basis_ref, factor_ref, coef_ref):
    order = weighted_ref.shape[1]
    probes = coef_ref.shape[0]
    half = order // 2
    low = own_part() == 0
    mine, other = mine_ref[...], other_ref[...]
    packed = jnp.concatenate([jnp.where(low, mine, other), jnp.where(low, other, mine)], axis=0)
    row_ids = lax.broadcasted_iota(jnp.int32, (half, half), 0)
    column_ids = lax.broadcasted_iota(jnp.int32, (half, half), 1)
    in_upper = row_ids <= column_ids
    square = packed[:half, :half]
    turned = square.T
    cross = packed[half : half + probes, :]
    diagonal = packed[half + probes : half + probes + 1, :half]

    first = jnp.where(in_upper, square, turned)
    inverse = eliminate(first)
    beside = product(inverse, packed[:half, half:], ((1,), (0,)))
    second = jnp.where(row_ids > column_ids, square, turned)
    second = jnp.where(row_ids == column_ids, diagonal, second) - product(beside, beside, ((0,), (0,)))
    factor_ref[:half, :half] = jnp.where(in_upper, product(inverse, first, ((1,), (0,))), 0.0)
    factor_ref[:half, half:] = beside
    factor_ref[half:, :half] = jnp.zeros((half, half), F32)

    left = product(cross[:, :half], inverse, ((1,), (1,)))
    coef_ref[:, :half] = left
    cross_rest = cross[:, half:] - product(left, beside, ((1,), (0,)))
    left = product(weighted_ref[:, :half], inverse, ((1,), (1,)))
    basis_ref[:, :half] = left
    rest = weighted_ref[:, half:] - product(left, beside, ((1,), (0,)))

    inverse_second = eliminate(second)
    coef_ref[:, half:] = product(cross_rest, inverse_second, ((1,), (1,)))
    basis_ref[:, half:] = product(rest, inverse_second, ((1,), (1,)))
    factor_ref[half:, half:] = jnp.where(in_upper, product(inverse_second, second, ((1,), (0,))), 0.0)


def finish(mine, other, weighted, probes):
    row_count, order = weighted.shape
    whole = pl.BlockSpec(memory_space=pltpu.VMEM)
    return pl.pallas_call(
        finish_kernel,
        out_shape=(
            jax.ShapeDtypeStruct((row_count, order), F32),
            jax.ShapeDtypeStruct((order, order), F32),
            jax.ShapeDtypeStruct((probes, order), F32),
        ),
        in_specs=[whole] * 3,
        out_specs=(whole,) * 3,
        compiler_params=pltpu.CompilerParams(vmem_limit_bytes=32 * 1024 * 1024),
    )(mine, other, weighted)


def exchange(value, masks):
    count = lax.axis_size("cells") * lax.axis_size("sub")
    pairs = [(i, i ^ masks[bin(i & part_mask()).count("1") % 2]) for i in range(count)]
    return lax.ppermute(value, ("cells", "sub"), pairs)


def reduce_halves(keep, send):
    phases, single = chip_bits()
    split = len(phases) // 2
    mine = keep + exchange(send, (1, 1))
    for (low, high), (other_low, other_high) in zip(phases, phases[split:] + phases[:split]):
        near = exchange(mine, (low ^ 1, other_low ^ 1))
        far = exchange(mine, (high, other_high))
        across = exchange(mine, (low ^ high ^ 1, other_low ^ other_high ^ 1))
        mine = (mine + near) + (far + across)
    for bit in single:
        mine = mine + exchange(mine, (bit, bit))
    return mine, exchange(mine, (1, 1))


def per_device(snapshots, volumes, live_rows, probes):
    count = lax.axis_size("cells") * lax.axis_size("sub")
    keep, send, scale = local_sums(snapshots.shape[0] * count, snapshots, volumes, live_rows, probes)
    mine, other = reduce_halves(keep, send)
    return finish(mine, other, weigh(snapshots, scale), probes.shape[0])


def solution(mesh):
    placed = (
        P(("cells", "sub"), None),
        P(("cells", "sub")),
        P(("cells", "sub")),
        P(None, ("cells", "sub")),
    )
    return jax.shard_map(
        per_device,
        mesh=mesh,
        in_specs=placed,
        out_specs=(P(("cells", "sub"), None), P(), P()),
        check_vma=False,
    )
```

```python
import functools
import jax
import jax.numpy as jnp
from jax import lax
from jax.experimental import pallas as pl
from jax.experimental.pallas import tpu as pltpu
from jax.sharding import PartitionSpec as P

HIGHEST = lax.Precision.HIGHEST
LANES = 128
BLOCK = 8
AHEAD = 2
F32 = jnp.float32


def lanes_of(tile, column):
    return jnp.broadcast_to(tile[:, column : column + 1], tile.shape)


def row_of(tile, index):
    return jnp.broadcast_to(tile[index : index + 1, :], tile.shape)


def product(left, right, dims):
    return lax.dot_general(left, right, (dims, ((), ())), precision=HIGHEST, preferred_element_type=F32)


def eliminate(matrix):
    width = matrix.shape[1]
    count = width // BLOCK
    shape = (BLOCK, width)
    tiles = [matrix[k * BLOCK : (k + 1) * BLOCK, :] for k in range(count)]
    sub_ids = lax.broadcasted_iota(jnp.int32, shape, 0)
    lane_ids = lax.broadcasted_iota(jnp.int32, shape, 1)
    spread_ids = lane_ids - sub_ids

    def gather(parts):
        total = parts[0]
        for r in range(1, BLOCK):
            total = jnp.where(sub_ids == r, parts[r], total)
        return total

    lower_rows = []
    for block in range(count):
        offset = block * BLOCK
        in_block = (lane_ids >= offset) & (lane_ids < offset + BLOCK)
        columns = [lanes_of(tiles[block], offset + c) for c in range(BLOCK)]
        own = jnp.where(in_block, jnp.where(spread_ids == offset, 1.0, 0.0), tiles[block])
        rows = [row_of(own, r) for r in range(BLOCK)]
        near = range(block + 1, min(block + 1 + AHEAD, count))
        weights = {k: [lanes_of(tiles[k], offset + c) for c in range(BLOCK)] for k in near}
        for k in near:
            tiles[k] = jnp.where(in_block, 0.0, tiles[k])
        pivots, inverse, scaled = [row_of(columns[0], 0)], [], {}
        for i in range(BLOCK):
            inv = pl.reciprocal(pivots[i], approx=True)
            inverse.append(inv)
            beside = {c: row_of(columns[c], i) for c in range(i + 1, BLOCK)}
            if i + 1 < BLOCK:
                square = beside[i + 1] * beside[i + 1]
                pivots.append(row_of(columns[i + 1], i + 1) - square * inv)
            for c in range(i + 1, BLOCK):
                scaled[c, i] = beside[c] * inv
                columns[c] = columns[c] - columns[i] * scaled[c, i]
            for k in near:
                here = weights[k][i]
                weight = here * inv
                for c in range(i + 1, BLOCK):
                    weights[k][c] = weights[k][c] - here * scaled[c, i]
                tiles[k] = tiles[k] - weight * rows[i]
            for r in range(i + 1, BLOCK):
                rows[r] = rows[r] - scaled[r, i] * rows[i]
        merged = gather(rows) * lax.rsqrt(gather(pivots))
        lower_rows.append(jnp.where(spread_ids <= offset, merged, 0.0))
        if block + 1 + AHEAD < count:
            solved = [None] * BLOCK
            for r in reversed(range(BLOCK)):
                solved[r] = rows[r] * inverse[r]
                for c in range(r + 1, BLOCK):
                    solved[r] = solved[r] - scaled[c, r] * solved[c]
            for k in range(block + 1 + AHEAD, count):
                terms = [lanes_of(tiles[k], offset + c) * solved[c] for c in range(BLOCK)]
                while len(terms) > 1:
                    terms = [terms[t] + terms[t + 1] for t in range(0, len(terms), 2)]
                tiles[k] = jnp.where(in_block, 0.0, tiles[k]) - terms[0]
    return jnp.concatenate(lower_rows, axis=0)


def packed_rows(order, probes):
    return -(-(order // 2 + probes + 1) // (2 * BLOCK)) * 2 * BLOCK


def chip_bits():
    count = lax.axis_size("cells") * lax.axis_size("sub")
    bits = [1 << k for k in range(1, count.bit_length() - 1)]
    whole = len(bits) // 2 * 2
    return [bits[k : k + 2] for k in range(0, whole, 2)], bits[whole:]


def part_mask():
    return 1 + sum(pair[0] for pair in chip_bits()[0])


def own_part():
    bits = (lax.axis_index("cells") * lax.axis_size("sub") + lax.axis_index("sub")) & part_mask()
    for shift in (16, 8, 4, 2, 1):
        bits = bits ^ (bits >> shift)
    return bits & 1


def live_volumes(volumes_ref, live_ref, begin):
    ids = lax.broadcasted_iota(jnp.int32, (1, LANES), 1) + begin
    part = volumes_ref[pl.ds(begin, LANES)].reshape(1, LANES)
    return jnp.where(ids < live_ref[0], part, 0.0)


def sums_kernel(total_rows, snapshots_hbm, volumes_hbm, live_ref, probes_hbm, keep_ref, send_ref, scale_ref, snapshots_ref, volumes_ref, probes_ref, packed, sems):
    copies = [
        pltpu.make_async_copy(source, target, sems.at[i])
        for i, (source, target) in enumerate(
            ((volumes_hbm, volumes_ref), (snapshots_hbm, snapshots_ref), (probes_hbm, probes_ref))
        )
    ]
    for copy in copies:
        copy.start()
    row_count, order = snapshots_ref.shape
    probes = probes_ref.shape[0]
    half = order // 2
    copies[0].wait()
    volume = jnp.concatenate([live_volumes(volumes_ref, live_ref, b) for b in range(0, row_count, LANES)], axis=1)
    scale_ref[...] = jnp.sqrt(volume)
    copies[1].wait()
    snapshots = snapshots_ref[...]
    scaled = snapshots.T * (volume * (1.0 / total_rows))
    gram = product(scaled, snapshots, ((1,), (0,)))
    row_ids = lax.broadcasted_iota(jnp.int32, (half, half), 0)
    column_ids = lax.broadcasted_iota(jnp.int32, (half, half), 1)
    packed[:half, :half] = jnp.where(row_ids <= column_ids, gram[:half, :half], gram[half:, half:])
    packed[:half, half:] = gram[:half, half:]
    rest = packed.shape[0] - half - probes
    diagonal = jnp.sum(jnp.where(row_ids == column_ids, gram[half:, half:], 0.0), axis=0, keepdims=True)
    packed[half + probes :, :] = jnp.concatenate([jnp.broadcast_to(diagonal, (rest, half))] * 2, axis=1)
    copies[2].wait()
    probe_scaled = probes_ref[...] * (volume * (1.0 / total_rows**0.5))
    packed[half : half + probes, :] = product(probe_scaled, snapshots, ((1,), (0,)))
    middle = packed.shape[0] // 2
    low = own_part() == 0

    @pl.when(low)
    def _():
        keep_ref[...] = packed[:middle, :]
        send_ref[...] = packed[middle:, :]

    @pl.when(jnp.logical_not(low))
    def _():
        keep_ref[...] = packed[middle:, :]
        send_ref[...] = packed[:middle, :]


def hold(array):
    return pltpu.with_memory_space_constraint(array, pltpu.HBM)


def local_sums(total_rows, snapshots, volumes, live_rows, probes):
    order = snapshots.shape[1]
    size = packed_rows(order, probes.shape[0])
    hbm = pl.BlockSpec(memory_space=pltpu.HBM)
    whole = pl.BlockSpec(memory_space=pltpu.VMEM)
    return pl.pallas_call(
        functools.partial(sums_kernel, total_rows),
        out_shape=(jax.ShapeDtypeStruct((size // 2, order), F32),) * 2 + (jax.ShapeDtypeStruct((1, volumes.shape[0]), F32),),
        in_specs=[hbm, hbm, pl.BlockSpec(memory_space=pltpu.SMEM), hbm],
        out_specs=(whole, whole, whole),
        scratch_shapes=[
            pltpu.VMEM(snapshots.shape, F32),
            pltpu.VMEM(volumes.shape, F32),
            pltpu.VMEM(probes.shape, F32),
            pltpu.VMEM((size, order), F32),
            pltpu.SemaphoreType.DMA((3,)),
        ],
        compiler_params=pltpu.CompilerParams(vmem_limit_bytes=24 * 1024 * 1024),
    )(hold(snapshots), hold(volumes), live_rows, hold(probes))


def weigh_kernel(snapshots_ref, scale_ref, weighted_ref):
    row_count, order = snapshots_ref.shape
    for begin in range(0, row_count, LANES):
        rows = pl.ds(begin, LANES)
        scale = jnp.broadcast_to(scale_ref[:, rows], (LANES, LANES)).T
        weighted_ref[rows, :] = snapshots_ref[rows, :] * jnp.concatenate([scale] * (order // LANES), axis=1)


def weigh(snapshots, scale):
    whole = pl.BlockSpec(memory_space=pltpu.VMEM)
    return pl.pallas_call(
        weigh_kernel,
        out_shape=jax.ShapeDtypeStruct(snapshots.shape, F32),
        in_specs=[whole, whole],
        out_specs=whole,
        compiler_params=pltpu.CompilerParams(vmem_limit_bytes=24 * 1024 * 1024),
        cost_estimate=pl.CostEstimate(flops=snapshots.size, bytes_accessed=8 * snapshots.size, transcendentals=0),
    )(snapshots, scale)


def finish_kernel(mine_ref, other_ref, weighted_ref, basis_ref, factor_ref, coef_ref):
    order = weighted_ref.shape[1]
    probes = coef_ref.shape[0]
    half = order // 2
    low = own_part() == 0
    mine, other = mine_ref[...], other_ref[...]
    packed = jnp.concatenate([jnp.where(low, mine, other), jnp.where(low, other, mine)], axis=0)
    row_ids = lax.broadcasted_iota(jnp.int32, (half, half), 0)
    column_ids = lax.broadcasted_iota(jnp.int32, (half, half), 1)
    in_upper = row_ids <= column_ids
    square = packed[:half, :half]
    turned = square.T
    cross = packed[half : half + probes, :]
    diagonal = packed[half + probes : half + probes + 1, :half]

    first = jnp.where(in_upper, square, turned)
    inverse = eliminate(first)
    beside = product(inverse, packed[:half, half:], ((1,), (0,)))
    second = jnp.where(row_ids > column_ids, square, turned)
    second = jnp.where(row_ids == column_ids, diagonal, second) - product(beside, beside, ((0,), (0,)))
    factor_ref[:half, :half] = jnp.where(in_upper, product(inverse, first, ((1,), (0,))), 0.0)
    factor_ref[:half, half:] = beside
    factor_ref[half:, :half] = jnp.zeros((half, half), F32)

    left = product(cross[:, :half], inverse, ((1,), (1,)))
    coef_ref[:, :half] = left
    cross_rest = cross[:, half:] - product(left, beside, ((1,), (0,)))
    left = product(weighted_ref[:, :half], inverse, ((1,), (1,)))
    basis_ref[:, :half] = left
    rest = weighted_ref[:, half:] - product(left, beside, ((1,), (0,)))

    inverse_second = eliminate(second)
    coef_ref[:, half:] = product(cross_rest, inverse_second, ((1,), (1,)))
    basis_ref[:, half:] = product(rest, inverse_second, ((1,), (1,)))
    factor_ref[half:, half:] = jnp.where(in_upper, product(inverse_second, second, ((1,), (0,))), 0.0)


def finish(mine, other, weighted, probes):
    row_count, order = weighted.shape
    whole = pl.BlockSpec(memory_space=pltpu.VMEM)
    return pl.pallas_call(
        finish_kernel,
        out_shape=(
            jax.ShapeDtypeStruct((row_count, order), F32),
            jax.ShapeDtypeStruct((order, order), F32),
            jax.ShapeDtypeStruct((probes, order), F32),
        ),
        in_specs=[whole] * 3,
        out_specs=(whole,) * 3,
        compiler_params=pltpu.CompilerParams(vmem_limit_bytes=32 * 1024 * 1024),
    )(mine, other, weighted)


def exchange(value, masks):
    count = lax.axis_size("cells") * lax.axis_size("sub")
    pairs = [(i, i ^ masks[bin(i & part_mask()).count("1") % 2]) for i in range(count)]
    return lax.ppermute(value, ("cells", "sub"), pairs)


def reduce_halves(keep, send):
    phases, single = chip_bits()
    split = len(phases) // 2
    mine = keep + exchange(send, (1, 1))
    for (low, high), (other_low, other_high) in zip(phases, phases[split:] + phases[:split]):
        near = exchange(mine, (low ^ 1, other_low ^ 1))
        far = exchange(mine, (high, other_high))
        across = exchange(mine, (low ^ high ^ 1, other_low ^ other_high ^ 1))
        mine = (mine + near) + (far + across)
    for bit in single:
        mine = mine + exchange(mine, (bit, bit))
    return mine, exchange(mine, (1, 1))


def per_device(snapshots, volumes, live_rows, probes):
    count = lax.axis_size("cells") * lax.axis_size("sub")
    keep, send, scale = local_sums(snapshots.shape[0] * count, snapshots, volumes, live_rows, probes)
    mine, other = reduce_halves(keep, send)
    return finish(mine, other, weigh(snapshots, scale), probes.shape[0])


def solution(mesh):
    placed = (
        P(("cells", "sub"), None),
        P(("cells", "sub")),
        P(("cells", "sub")),
        P(None, ("cells", "sub")),
    )
    return jax.shard_map(
        per_device,
        mesh=mesh,
        in_specs=placed,
        out_specs=(P(("cells", "sub"), None), P(), P()),
        check_vma=False,
    )
```

```python
import functools
import jax
import jax.numpy as jnp
from jax import lax
from jax.experimental import pallas as pl
from jax.experimental.pallas import tpu as pltpu
from jax.sharding import PartitionSpec as P

HIGHEST = lax.Precision.HIGHEST
LANES = 128
BLOCK = 8
AHEAD = 2
F32 = jnp.float32


def lanes_of(tile, column):
    index = jnp.full(tile.shape, column, jnp.int32)
    return jnp.take_along_axis(tile, index, axis=1, mode="promise_in_bounds")


def row_of(tile, index):
    return jnp.broadcast_to(tile[index : index + 1, :], tile.shape)


def product(left, right, dims):
    return lax.dot_general(left, right, (dims, ((), ())), precision=HIGHEST, preferred_element_type=F32)


def eliminate(matrix):
    width = matrix.shape[1]
    count = width // BLOCK
    shape = (BLOCK, width)
    tiles = [matrix[k * BLOCK : (k + 1) * BLOCK, :] for k in range(count)]
    sub_ids = lax.broadcasted_iota(jnp.int32, shape, 0)
    lane_ids = lax.broadcasted_iota(jnp.int32, shape, 1)
    spread_ids = lane_ids - sub_ids

    def gather(parts):
        total = parts[0]
        for r in range(1, BLOCK):
            total = jnp.where(sub_ids == r, parts[r], total)
        return total

    lower_rows = []
    following = [lanes_of(tiles[0], c) for c in range(BLOCK)]
    carried = [lanes_of(tiles[1], c) for c in range(BLOCK)]
    for block in range(count):
        offset = block * BLOCK
        in_block = (lane_ids >= offset) & (lane_ids < offset + BLOCK)
        columns = following
        own = jnp.where(in_block, jnp.where(spread_ids == offset, 1.0, 0.0), tiles[block])
        rows = [row_of(own, r) for r in range(BLOCK)]
        near = range(block + 1, min(block + 1 + AHEAD, count))
        weights = {k: [lanes_of(tiles[k], offset + c) for c in range(BLOCK)] for k in near if k > block + 1}
        weights[block + 1] = carried
        bases = {k: [lanes_of(tiles[k], offset + BLOCK + c) for c in range(BLOCK)] for k in near if k <= block + 2}
        changes = {k: [None] * BLOCK for k in bases}
        for k in near:
            tiles[k] = jnp.where(in_block, 0.0, tiles[k])
        pivots, inverse, scaled = [row_of(columns[0], 0)], [], {}
        for i in range(BLOCK):
            inv = pl.reciprocal(pivots[i], approx=True)
            inverse.append(inv)
            beside = {c: row_of(columns[c], i) for c in range(i + 1, BLOCK)}
            if i + 1 < BLOCK:
                square = beside[i + 1] * beside[i + 1]
                pivots.append(row_of(columns[i + 1], i + 1) - square * inv)
            for c in range(i + 1, BLOCK):
                scaled[c, i] = beside[c] * inv
                columns[c] = columns[c] - columns[i] * scaled[c, i]
            for k in near:
                here = weights[k][i]
                weight = here * inv
                if k == block + 1:
                    splats = [row_of(here, c) for c in range(BLOCK)]
                if k in changes:
                    for c in range(BLOCK):
                        change = weight * splats[c]
                        changes[k][c] = change if i == 0 else changes[k][c] + change
                for c in range(i + 1, BLOCK):
                    weights[k][c] = weights[k][c] - here * scaled[c, i]
                tiles[k] = tiles[k] - weight * rows[i]
            for r in range(i + 1, BLOCK):
                rows[r] = rows[r] - scaled[r, i] * rows[i]
        updated = {k: [base - change for base, change in zip(bases[k], changes[k])] for k in bases}
        following, carried = updated.get(block + 1), updated.get(block + 2)
        merged = gather(rows) * lax.rsqrt(gather(pivots))
        lower_rows.append(jnp.where(spread_ids <= offset, merged, 0.0))
        if block + 1 + AHEAD < count:
            solved = [None] * BLOCK
            for r in reversed(range(BLOCK)):
                solved[r] = rows[r] * inverse[r]
                for c in range(r + 1, BLOCK):
                    solved[r] = solved[r] - scaled[c, r] * solved[c]
            for k in range(block + 1 + AHEAD, count):
                terms = [lanes_of(tiles[k], offset + c) * solved[c] for c in range(BLOCK)]
                while len(terms) > 1:
                    terms = [terms[t] + terms[t + 1] for t in range(0, len(terms), 2)]
                tiles[k] = jnp.where(in_block, 0.0, tiles[k]) - terms[0]
    return jnp.concatenate(lower_rows, axis=0)


def packed_rows(order, probes):
    return -(-(order // 2 + probes + 1) // (2 * BLOCK)) * 2 * BLOCK


def chip_bits():
    count = lax.axis_size("cells") * lax.axis_size("sub")
    bits = [1 << k for k in range(1, count.bit_length() - 1)]
    whole = len(bits) // 2 * 2
    return [bits[k : k + 2] for k in range(0, whole, 2)], bits[whole:]


def part_mask():
    return 1 + sum(pair[0] for pair in chip_bits()[0])


def own_part():
    bits = (lax.axis_index("cells") * lax.axis_size("sub") + lax.axis_index("sub")) & part_mask()
    for shift in (16, 8, 4, 2, 1):
        bits = bits ^ (bits >> shift)
    return bits & 1


def live_volumes(volumes_ref, live_ref, begin):
    ids = lax.broadcasted_iota(jnp.int32, (1, LANES), 1) + begin
    part = volumes_ref[pl.ds(begin, LANES)].reshape(1, LANES)
    return jnp.where(ids < live_ref[0], part, 0.0)


def sums_kernel(total_rows, snapshots_hbm, volumes_hbm, live_ref, probes_hbm, keep_ref, send_ref, scale_ref, snapshots_ref, volumes_ref, probes_ref, packed, sems):
    copies = [
        pltpu.make_async_copy(source, target, sems.at[i])
        for i, (source, target) in enumerate(
            ((volumes_hbm, volumes_ref), (snapshots_hbm, snapshots_ref), (probes_hbm, probes_ref))
        )
    ]
    for copy in copies:
        copy.start()
    row_count, order = snapshots_ref.shape
    probes = probes_ref.shape[0]
    half = order // 2
    copies[0].wait()
    volume = jnp.concatenate([live_volumes(volumes_ref, live_ref, b) for b in range(0, row_count, LANES)], axis=1)
    scale_ref[...] = jnp.sqrt(volume)
    copies[1].wait()
    snapshots = snapshots_ref[...]
    scaled = snapshots.T * (volume * (1.0 / total_rows))
    gram = product(scaled, snapshots, ((1,), (0,)))
    row_ids = lax.broadcasted_iota(jnp.int32, (half, half), 0)
    column_ids = lax.broadcasted_iota(jnp.int32, (half, half), 1)
    packed[:half, :half] = jnp.where(row_ids <= column_ids, gram[:half, :half], gram[half:, half:])
    packed[:half, half:] = gram[:half, half:]
    rest = packed.shape[0] - half - probes
    diagonal = jnp.sum(jnp.where(row_ids == column_ids, gram[half:, half:], 0.0), axis=0, keepdims=True)
    packed[half + probes :, :] = jnp.concatenate([jnp.broadcast_to(diagonal, (rest, half))] * 2, axis=1)
    copies[2].wait()
    probe_scaled = probes_ref[...] * (volume * (1.0 / total_rows**0.5))
    packed[half : half + probes, :] = product(probe_scaled, snapshots, ((1,), (0,)))
    middle = packed.shape[0] // 2
    low = own_part() == 0

    @pl.when(low)
    def _():
        keep_ref[...] = packed[:middle, :]
        send_ref[...] = packed[middle:, :]

    @pl.when(jnp.logical_not(low))
    def _():
        keep_ref[...] = packed[middle:, :]
        send_ref[...] = packed[:middle, :]


def hold(array):
    return pltpu.with_memory_space_constraint(array, pltpu.HBM)


def local_sums(total_rows, snapshots, volumes, live_rows, probes):
    order = snapshots.shape[1]
    size = packed_rows(order, probes.shape[0])
    hbm = pl.BlockSpec(memory_space=pltpu.HBM)
    whole = pl.BlockSpec(memory_space=pltpu.VMEM)
    return pl.pallas_call(
        functools.partial(sums_kernel, total_rows),
        out_shape=(jax.ShapeDtypeStruct((size // 2, order), F32),) * 2 + (jax.ShapeDtypeStruct((1, volumes.shape[0]), F32),),
        in_specs=[hbm, hbm, pl.BlockSpec(memory_space=pltpu.SMEM), hbm],
        out_specs=(whole, whole, whole),
        scratch_shapes=[
            pltpu.VMEM(snapshots.shape, F32),
            pltpu.VMEM(volumes.shape, F32),
            pltpu.VMEM(probes.shape, F32),
            pltpu.VMEM((size, order), F32),
            pltpu.SemaphoreType.DMA((3,)),
        ],
        compiler_params=pltpu.CompilerParams(vmem_limit_bytes=24 * 1024 * 1024),
    )(hold(snapshots), hold(volumes), live_rows, hold(probes))


def weigh_kernel(snapshots_ref, scale_ref, weighted_ref):
    row_count, order = snapshots_ref.shape
    for begin in range(0, row_count, LANES):
        rows = pl.ds(begin, LANES)
        scale = jnp.broadcast_to(scale_ref[:, rows], (LANES, LANES)).T
        weighted_ref[rows, :] = snapshots_ref[rows, :] * jnp.concatenate([scale] * (order // LANES), axis=1)


def weigh(snapshots, scale):
    whole = pl.BlockSpec(memory_space=pltpu.VMEM)
    return pl.pallas_call(
        weigh_kernel,
        out_shape=jax.ShapeDtypeStruct(snapshots.shape, F32),
        in_specs=[whole, whole],
        out_specs=whole,
        compiler_params=pltpu.CompilerParams(vmem_limit_bytes=24 * 1024 * 1024),
        cost_estimate=pl.CostEstimate(flops=snapshots.size, bytes_accessed=8 * snapshots.size, transcendentals=0),
    )(snapshots, scale)


def finish_kernel(mine_ref, other_ref, weighted_ref, basis_ref, factor_ref, coef_ref):
    order = weighted_ref.shape[1]
    probes = coef_ref.shape[0]
    half = order // 2
    low = own_part() == 0
    mine, other = mine_ref[...], other_ref[...]
    packed = jnp.concatenate([jnp.where(low, mine, other), jnp.where(low, other, mine)], axis=0)
    row_ids = lax.broadcasted_iota(jnp.int32, (half, half), 0)
    column_ids = lax.broadcasted_iota(jnp.int32, (half, half), 1)
    in_upper = row_ids <= column_ids
    square = packed[:half, :half]
    turned = square.T
    cross = packed[half : half + probes, :]
    diagonal = packed[half + probes : half + probes + 1, :half]

    first = jnp.where(in_upper, square, turned)
    inverse = eliminate(first)
    beside = product(inverse, packed[:half, half:], ((1,), (0,)))
    second = jnp.where(row_ids > column_ids, square, turned)
    second = jnp.where(row_ids == column_ids, diagonal, second) - product(beside, beside, ((0,), (0,)))
    factor_ref[:half, :half] = jnp.where(in_upper, product(inverse, first, ((1,), (0,))), 0.0)
    factor_ref[:half, half:] = beside
    factor_ref[half:, :half] = jnp.zeros((half, half), F32)

    left = product(cross[:, :half], inverse, ((1,), (1,)))
    coef_ref[:, :half] = left
    cross_rest = cross[:, half:] - product(left, beside, ((1,), (0,)))
    left = product(weighted_ref[:, :half], inverse, ((1,), (1,)))
    basis_ref[:, :half] = left
    rest = weighted_ref[:, half:] - product(left, beside, ((1,), (0,)))

    inverse_second = eliminate(second)
    coef_ref[:, half:] = product(cross_rest, inverse_second, ((1,), (1,)))
    basis_ref[:, half:] = product(rest, inverse_second, ((1,), (1,)))
    factor_ref[half:, half:] = jnp.where(in_upper, product(inverse_second, second, ((1,), (0,))), 0.0)


def finish(mine, other, weighted, probes):
    row_count, order = weighted.shape
    whole = pl.BlockSpec(memory_space=pltpu.VMEM)
    return pl.pallas_call(
        finish_kernel,
        out_shape=(
            jax.ShapeDtypeStruct((row_count, order), F32),
            jax.ShapeDtypeStruct((order, order), F32),
            jax.ShapeDtypeStruct((probes, order), F32),
        ),
        in_specs=[whole] * 3,
        out_specs=(whole,) * 3,
        compiler_params=pltpu.CompilerParams(vmem_limit_bytes=32 * 1024 * 1024),
    )(mine, other, weighted)


def exchange(value, masks):
    count = lax.axis_size("cells") * lax.axis_size("sub")
    pairs = [(i, i ^ masks[bin(i & part_mask()).count("1") % 2]) for i in range(count)]
    return lax.ppermute(value, ("cells", "sub"), pairs)


def reduce_halves(keep, send):
    phases, single = chip_bits()
    split = len(phases) // 2
    mine = keep + exchange(send, (1, 1))
    for (low, high), (other_low, other_high) in zip(phases, phases[split:] + phases[:split]):
        near = exchange(mine, (low ^ 1, other_low ^ 1))
        far = exchange(mine, (high, other_high))
        across = exchange(mine, (low ^ high ^ 1, other_low ^ other_high ^ 1))
        mine = (mine + near) + (far + across)
    for bit in single:
        mine = mine + exchange(mine, (bit, bit))
    return mine, exchange(mine, (1, 1))


def per_device(snapshots, volumes, live_rows, probes):
    count = lax.axis_size("cells") * lax.axis_size("sub")
    keep, send, scale = local_sums(snapshots.shape[0] * count, snapshots, volumes, live_rows, probes)
    mine, other = reduce_halves(keep, send)
    return finish(mine, other, weigh(snapshots, scale), probes.shape[0])


def solution(mesh):
    placed = (
        P(("cells", "sub"), None),
        P(("cells", "sub")),
        P(("cells", "sub")),
        P(None, ("cells", "sub")),
    )
    return jax.shard_map(
        per_device,
        mesh=mesh,
        in_specs=placed,
        out_specs=(P(("cells", "sub"), None), P(), P()),
        check_vma=False,
    )
```

```python
import functools
import jax
import jax.numpy as jnp
from jax import lax
from jax.experimental import pallas as pl
from jax.experimental.pallas import tpu as pltpu
from jax.sharding import PartitionSpec as P

HIGHEST = lax.Precision.HIGHEST
LANES = 128
BLOCK = 8
AHEAD = 2
F32 = jnp.float32


def lanes_of(tile, column):
    return jnp.broadcast_to(tile[:, column : column + 1], tile.shape)


def row_of(tile, index):
    return jnp.broadcast_to(tile[index : index + 1, :], tile.shape)


def product(left, right, dims):
    return lax.dot_general(left, right, (dims, ((), ())), precision=HIGHEST, preferred_element_type=F32)


def eliminate(matrix):
    width = matrix.shape[1]
    count = width // BLOCK
    shape = (BLOCK, width)
    tiles = [matrix[k * BLOCK : (k + 1) * BLOCK, :] for k in range(count)]
    sub_ids = lax.broadcasted_iota(jnp.int32, shape, 0)
    lane_ids = lax.broadcasted_iota(jnp.int32, shape, 1)
    spread_ids = lane_ids - sub_ids

    def gather(parts):
        total = parts[0]
        for r in range(1, BLOCK):
            total = jnp.where(sub_ids == r, parts[r], total)
        return total

    lower_rows = []
    following = [lanes_of(tiles[0], c) for c in range(BLOCK)]
    carried = [lanes_of(tiles[1], c) for c in range(BLOCK)]
    pending = [lanes_of(tiles[1], BLOCK + c) for c in range(BLOCK)]
    for block in range(count):
        offset = block * BLOCK
        in_block = (lane_ids >= offset) & (lane_ids < offset + BLOCK)
        columns = following
        own = jnp.where(in_block, jnp.where(spread_ids == offset, 1.0, 0.0), tiles[block])
        rows = [row_of(own, r) for r in range(BLOCK)]
        near = range(block + 1, min(block + 1 + AHEAD, count))
        weights = {k: [lanes_of(tiles[k], offset + c) for c in range(BLOCK)] for k in near if k > block + 1}
        weights[block + 1] = carried
        bases = {k: [lanes_of(tiles[k], offset + BLOCK + c) for c in range(BLOCK)] for k in near if k == block + 2}
        if block + 1 < count:
            bases[block + 1] = pending
        changes = {k: [None] * BLOCK for k in bases}
        pending, pending_changes = [lanes_of(tiles[k], offset + 2 * BLOCK + c) for k in near if k == block + 2 for c in range(BLOCK)], []
        for k in near:
            tiles[k] = jnp.where(in_block, 0.0, tiles[k])
        pivots, inverse, scaled = [row_of(columns[0], 0)], [], {}
        for i in range(BLOCK):
            inv = pl.reciprocal(pivots[i], approx=True)
            inverse.append(inv)
            beside = {c: row_of(columns[c], i) for c in range(i + 1, BLOCK)}
            if i + 1 < BLOCK:
                square = beside[i + 1] * beside[i + 1]
                pivots.append(row_of(columns[i + 1], i + 1) - square * inv)
            for c in range(i + 1, BLOCK):
                scaled[c, i] = beside[c] * inv
                columns[c] = columns[c] - columns[i] * scaled[c, i]
            for k in near:
                here = weights[k][i]
                weight = here * inv
                if k == block + 1:
                    splats = [row_of(here, c) for c in range(BLOCK)]
                if k in changes:
                    for c in range(BLOCK):
                        change = weight * splats[c]
                        changes[k][c] = change if i == 0 else changes[k][c] + change
                if k == block + 2:
                    terms = [weight * row_of(here, c) for c in range(BLOCK)]
                    pending_changes = [a + b for a, b in zip(pending_changes, terms)] if i else terms
                for c in range(i + 1, BLOCK):
                    weights[k][c] = weights[k][c] - here * scaled[c, i]
                tiles[k] = tiles[k] - weight * rows[i]
            for r in range(i + 1, BLOCK):
                rows[r] = rows[r] - scaled[r, i] * rows[i]
        updated = {k: [base - change for base, change in zip(bases[k], changes[k])] for k in bases}
        pending = [base - change for base, change in zip(pending, pending_changes)]
        following, carried = updated.get(block + 1), updated.get(block + 2)
        merged = gather(rows) * lax.rsqrt(gather(pivots))
        lower_rows.append(jnp.where(spread_ids <= offset, merged, 0.0))
        if block + 1 + AHEAD < count:
            solved = [None] * BLOCK
            for r in reversed(range(BLOCK)):
                solved[r] = rows[r] * inverse[r]
                for c in range(r + 1, BLOCK):
                    solved[r] = solved[r] - scaled[c, r] * solved[c]
            for k in range(block + 1 + AHEAD, count):
                terms = [lanes_of(tiles[k], offset + c) * solved[c] for c in range(BLOCK)]
                while len(terms) > 1:
                    terms = [terms[t] + terms[t + 1] for t in range(0, len(terms), 2)]
                tiles[k] = jnp.where(in_block, 0.0, tiles[k]) - terms[0]
    return jnp.concatenate(lower_rows, axis=0)


def packed_rows(order, probes):
    return -(-(order // 2 + probes + 1) // (2 * BLOCK)) * 2 * BLOCK


def chip_bits():
    count = lax.axis_size("cells") * lax.axis_size("sub")
    bits = [1 << k for k in range(1, count.bit_length() - 1)]
    whole = len(bits) // 2 * 2
    return [bits[k : k + 2] for k in range(0, whole, 2)], bits[whole:]


def part_mask():
    return 1 + sum(pair[0] for pair in chip_bits()[0])


def own_part():
    bits = (lax.axis_index("cells") * lax.axis_size("sub") + lax.axis_index("sub")) & part_mask()
    for shift in (16, 8, 4, 2, 1):
        bits = bits ^ (bits >> shift)
    return bits & 1


def live_volumes(volumes_ref, live_ref, begin):
    ids = lax.broadcasted_iota(jnp.int32, (1, LANES), 1) + begin
    part = volumes_ref[pl.ds(begin, LANES)].reshape(1, LANES)
    return jnp.where(ids < live_ref[0], part, 0.0)


def sums_kernel(total_rows, snapshots_hbm, volumes_hbm, live_ref, probes_hbm, keep_ref, send_ref, scale_ref, snapshots_ref, volumes_ref, probes_ref, packed, sems):
    copies = [
        pltpu.make_async_copy(source, target, sems.at[i])
        for i, (source, target) in enumerate(
            ((volumes_hbm, volumes_ref), (snapshots_hbm, snapshots_ref), (probes_hbm, probes_ref))
        )
    ]
    for copy in copies:
        copy.start()
    row_count, order = snapshots_ref.shape
    probes = probes_ref.shape[0]
    half = order // 2
    copies[0].wait()
    volume = jnp.concatenate([live_volumes(volumes_ref, live_ref, b) for b in range(0, row_count, LANES)], axis=1)
    scale_ref[...] = jnp.sqrt(volume)
    copies[1].wait()
    snapshots = snapshots_ref[...]
    scaled = snapshots.T * (volume * (1.0 / total_rows))
    gram = product(scaled, snapshots, ((1,), (0,)))
    row_ids = lax.broadcasted_iota(jnp.int32, (half, half), 0)
    column_ids = lax.broadcasted_iota(jnp.int32, (half, half), 1)
    packed[:half, :half] = jnp.where(row_ids <= column_ids, gram[:half, :half], gram[half:, half:])
    packed[:half, half:] = gram[:half, half:]
    rest = packed.shape[0] - half - probes
    diagonal = jnp.sum(jnp.where(row_ids == column_ids, gram[half:, half:], 0.0), axis=0, keepdims=True)
    packed[half + probes :, :] = jnp.concatenate([jnp.broadcast_to(diagonal, (rest, half))] * 2, axis=1)
    copies[2].wait()
    probe_scaled = probes_ref[...] * (volume * (1.0 / total_rows**0.5))
    packed[half : half + probes, :] = product(probe_scaled, snapshots, ((1,), (0,)))
    middle = packed.shape[0] // 2
    low = own_part() == 0

    @pl.when(low)
    def _():
        keep_ref[...] = packed[:middle, :]
        send_ref[...] = packed[middle:, :]

    @pl.when(jnp.logical_not(low))
    def _():
        keep_ref[...] = packed[middle:, :]
        send_ref[...] = packed[:middle, :]


def hold(array):
    return pltpu.with_memory_space_constraint(array, pltpu.HBM)


def local_sums(total_rows, snapshots, volumes, live_rows, probes):
    order = snapshots.shape[1]
    size = packed_rows(order, probes.shape[0])
    hbm = pl.BlockSpec(memory_space=pltpu.HBM)
    whole = pl.BlockSpec(memory_space=pltpu.VMEM)
    return pl.pallas_call(
        functools.partial(sums_kernel, total_rows),
        out_shape=(jax.ShapeDtypeStruct((size // 2, order), F32),) * 2 + (jax.ShapeDtypeStruct((1, volumes.shape[0]), F32),),
        in_specs=[hbm, hbm, pl.BlockSpec(memory_space=pltpu.SMEM), hbm],
        out_specs=(whole, whole, whole),
        scratch_shapes=[
            pltpu.VMEM(snapshots.shape, F32),
            pltpu.VMEM(volumes.shape, F32),
            pltpu.VMEM(probes.shape, F32),
            pltpu.VMEM((size, order), F32),
            pltpu.SemaphoreType.DMA((3,)),
        ],
        compiler_params=pltpu.CompilerParams(vmem_limit_bytes=24 * 1024 * 1024),
    )(hold(snapshots), hold(volumes), live_rows, hold(probes))


def weigh_kernel(snapshots_ref, scale_ref, weighted_ref):
    row_count, order = snapshots_ref.shape
    for begin in range(0, row_count, LANES):
        rows = pl.ds(begin, LANES)
        scale = jnp.broadcast_to(scale_ref[:, rows], (LANES, LANES)).T
        weighted_ref[rows, :] = snapshots_ref[rows, :] * jnp.concatenate([scale] * (order // LANES), axis=1)


def weigh(snapshots, scale):
    whole = pl.BlockSpec(memory_space=pltpu.VMEM)
    return pl.pallas_call(
        weigh_kernel,
        out_shape=jax.ShapeDtypeStruct(snapshots.shape, F32),
        in_specs=[whole, whole],
        out_specs=whole,
        compiler_params=pltpu.CompilerParams(vmem_limit_bytes=24 * 1024 * 1024),
        cost_estimate=pl.CostEstimate(flops=snapshots.size, bytes_accessed=8 * snapshots.size, transcendentals=0),
    )(snapshots, scale)


def finish_kernel(mine_ref, other_ref, weighted_ref, basis_ref, factor_ref, coef_ref):
    order = weighted_ref.shape[1]
    probes = coef_ref.shape[0]
    half = order // 2
    low = own_part() == 0
    mine, other = mine_ref[...], other_ref[...]
    packed = jnp.concatenate([jnp.where(low, mine, other), jnp.where(low, other, mine)], axis=0)
    row_ids = lax.broadcasted_iota(jnp.int32, (half, half), 0)
    column_ids = lax.broadcasted_iota(jnp.int32, (half, half), 1)
    in_upper = row_ids <= column_ids
    square = packed[:half, :half]
    turned = square.T
    cross = packed[half : half + probes, :]
    diagonal = packed[half + probes : half + probes + 1, :half]

    first = jnp.where(in_upper, square, turned)
    inverse = eliminate(first)
    beside = product(inverse, packed[:half, half:], ((1,), (0,)))
    second = jnp.where(row_ids > column_ids, square, turned)
    second = jnp.where(row_ids == column_ids, diagonal, second) - product(beside, beside, ((0,), (0,)))
    factor_ref[:half, :half] = jnp.where(in_upper, product(inverse, first, ((1,), (0,))), 0.0)
    factor_ref[:half, half:] = beside
    factor_ref[half:, :half] = jnp.zeros((half, half), F32)

    left = product(cross[:, :half], inverse, ((1,), (1,)))
    coef_ref[:, :half] = left
    cross_rest = cross[:, half:] - product(left, beside, ((1,), (0,)))
    left = product(weighted_ref[:, :half], inverse, ((1,), (1,)))
    basis_ref[:, :half] = left
    rest = weighted_ref[:, half:] - product(left, beside, ((1,), (0,)))

    inverse_second = eliminate(second)
    coef_ref[:, half:] = product(cross_rest, inverse_second, ((1,), (1,)))
    basis_ref[:, half:] = product(rest, inverse_second, ((1,), (1,)))
    factor_ref[half:, half:] = jnp.where(in_upper, product(inverse_second, second, ((1,), (0,))), 0.0)


def finish(mine, other, weighted, probes):
    row_count, order = weighted.shape
    whole = pl.BlockSpec(memory_space=pltpu.VMEM)
    return pl.pallas_call(
        finish_kernel,
        out_shape=(
            jax.ShapeDtypeStruct((row_count, order), F32),
            jax.ShapeDtypeStruct((order, order), F32),
            jax.ShapeDtypeStruct((probes, order), F32),
        ),
        in_specs=[whole] * 3,
        out_specs=(whole,) * 3,
        compiler_params=pltpu.CompilerParams(vmem_limit_bytes=32 * 1024 * 1024),
    )(mine, other, weighted)


def exchange(value, masks):
    count = lax.axis_size("cells") * lax.axis_size("sub")
    pairs = [(i, i ^ masks[bin(i & part_mask()).count("1") % 2]) for i in range(count)]
    return lax.ppermute(value, ("cells", "sub"), pairs)


def reduce_halves(keep, send):
    phases, single = chip_bits()
    split = len(phases) // 2
    mine = keep + exchange(send, (1, 1))
    for (low, high), (other_low, other_high) in zip(phases, phases[split:] + phases[:split]):
        near = exchange(mine, (low ^ 1, other_low ^ 1))
        far = exchange(mine, (high, other_high))
        across = exchange(mine, (low ^ high ^ 1, other_low ^ other_high ^ 1))
        mine = (mine + near) + (far + across)
    for bit in single:
        mine = mine + exchange(mine, (bit, bit))
    return mine, exchange(mine, (1, 1))


def per_device(snapshots, volumes, live_rows, probes):
    count = lax.axis_size("cells") * lax.axis_size("sub")
    keep, send, scale = local_sums(snapshots.shape[0] * count, snapshots, volumes, live_rows, probes)
    mine, other = reduce_halves(keep, send)
    return finish(mine, other, weigh(snapshots, scale), probes.shape[0])


def solution(mesh):
    placed = (
        P(("cells", "sub"), None),
        P(("cells", "sub")),
        P(("cells", "sub")),
        P(None, ("cells", "sub")),
    )
    return jax.shard_map(
        per_device,
        mesh=mesh,
        in_specs=placed,
        out_specs=(P(("cells", "sub"), None), P(), P()),
        check_vma=False,
    )
```

```python
import functools
import jax
import jax.numpy as jnp
from jax import lax
from jax.experimental import pallas as pl
from jax.experimental.pallas import tpu as pltpu
from jax.sharding import PartitionSpec as P

HIGHEST = lax.Precision.HIGHEST
LANES = 128
BLOCK = 8
AHEAD = 2
F32 = jnp.float32


def lanes_of(tile, column):
    return jnp.broadcast_to(tile[:, column : column + 1], tile.shape)


def row_of(tile, index):
    return jnp.broadcast_to(tile[index : index + 1, :], tile.shape)


def product(left, right, dims):
    return lax.dot_general(left, right, (dims, ((), ())), precision=HIGHEST, preferred_element_type=F32)


def eliminate(matrix, scratch):
    width = matrix.shape[1]
    count = width // BLOCK
    shape = (BLOCK, width)
    tiles = [matrix[k * BLOCK : (k + 1) * BLOCK, :] for k in range(count)]
    sub_ids = lax.broadcasted_iota(jnp.int32, shape, 0)
    lane_ids = lax.broadcasted_iota(jnp.int32, shape, 1)
    spread_ids = lane_ids - sub_ids

    def gather(parts):
        total = parts[0]
        for r in range(1, BLOCK):
            total = jnp.where(sub_ids == r, parts[r], total)
        return total

    lower_rows = []
    following = [lanes_of(tiles[0], c) for c in range(BLOCK)]
    carried = [lanes_of(tiles[1], c) for c in range(BLOCK)]
    for block in range(count):
        offset = block * BLOCK
        in_block = (lane_ids >= offset) & (lane_ids < offset + BLOCK)
        columns = following
        own = jnp.where(in_block, jnp.where(spread_ids == offset, 1.0, 0.0), tiles[block])
        rows = [row_of(own, r) for r in range(BLOCK)]
        near = range(block + 1, min(block + 1 + AHEAD, count))
        weights = {k: [lanes_of(tiles[k], offset + c) for c in range(BLOCK)] for k in near if k > block + 1}
        weights[block + 1] = carried
        bases = {k: [lanes_of(tiles[k], offset + BLOCK + c) for c in range(BLOCK)] for k in near if k <= block + 2}
        changes = {k: [None] * BLOCK for k in bases}
        for k in near:
            tiles[k] = jnp.where(in_block, 0.0, tiles[k])
        pivots, inverse, scaled = [row_of(columns[0], 0)], [], {}
        for i in range(BLOCK):
            inv = pl.reciprocal(pivots[i], approx=True)
            inverse.append(inv)
            beside = {c: row_of(columns[c], i) for c in range(i + 1, BLOCK)}
            if i + 1 < BLOCK:
                square = beside[i + 1] * beside[i + 1]
                pivots.append(row_of(columns[i + 1], i + 1) - square * inv)
            for c in range(i + 1, BLOCK):
                scaled[c, i] = beside[c] * inv
                columns[c] = columns[c] - columns[i] * scaled[c, i]
            for k in near:
                here = weights[k][i]
                weight = here * inv
                if k == block + 1:
                    slot = (block % 2 * BLOCK + i) * BLOCK
                    scratch[slot : slot + BLOCK, :] = here
                    splats = [jnp.broadcast_to(scratch[slot + c : slot + c + 1, :], shape) for c in range(BLOCK)]
                if k in changes:
                    for c in range(BLOCK):
                        change = weight * splats[c]
                        changes[k][c] = change if i == 0 else changes[k][c] + change
                for c in range(i + 1, BLOCK):
                    weights[k][c] = weights[k][c] - here * scaled[c, i]
                tiles[k] = tiles[k] - weight * rows[i]
            for r in range(i + 1, BLOCK):
                rows[r] = rows[r] - scaled[r, i] * rows[i]
        updated = {k: [base - change for base, change in zip(bases[k], changes[k])] for k in bases}
        following, carried = updated.get(block + 1), updated.get(block + 2)
        merged = gather(rows) * lax.rsqrt(gather(pivots))
        lower_rows.append(jnp.where(spread_ids <= offset, merged, 0.0))
        if block + 1 + AHEAD < count:
            solved = [None] * BLOCK
            for r in reversed(range(BLOCK)):
                solved[r] = rows[r] * inverse[r]
                for c in range(r + 1, BLOCK):
                    solved[r] = solved[r] - scaled[c, r] * solved[c]
            for k in range(block + 1 + AHEAD, count):
                terms = [lanes_of(tiles[k], offset + c) * solved[c] for c in range(BLOCK)]
                while len(terms) > 1:
                    terms = [terms[t] + terms[t + 1] for t in range(0, len(terms), 2)]
                tiles[k] = jnp.where(in_block, 0.0, tiles[k]) - terms[0]
    return jnp.concatenate(lower_rows, axis=0)


def packed_rows(order, probes):
    return -(-(order // 2 + probes + 1) // (2 * BLOCK)) * 2 * BLOCK


def chip_bits():
    count = lax.axis_size("cells") * lax.axis_size("sub")
    bits = [1 << k for k in range(1, count.bit_length() - 1)]
    whole = len(bits) // 2 * 2
    return [bits[k : k + 2] for k in range(0, whole, 2)], bits[whole:]


def part_mask():
    return 1 + sum(pair[0] for pair in chip_bits()[0])


def own_part():
    bits = (lax.axis_index("cells") * lax.axis_size("sub") + lax.axis_index("sub")) & part_mask()
    for shift in (16, 8, 4, 2, 1):
        bits = bits ^ (bits >> shift)
    return bits & 1


def live_volumes(volumes_ref, live_ref, begin):
    ids = lax.broadcasted_iota(jnp.int32, (1, LANES), 1) + begin
    part = volumes_ref[pl.ds(begin, LANES)].reshape(1, LANES)
    return jnp.where(ids < live_ref[0], part, 0.0)


def sums_kernel(total_rows, snapshots_hbm, volumes_hbm, live_ref, probes_hbm, keep_ref, send_ref, scale_ref, snapshots_ref, volumes_ref, probes_ref, packed, sems):
    copies = [
        pltpu.make_async_copy(source, target, sems.at[i])
        for i, (source, target) in enumerate(
            ((volumes_hbm, volumes_ref), (snapshots_hbm, snapshots_ref), (probes_hbm, probes_ref))
        )
    ]
    for copy in copies:
        copy.start()
    row_count, order = snapshots_ref.shape
    probes = probes_ref.shape[0]
    half = order // 2
    copies[0].wait()
    volume = jnp.concatenate([live_volumes(volumes_ref, live_ref, b) for b in range(0, row_count, LANES)], axis=1)
    scale_ref[...] = jnp.sqrt(volume)
    copies[1].wait()
    snapshots = snapshots_ref[...]
    scaled = snapshots.T * (volume * (1.0 / total_rows))
    gram = product(scaled, snapshots, ((1,), (0,)))
    row_ids = lax.broadcasted_iota(jnp.int32, (half, half), 0)
    column_ids = lax.broadcasted_iota(jnp.int32, (half, half), 1)
    packed[:half, :half] = jnp.where(row_ids <= column_ids, gram[:half, :half], gram[half:, half:])
    packed[:half, half:] = gram[:half, half:]
    rest = packed.shape[0] - half - probes
    diagonal = jnp.sum(jnp.where(row_ids == column_ids, gram[half:, half:], 0.0), axis=0, keepdims=True)
    packed[half + probes :, :] = jnp.concatenate([jnp.broadcast_to(diagonal, (rest, half))] * 2, axis=1)
    copies[2].wait()
    probe_scaled = probes_ref[...] * (volume * (1.0 / total_rows**0.5))
    packed[half : half + probes, :] = product(probe_scaled, snapshots, ((1,), (0,)))
    middle = packed.shape[0] // 2
    low = own_part() == 0

    @pl.when(low)
    def _():
        keep_ref[...] = packed[:middle, :]
        send_ref[...] = packed[middle:, :]

    @pl.when(jnp.logical_not(low))
    def _():
        keep_ref[...] = packed[middle:, :]
        send_ref[...] = packed[:middle, :]


def hold(array):
    return pltpu.with_memory_space_constraint(array, pltpu.HBM)


def local_sums(total_rows, snapshots, volumes, live_rows, probes):
    order = snapshots.shape[1]
    size = packed_rows(order, probes.shape[0])
    hbm = pl.BlockSpec(memory_space=pltpu.HBM)
    whole = pl.BlockSpec(memory_space=pltpu.VMEM)
    return pl.pallas_call(
        functools.partial(sums_kernel, total_rows),
        out_shape=(jax.ShapeDtypeStruct((size // 2, order), F32),) * 2 + (jax.ShapeDtypeStruct((1, volumes.shape[0]), F32),),
        in_specs=[hbm, hbm, pl.BlockSpec(memory_space=pltpu.SMEM), hbm],
        out_specs=(whole, whole, whole),
        scratch_shapes=[
            pltpu.VMEM(snapshots.shape, F32),
            pltpu.VMEM(volumes.shape, F32),
            pltpu.VMEM(probes.shape, F32),
            pltpu.VMEM((size, order), F32),
            pltpu.SemaphoreType.DMA((3,)),
        ],
        compiler_params=pltpu.CompilerParams(vmem_limit_bytes=24 * 1024 * 1024),
    )(hold(snapshots), hold(volumes), live_rows, hold(probes))


def weigh_kernel(snapshots_ref, scale_ref, weighted_ref):
    row_count, order = snapshots_ref.shape
    for begin in range(0, row_count, LANES):
        rows = pl.ds(begin, LANES)
        scale = jnp.broadcast_to(scale_ref[:, rows], (LANES, LANES)).T
        weighted_ref[rows, :] = snapshots_ref[rows, :] * jnp.concatenate([scale] * (order // LANES), axis=1)


def weigh(snapshots, scale):
    whole = pl.BlockSpec(memory_space=pltpu.VMEM)
    return pl.pallas_call(
        weigh_kernel,
        out_shape=jax.ShapeDtypeStruct(snapshots.shape, F32),
        in_specs=[whole, whole],
        out_specs=whole,
        compiler_params=pltpu.CompilerParams(vmem_limit_bytes=24 * 1024 * 1024),
        cost_estimate=pl.CostEstimate(flops=snapshots.size, bytes_accessed=8 * snapshots.size, transcendentals=0),
    )(snapshots, scale)


def finish_kernel(mine_ref, other_ref, weighted_ref, basis_ref, factor_ref, coef_ref, scratch):
    order = weighted_ref.shape[1]
    probes = coef_ref.shape[0]
    half = order // 2
    low = own_part() == 0
    mine, other = mine_ref[...], other_ref[...]
    packed = jnp.concatenate([jnp.where(low, mine, other), jnp.where(low, other, mine)], axis=0)
    row_ids = lax.broadcasted_iota(jnp.int32, (half, half), 0)
    column_ids = lax.broadcasted_iota(jnp.int32, (half, half), 1)
    in_upper = row_ids <= column_ids
    square = packed[:half, :half]
    turned = square.T
    cross = packed[half : half + probes, :]
    diagonal = packed[half + probes : half + probes + 1, :half]

    first = jnp.where(in_upper, square, turned)
    inverse = eliminate(first, scratch)
    beside = product(inverse, packed[:half, half:], ((1,), (0,)))
    second = jnp.where(row_ids > column_ids, square, turned)
    second = jnp.where(row_ids == column_ids, diagonal, second) - product(beside, beside, ((0,), (0,)))
    factor_ref[:half, :half] = jnp.where(in_upper, product(inverse, first, ((1,), (0,))), 0.0)
    factor_ref[:half, half:] = beside
    factor_ref[half:, :half] = jnp.zeros((half, half), F32)

    left = product(cross[:, :half], inverse, ((1,), (1,)))
    coef_ref[:, :half] = left
    cross_rest = cross[:, half:] - product(left, beside, ((1,), (0,)))
    left = product(weighted_ref[:, :half], inverse, ((1,), (1,)))
    basis_ref[:, :half] = left
    rest = weighted_ref[:, half:] - product(left, beside, ((1,), (0,)))

    inverse_second = eliminate(second, scratch)
    coef_ref[:, half:] = product(cross_rest, inverse_second, ((1,), (1,)))
    basis_ref[:, half:] = product(rest, inverse_second, ((1,), (1,)))
    factor_ref[half:, half:] = jnp.where(in_upper, product(inverse_second, second, ((1,), (0,))), 0.0)


def finish(mine, other, weighted, probes):
    row_count, order = weighted.shape
    whole = pl.BlockSpec(memory_space=pltpu.VMEM)
    return pl.pallas_call(
        finish_kernel,
        out_shape=(
            jax.ShapeDtypeStruct((row_count, order), F32),
            jax.ShapeDtypeStruct((order, order), F32),
            jax.ShapeDtypeStruct((probes, order), F32),
        ),
        in_specs=[whole] * 3,
        out_specs=(whole,) * 3,
        scratch_shapes=[pltpu.VMEM((2 * BLOCK * BLOCK, order // 2), F32)],
        compiler_params=pltpu.CompilerParams(vmem_limit_bytes=32 * 1024 * 1024),
    )(mine, other, weighted)


def exchange(value, masks):
    count = lax.axis_size("cells") * lax.axis_size("sub")
    pairs = [(i, i ^ masks[bin(i & part_mask()).count("1") % 2]) for i in range(count)]
    return lax.ppermute(value, ("cells", "sub"), pairs)


def reduce_halves(keep, send):
    phases, single = chip_bits()
    split = len(phases) // 2
    mine = keep + exchange(send, (1, 1))
    for (low, high), (other_low, other_high) in zip(phases, phases[split:] + phases[:split]):
        near = exchange(mine, (low ^ 1, other_low ^ 1))
        far = exchange(mine, (high, other_high))
        across = exchange(mine, (low ^ high ^ 1, other_low ^ other_high ^ 1))
        mine = (mine + near) + (far + across)
    for bit in single:
        mine = mine + exchange(mine, (bit, bit))
    return mine, exchange(mine, (1, 1))


def per_device(snapshots, volumes, live_rows, probes):
    count = lax.axis_size("cells") * lax.axis_size("sub")
    keep, send, scale = local_sums(snapshots.shape[0] * count, snapshots, volumes, live_rows, probes)
    mine, other = reduce_halves(keep, send)
    return finish(mine, other, weigh(snapshots, scale), probes.shape[0])


def solution(mesh):
    placed = (
        P(("cells", "sub"), None),
        P(("cells", "sub")),
        P(("cells", "sub")),
        P(None, ("cells", "sub")),
    )
    return jax.shard_map(
        per_device,
        mesh=mesh,
        in_specs=placed,
        out_specs=(P(("cells", "sub"), None), P(), P()),
        check_vma=False,
    )
```

```python
import functools
import jax
import jax.numpy as jnp
from jax import lax
from jax.experimental import pallas as pl
from jax.experimental.pallas import tpu as pltpu
from jax.sharding import PartitionSpec as P

HIGHEST = lax.Precision.HIGHEST
LANES = 128
BLOCK = 8
AHEAD = 2
F32 = jnp.float32


def lanes_of(tile, column):
    return jnp.broadcast_to(tile[:, column : column + 1], tile.shape)


def row_of(tile, index):
    return jnp.broadcast_to(tile[index : index + 1, :], tile.shape)


def product(left, right, dims):
    return lax.dot_general(left, right, (dims, ((), ())), precision=HIGHEST, preferred_element_type=F32)


def eliminate(matrix):
    width = matrix.shape[1]
    count = width // BLOCK
    shape = (BLOCK, width)
    tiles = [matrix[k * BLOCK : (k + 1) * BLOCK, :] for k in range(count)]
    sub_ids = lax.broadcasted_iota(jnp.int32, shape, 0)
    lane_ids = lax.broadcasted_iota(jnp.int32, shape, 1)
    spread_ids = lane_ids - sub_ids

    def gather(parts):
        total = parts[0]
        for r in range(1, BLOCK):
            total = jnp.where(sub_ids == r, parts[r], total)
        return total

    lower_rows = []
    following = [lanes_of(tiles[0], c) for c in range(BLOCK)]
    carried = [lanes_of(tiles[1], c) for c in range(BLOCK)]
    for block in range(count):
        offset = block * BLOCK
        in_block = (lane_ids >= offset) & (lane_ids < offset + BLOCK)
        columns = following
        own = jnp.where(in_block, jnp.where(spread_ids == offset, 1.0, 0.0), tiles[block])
        rows = [row_of(own, r) for r in range(BLOCK)]
        near = range(block + 1, min(block + 1 + AHEAD, count))
        weights = {k: [lanes_of(tiles[k], offset + c) for c in range(BLOCK)] for k in near if k > block + 1}
        weights[block + 1] = carried
        bases = {k: [lanes_of(tiles[k], offset + BLOCK + c) for c in range(BLOCK)] for k in near if k <= block + 2}
        changes = {k: [None] * BLOCK for k in bases}
        for k in near:
            tiles[k] = jnp.where(in_block, 0.0, tiles[k])
        pivots, inverse, scaled = [row_of(columns[0], 0)], [], {}
        for i in range(BLOCK):
            inv = pl.reciprocal(pivots[i], approx=True)
            inverse.append(inv)
            beside = {c: row_of(columns[c], i) for c in range(i + 1, BLOCK)}
            if i + 1 < BLOCK:
                square = beside[i + 1] * beside[i + 1]
                pivots.append(row_of(columns[i + 1], i + 1) - square * inv)
            for c in range(i + 1, BLOCK):
                scaled[c, i] = beside[c] * inv
                columns[c] = columns[c] - columns[i] * scaled[c, i]
            for k in near:
                here = weights[k][i]
                weight = here * inv
                if k == block + 1:
                    splats = [row_of(here, c) for c in range(BLOCK)]
                if k in changes:
                    for c in range(BLOCK):
                        change = weight * splats[c]
                        changes[k][c] = change if i == 0 else changes[k][c] + change
                for c in range(i + 1, BLOCK):
                    weights[k][c] = weights[k][c] - here * scaled[c, i]
                tiles[k] = tiles[k] - weight * rows[i]
            for r in range(i + 1, BLOCK):
                rows[r] = rows[r] - scaled[r, i] * rows[i]
        updated = {k: [base - change for base, change in zip(bases[k], changes[k])] for k in bases}
        following, carried = updated.get(block + 1), updated.get(block + 2)
        merged = gather(rows) * lax.rsqrt(gather(pivots))
        lower_rows.append(jnp.where(spread_ids <= offset, merged, 0.0))
        if block + 1 + AHEAD < count:
            solved = [None] * BLOCK
            for r in reversed(range(BLOCK)):
                solved[r] = rows[r] * inverse[r]
                for c in range(r + 1, BLOCK):
                    solved[r] = solved[r] - scaled[c, r] * solved[c]
            for k in range(block + 1 + AHEAD, count):
                terms = [lanes_of(tiles[k], offset + c) * solved[c] for c in range(BLOCK)]
                while len(terms) > 1:
                    terms = [terms[t] + terms[t + 1] for t in range(0, len(terms), 2)]
                tiles[k] = jnp.where(in_block, 0.0, tiles[k]) - terms[0]
    return jnp.concatenate(lower_rows, axis=0)


def packed_rows(order, probes):
    return -(-(order // 2 + probes + 1) // (2 * BLOCK)) * 2 * BLOCK


def chip_bits():
    count = lax.axis_size("cells") * lax.axis_size("sub")
    bits = [1 << k for k in range(1, count.bit_length() - 1)]
    whole = len(bits) // 2 * 2
    return [bits[k : k + 2] for k in range(0, whole, 2)], bits[whole:]


def part_mask():
    return 1 + sum(pair[0] for pair in chip_bits()[0])


def own_part():
    bits = (lax.axis_index("cells") * lax.axis_size("sub") + lax.axis_index("sub")) & part_mask()
    for shift in (16, 8, 4, 2, 1):
        bits = bits ^ (bits >> shift)
    return bits & 1


def live_volumes(volumes_ref, live_ref, begin):
    ids = lax.broadcasted_iota(jnp.int32, (1, LANES), 1) + begin
    part = volumes_ref[pl.ds(begin, LANES)].reshape(1, LANES)
    return jnp.where(ids < live_ref[0], part, 0.0)


def sums_kernel(total_rows, snapshots_hbm, volumes_hbm, live_ref, probes_hbm, keep_ref, send_ref, scale_ref, snapshots_ref, volumes_ref, probes_ref, packed, sems):
    copies = [
        pltpu.make_async_copy(source, target, sems.at[i])
        for i, (source, target) in enumerate(
            ((volumes_hbm, volumes_ref), (snapshots_hbm, snapshots_ref), (probes_hbm, probes_ref))
        )
    ]
    for copy in copies:
        copy.start()
    row_count, order = snapshots_ref.shape
    probes = probes_ref.shape[0]
    half = order // 2
    copies[0].wait()
    volume = jnp.concatenate([live_volumes(volumes_ref, live_ref, b) for b in range(0, row_count, LANES)], axis=1)
    scale_ref[...] = jnp.sqrt(volume)
    copies[1].wait()
    snapshots = snapshots_ref[...]
    scaled = snapshots.T * (volume * (1.0 / total_rows))
    gram = product(scaled, snapshots, ((1,), (0,)))
    row_ids = lax.broadcasted_iota(jnp.int32, (half, half), 0)
    column_ids = lax.broadcasted_iota(jnp.int32, (half, half), 1)
    packed[:half, :half] = jnp.where(row_ids <= column_ids, gram[:half, :half], gram[half:, half:])
    packed[:half, half:] = gram[:half, half:]
    rest = packed.shape[0] - half - probes
    diagonal = jnp.sum(jnp.where(row_ids == column_ids, gram[half:, half:], 0.0), axis=0, keepdims=True)
    packed[half + probes :, :] = jnp.concatenate([jnp.broadcast_to(diagonal, (rest, half))] * 2, axis=1)
    copies[2].wait()
    probe_scaled = probes_ref[...] * (volume * (1.0 / total_rows**0.5))
    packed[half : half + probes, :] = product(probe_scaled, snapshots, ((1,), (0,)))
    middle = packed.shape[0] // 2
    low = own_part() == 0

    @pl.when(low)
    def _():
        keep_ref[...] = packed[:middle, :]
        send_ref[...] = packed[middle:, :]

    @pl.when(jnp.logical_not(low))
    def _():
        keep_ref[...] = packed[middle:, :]
        send_ref[...] = packed[:middle, :]


def hold(array):
    return pltpu.with_memory_space_constraint(array, pltpu.HBM)


def local_sums(total_rows, snapshots, volumes, live_rows, probes):
    order = snapshots.shape[1]
    size = packed_rows(order, probes.shape[0])
    hbm = pl.BlockSpec(memory_space=pltpu.HBM)
    whole = pl.BlockSpec(memory_space=pltpu.VMEM)
    return pl.pallas_call(
        functools.partial(sums_kernel, total_rows),
        out_shape=(jax.ShapeDtypeStruct((size // 2, order), F32),) * 2 + (jax.ShapeDtypeStruct((1, volumes.shape[0]), F32),),
        in_specs=[hbm, hbm, pl.BlockSpec(memory_space=pltpu.SMEM), hbm],
        out_specs=(whole, whole, whole),
        scratch_shapes=[
            pltpu.VMEM(snapshots.shape, F32),
            pltpu.VMEM(volumes.shape, F32),
            pltpu.VMEM(probes.shape, F32),
            pltpu.VMEM((size, order), F32),
            pltpu.SemaphoreType.DMA((3,)),
        ],
        compiler_params=pltpu.CompilerParams(vmem_limit_bytes=24 * 1024 * 1024),
    )(hold(snapshots), hold(volumes), live_rows, hold(probes))


def weigh_kernel(snapshots_ref, scale_ref, weighted_ref):
    row_count, order = snapshots_ref.shape
    for begin in range(0, row_count, LANES):
        rows = pl.ds(begin, LANES)
        scale = jnp.broadcast_to(scale_ref[:, rows], (LANES, LANES)).T
        weighted_ref[rows, :] = snapshots_ref[rows, :] * jnp.concatenate([scale] * (order // LANES), axis=1)


def weigh(snapshots, scale):
    whole = pl.BlockSpec(memory_space=pltpu.VMEM)
    return pl.pallas_call(
        weigh_kernel,
        out_shape=jax.ShapeDtypeStruct(snapshots.shape, F32),
        in_specs=[whole, whole],
        out_specs=whole,
        compiler_params=pltpu.CompilerParams(vmem_limit_bytes=24 * 1024 * 1024),
        cost_estimate=pl.CostEstimate(flops=snapshots.size, bytes_accessed=8 * snapshots.size, transcendentals=0),
    )(snapshots, scale)


def finish_kernel(mine_ref, other_ref, weighted_ref, basis_ref, factor_ref, coef_ref):
    order = weighted_ref.shape[1]
    probes = coef_ref.shape[0]
    half = order // 2
    low = own_part() == 0
    mine, other = mine_ref[...], other_ref[...]
    packed = jnp.concatenate([jnp.where(low, mine, other), jnp.where(low, other, mine)], axis=0)
    row_ids = lax.broadcasted_iota(jnp.int32, (half, half), 0)
    column_ids = lax.broadcasted_iota(jnp.int32, (half, half), 1)
    in_upper = row_ids <= column_ids
    square = packed[:half, :half]
    turned = square.T
    cross = packed[half : half + probes, :]
    diagonal = packed[half + probes : half + probes + 1, :half]

    first = jnp.where(in_upper, square, turned)
    inverse = eliminate(first)
    beside = product(inverse, packed[:half, half:], ((1,), (0,)))
    second = jnp.where(row_ids > column_ids, square, turned)
    second = jnp.where(row_ids == column_ids, diagonal, second) - product(beside, beside, ((0,), (0,)))
    factor_ref[:half, :half] = jnp.where(in_upper, product(inverse, first, ((1,), (0,))), 0.0)
    factor_ref[:half, half:] = beside
    factor_ref[half:, :half] = jnp.zeros((half, half), F32)

    left = product(cross[:, :half], inverse, ((1,), (1,)))
    coef_ref[:, :half] = left
    cross_rest = cross[:, half:] - product(left, beside, ((1,), (0,)))
    left = product(weighted_ref[:, :half], inverse, ((1,), (1,)))
    basis_ref[:, :half] = left
    rest = weighted_ref[:, half:] - product(left, beside, ((1,), (0,)))

    inverse_second = eliminate(second)
    coef_ref[:, half:] = product(cross_rest, inverse_second, ((1,), (1,)))
    basis_ref[:, half:] = product(rest, inverse_second, ((1,), (1,)))
    factor_ref[half:, half:] = jnp.where(in_upper, product(inverse_second, second, ((1,), (0,))), 0.0)


def finish(mine, other, weighted, probes):
    row_count, order = weighted.shape
    whole = pl.BlockSpec(memory_space=pltpu.VMEM)
    return pl.pallas_call(
        finish_kernel,
        out_shape=(
            jax.ShapeDtypeStruct((row_count, order), F32),
            jax.ShapeDtypeStruct((order, order), F32),
            jax.ShapeDtypeStruct((probes, order), F32),
        ),
        in_specs=[whole] * 3,
        out_specs=(whole,) * 3,
        compiler_params=pltpu.CompilerParams(vmem_limit_bytes=32 * 1024 * 1024),
    )(mine, other, weighted)


def exchange(value, masks):
    count = lax.axis_size("cells") * lax.axis_size("sub")
    pairs = [(i, i ^ masks[bin(i & part_mask()).count("1") % 2]) for i in range(count)]
    return lax.ppermute(value, ("cells", "sub"), pairs)


def reduce_halves(keep, send):
    phases, single = chip_bits()
    split = len(phases) // 2
    mine = keep + exchange(send, (1, 1))
    for (low, high), (other_low, other_high) in zip(phases, phases[split:] + phases[:split]):
        across = exchange(mine, (low ^ high ^ 1, other_low ^ other_high ^ 1))
        far = exchange(mine, (high, other_high))
        near = exchange(mine, (low ^ 1, other_low ^ 1))
        mine = (mine + near) + (far + across)
    for bit in single:
        mine = mine + exchange(mine, (bit, bit))
    return mine, exchange(mine, (1, 1))


def per_device(snapshots, volumes, live_rows, probes):
    count = lax.axis_size("cells") * lax.axis_size("sub")
    keep, send, scale = local_sums(snapshots.shape[0] * count, snapshots, volumes, live_rows, probes)
    mine, other = reduce_halves(keep, send)
    return finish(mine, other, weigh(snapshots, scale), probes.shape[0])


def solution(mesh):
    placed = (
        P(("cells", "sub"), None),
        P(("cells", "sub")),
        P(("cells", "sub")),
        P(None, ("cells", "sub")),
    )
    return jax.shard_map(
        per_device,
        mesh=mesh,
        in_specs=placed,
        out_specs=(P(("cells", "sub"), None), P(), P()),
        check_vma=False,
    )
```
